32 devices in a mesh: rep: 4 (over z), shard: 8 (over y, x, core).
Axes of the slice: x: 2, y: 2, z: 4, core: 2. Of those that a mesh axis runs over, the one named last changes fastest.
Arguments:
- tokens: bfloat16 [8192, 1024], P(('rep', 'shard')), may hold values from -6 to 6
- cotangent: bfloat16 [8192, 1024], P(('rep', 'shard')), may hold values from -6 to 6
- deal: int32 [8192], P(('rep', 'shard')), may hold values from 0 to 2047, as said below
- offsets: int32 [32, 4], P(('rep', 'shard')), may hold values from 0 to 256, as said below
- lengths: int32 [32, 4], P(('rep', 'shard')), may hold values from 0 to 256, as said below
- norm1_gain: bfloat16 [1024], P('shard'), may hold values from 0.5 to 1.5
- q_weight: bfloat16 [1024, 768], P('shard'), may hold values from -0.1875 to 0.1875
- k_weight: bfloat16 [1024, 768], P('shard'), may hold values from -0.1875 to 0.1875
- v_weight: bfloat16 [1024, 1536], P('shard'), may hold values from -0.1875 to 0.1875
- conv_weight: bfloat16 [4, 3072], P(None, 'shard'), may hold values from -3 to 3
- beta_weight: bfloat16 [1024, 6], P('shard'), may hold values from -0.1875 to 0.1875
- decay_weight: bfloat16 [1024, 6], P('shard'), may hold values from -0.1875 to 0.1875
- log_rate: float32 [6], replicated, may hold values from -6.2 to -3
- step_bias: float32 [6], replicated, may hold values from -1 to 1
- out_gate_weight: bfloat16 [1024, 1536], P('shard'), may hold values from -0.1875 to 0.1875
- out_norm_gain: bfloat16 [256], P('shard'), may hold values from 0.5 to 1.5
- out_weight: bfloat16 [1536, 1024], P('shard'), may hold values from -0.15625 to 0.15625
- norm2_gain: bfloat16 [1024], P('shard'), may hold values from 0.5 to 1.5
- ffn_gate: bfloat16 [1024, 2816], P('shard'), may hold values from -0.1875 to 0.1875
- ffn_up: bfloat16 [1024, 2816], P('shard'), may hold values from -0.1875 to 0.1875
- ffn_down: bfloat16 [2816, 1024], P('shard'), may hold values from -0.109375 to 0.109375
Outputs:
- mixed_rows: bfloat16 [8192, 1024], P(('rep', 'shard'))
- tokens_grad: bfloat16 [8192, 1024], P(('rep', 'shard'))
- norm1_gain_grad: float32 [1024], P('shard')
- q_weight_grad: float32 [1024, 768], P('shard')
- k_weight_grad: float32 [1024, 768], P('shard')
- v_weight_grad: float32 [1024, 1536], P('shard')
- conv_weight_grad: float32 [4, 3072], P(None, 'shard')
- beta_weight_grad: float32 [1024, 6], P('shard')
- decay_weight_grad: float32 [1024, 6], P('shard')
- log_rate_grad: float32 [6], replicated
- step_bias_grad: float32 [6], replicated
- out_gate_weight_grad: float32 [1024, 1536], P('shard')
- out_norm_gain_grad: float32 [256], P('shard')
- out_weight_grad: float32 [1536, 1024], P('shard')
- norm2_gain_grad: float32 [1024], P('shard')
- ffn_gate_grad: float32 [1024, 2816], P('shard')
- ffn_up_grad: float32 [1024, 2816], P('shard')
- ffn_down_grad: float32 [2816, 1024], P('shard')
The draws below stay inside these ranges and needn't reach their ends.
Inputs may be any that keep to these rules, and one draw needn't show every extreme that they name: `deal`: within each replica's 2048 entries, a permutation of 0 to 2048 - 1 (a given row is numbered within its replica); each block takes exactly 32 rows from each device's given rows. `offsets`: per block, the first slots of up to 4 sequences: multiples of 64, not falling, the first 0; an entry equal to 256 means no sequence. `lengths`: each sequence's live tokens, from half of its slots to all of them, 0 exactly where there is no sequence; some sequence fills a whole block.
All inputs are finite; a program needn't handle non-finite values.
Results may differ from the reference program's by a relative error of at most 0.018.
Values may be sent and summed in bfloat16 or wider, within the bound.
A program may use at most 256 MiB of HBM per device.

```python
import jax
import jax.numpy as jnp
from jax import lax

D = 1024
H = 6
DV = 256
FF = 2816
CONV = 4
BLOCK_LEN = 64
TOK_DEV = 256
SEQ_DEV = 4
KEYS = 768
VALS = 1536
TOKENS = 8192
N_REP = 4
N_SHARD = 8


def layout_draw(key):
    block_total = N_REP * N_SHARD
    block_count = TOK_DEV // BLOCK_LEN
    key_cuts, key_used, key_lens = jax.random.split(key, 3)

    def cuts_for(sub_key):
        return jax.random.permutation(sub_key, block_count - 1)[:SEQ_DEV - 1] + 1
    cut_points = jax.vmap(cuts_for)(jax.random.split(key_cuts, block_total))
    used = jax.random.randint(key_used, (block_total, SEQ_DEV - 1), 0, 3) > 0
    row_ids = jnp.arange(block_total)[:, None]
    cut_points = jnp.where(used & (row_ids > 0), cut_points, block_count)
    cut_points = jnp.sort(cut_points, axis=1)
    begins = jnp.concatenate([jnp.zeros((block_total, 1), cut_points.dtype), cut_points], axis=1)
    finish = jnp.concatenate([cut_points, jnp.full((block_total, 1), block_count, cut_points.dtype)], axis=1)
    extent = (finish - begins) * BLOCK_LEN
    trimmed = jax.random.randint(key_lens, (block_total, SEQ_DEV), 0, jnp.maximum(extent // 2, 1))
    col_ids = jnp.arange(SEQ_DEV)[None, :]
    trimmed = jnp.where((row_ids == 0) & (col_ids == 0), 0, trimmed)
    seq_lens = jnp.where(extent > 0, extent - trimmed, 0)
    return ((begins * BLOCK_LEN).astype(jnp.int32), seq_lens.astype(jnp.int32))


def draw_offsets(key, part):
    shared = layout_draw(key)
    return shared[0]


def draw_lengths(key, part):
    shared = layout_draw(key)
    return shared[1]


def draw_deal(key, part):
    key = jax.random.fold_in(key, 11)
    key_send, key_mix = jax.random.split(key)
    per_peer = TOK_DEV // N_SHARD
    sources = N_REP * N_SHARD

    def shuffle(sub_key):
        return jax.random.permutation(sub_key, TOK_DEV)
    sent = jax.vmap(shuffle)(jax.random.split(key_send, sources)).reshape(N_REP, N_SHARD, TOK_DEV)
    sent = sent + (jnp.arange(N_SHARD) * TOK_DEV)[None, :, None]
    sent = sent.reshape(N_REP, N_SHARD, N_SHARD, per_peer).transpose(0, 2, 1, 3).reshape(sources, TOK_DEV)
    mixer_perm = jax.vmap(shuffle)(jax.random.split(key_mix, sources))
    placed = jnp.take_along_axis(sent, mixer_perm, axis=1)
    return placed.reshape(N_REP * N_SHARD * TOK_DEV).astype(jnp.int32)


def block_levels(rng, dims, cuts, low, top_value):
    level = 1.0
    for dim, blocks in cuts:
        draws = jax.random.uniform(jax.random.fold_in(jax.random.fold_in(rng, 6), dim), (blocks,), jnp.float32, low / len(cuts), top_value / len(cuts))
        level = level * jnp.repeat(jnp.exp(draws), dims[dim] // blocks).reshape((-1,) + (1,) * (len(dims) - 1 - dim))
    return level


def centred(key, shape, deviation, most, shards=(), kind=jnp.bfloat16):
    result = jax.random.normal(key, shape, jnp.float32) * deviation
    if len(shards) > 0:
        result = block_levels(key, shape, shards, -0.22, 0.18) * result
    return jnp.clip(result, min=-most, max=most).astype(kind)


def setup_inputs(seed: int = 0) -> dict:
    key_list = jax.random.split(jax.random.key(seed), 22)
    return {
        "tokens": centred(key_list[0], (TOKENS, D), 1.0, 6.0, ((0, 32),)),
        "cotangent": centred(key_list[1], (TOKENS, D), 1.0, 6.0, ((0, 32),)),
        "deal": draw_deal(jax.random.fold_in(key_list[21], 71), 0),
        "offsets": draw_offsets(jax.random.fold_in(key_list[21], 71), 0),
        "lengths": draw_lengths(jax.random.fold_in(key_list[21], 71), 0),
        "norm1_gain": jnp.clip(1.0 + 0.1 * jax.random.normal(key_list[5], (D,), jnp.float32), 0.5, 1.5).astype(jnp.bfloat16),
        "q_weight": centred(key_list[6], (D, KEYS), D ** -0.5, 0.1875, ((0, 8),)),
        "k_weight": centred(key_list[7], (D, KEYS), D ** -0.5, 0.1875, ((0, 8),)),
        "v_weight": centred(key_list[8], (D, VALS), D ** -0.5, 0.1875, ((0, 8),)),
        "conv_weight": centred(key_list[9], (CONV, 2 * KEYS + VALS), CONV ** -0.5, 3.0, ((1, 8),)),
        "beta_weight": centred(key_list[10], (D, H), D ** -0.5, 0.1875, ((0, 8),)),
        "decay_weight": centred(key_list[11], (D, H), D ** -0.5, 0.1875, ((0, 8),)),
        "log_rate": jnp.clip(jax.random.uniform(key_list[12], (H,), jnp.float32, -6.2, -3.0), -6.2, -3.0),
        "step_bias": jnp.clip(jax.random.uniform(key_list[13], (H,), jnp.float32, -1.0, 1.0), -1.0, 1.0),
        "out_gate_weight": centred(key_list[14], (D, VALS), D ** -0.5, 0.1875, ((0, 8),)),
        "out_norm_gain": jnp.clip(1.0 + 0.1 * jax.random.normal(key_list[15], (DV,), jnp.float32), 0.5, 1.5).astype(jnp.bfloat16),
        "out_weight": centred(key_list[16], (VALS, D), VALS ** -0.5, 0.15625, ((0, 8),)),
        "norm2_gain": jnp.clip(1.0 + 0.1 * jax.random.normal(key_list[17], (D,), jnp.float32), 0.5, 1.5).astype(jnp.bfloat16),
        "ffn_gate": centred(key_list[18], (D, FF), D ** -0.5, 0.1875, ((0, 8),)),
        "ffn_up": centred(key_list[19], (D, FF), D ** -0.5, 0.1875, ((0, 8),)),
        "ffn_down": centred(key_list[20], (FF, D), FF ** -0.5, 0.109375, ((0, 8),)),
    }


PRECISE_MODE = lax.Precision.HIGHEST

@jax.custom_vjp
def low(v):
    return lax.optimization_barrier(v.astype(jnp.bfloat16)).astype(jnp.float32)

@jax.custom_vjp
def low_back(v):
    return v

def low_keep(v):
    return (low(v), None)

def low_pass(kept, grad):
    return (grad,)

def back_keep(v):
    return (v, None)

def back_low(kept, grad):
    return (low(grad),)
low.defvjp(low_keep, low_pass)
low_back.defvjp(back_keep, back_low)

def exact_dot(left_in, right_in):
    return jnp.dot(left_in, right_in, precision=PRECISE_MODE)

def rms_norm(values_in):
    return values_in * lax.rsqrt(lax.optimization_barrier(jnp.mean(values_in * values_in, axis=-1, keepdims=True)) + 1e-05)

def seq_layout(starts_in, lengths_in, row_count, block_len):
    row_index = jnp.arange(row_count, dtype=jnp.int32)
    inside = (row_index[:, None] >= starts_in[None, :]).astype(jnp.int32)
    region = lax.optimization_barrier(jnp.sum(inside, axis=1)) - 1
    picked = (region[:, None] == jnp.arange(starts_in.shape[0], dtype=jnp.int32)[None, :]).astype(jnp.int32)
    seq_begin = lax.optimization_barrier(jnp.sum(picked * starts_in[None, :], axis=1))
    extent = lax.optimization_barrier(jnp.sum(picked * lengths_in[None, :], axis=1))
    position = row_index - seq_begin
    live_mask = (position < extent).astype(jnp.float32)
    block_heads = jnp.arange(row_count // block_len, dtype=jnp.int32) * block_len
    resets = jnp.any(block_heads[:, None] == starts_in[None, :], axis=1).astype(jnp.float32)
    return (position, live_mask, resets)

def causal_conv(linear_in, conv_taps, position):
    row_count = linear_in.shape[0]
    summed = jnp.zeros_like(linear_in)
    for lag_step in range(conv_taps.shape[0]):
        shifted = jnp.pad(linear_in, ((lag_step, 0), (0, 0)))[:row_count]
        allowed = (position >= lag_step).astype(jnp.float32)[:, None]
        summed = summed + conv_taps[lag_step][None, :] * shifted * allowed
    return summed

def delta_rule(queries, keys_in, values_in, beta_rate, log_decay, resets, block_len):
    row_count, head_count, key_width = queries.shape
    value_width = values_in.shape[2]
    block_count = row_count // block_len

    def split_blocks(tensor):
        return tensor.reshape(block_count, block_len, head_count, -1).transpose(0, 2, 1, 3)
    query_blocks = split_blocks(queries)
    key_blocks = split_blocks(keys_in)
    value_blocks = split_blocks(values_in)
    beta_blocks = beta_rate.reshape(block_count, block_len, head_count).transpose(0, 2, 1)
    decay_blocks = log_decay.reshape(block_count, block_len, head_count).transpose(0, 2, 1)
    cumulative = jnp.cumsum(decay_blocks, axis=-1)
    lower_mask = jnp.tril(jnp.ones((block_len, block_len), jnp.float32))
    strict = lower_mask - jnp.eye(block_len, dtype=jnp.float32)
    log_gaps = cumulative[..., :, None] - cumulative[..., None, :]
    pair_decay = jnp.exp(jnp.where(lower_mask > 0, log_gaps, 0.0)) * lower_mask
    key_gram = jnp.einsum('nhid,nhjd->nhij', key_blocks, key_blocks, precision=PRECISE_MODE)
    system = jnp.eye(block_len, dtype=jnp.float32) + beta_blocks[..., :, None] * key_gram * pair_decay * strict
    right_sides = jnp.concatenate([beta_blocks[..., None] * value_blocks, (beta_blocks * jnp.exp(cumulative))[..., None] * key_blocks], axis=-1)
    solved = lax.linalg.triangular_solve(system, right_sides, left_side=True, lower=True, unit_diagonal=True)
    fresh_vals = solved[..., :value_width]
    mixing = solved[..., value_width:]
    attend = jnp.einsum('nhid,nhjd->nhij', query_blocks, key_blocks, precision=PRECISE_MODE) * pair_decay
    grow_decay = jnp.exp(cumulative)[..., None]
    last_cumul = cumulative[..., -1:]
    tail_decay = jnp.exp(last_cumul)[..., None]
    kscaled = key_blocks * jnp.exp(last_cumul - cumulative)[..., None]

    def advance(carried, pieces):
        q_now, fresh_now, mix_now, att_now, grow_now, tail_now, kscaled_now, reset_now = pieces
        carried = carried * (1.0 - reset_now)
        new_vals = fresh_now - jnp.einsum('hcd,hde->hce', mix_now, carried, precision=PRECISE_MODE)
        output = grow_now * jnp.einsum('hcd,hde->hce', q_now, carried, precision=PRECISE_MODE)
        output = output + jnp.einsum('hij,hje->hie', att_now, new_vals, precision=PRECISE_MODE)
        carried = tail_now * carried + jnp.einsum('hcd,hce->hde', kscaled_now, new_vals, precision=PRECISE_MODE)
        return (carried, output)
    initial = jnp.zeros((head_count, key_width, value_width), jnp.float32)
    _, outputs = lax.scan(advance, initial, (query_blocks, fresh_vals, mixing, attend, grow_decay, tail_decay, kscaled, resets))
    return outputs.transpose(0, 2, 1, 3).reshape(row_count, head_count, value_width)

def mixer_core(q_lin, k_lin, v_lin, gate_out_lin, beta_lin, decay_lin, conv_taps, log_rate, step_bias, norm_gain, position, live_mask, resets):
    row_count = q_lin.shape[0]
    key_total = q_lin.shape[1]
    key_width = key_total // H
    value_width = v_lin.shape[1] // H
    joined = jnp.concatenate([q_lin, k_lin, v_lin], axis=1)
    active = jax.nn.silu(causal_conv(joined, conv_taps, position))
    queries = active[:, :key_total].reshape(row_count, H, key_width)
    keys_in = active[:, key_total:2 * key_total].reshape(row_count, H, key_width)
    values_in = active[:, 2 * key_total:].reshape(row_count, H, value_width)
    queries = queries * lax.rsqrt(lax.optimization_barrier(jnp.sum(queries * queries, axis=-1, keepdims=True)) + 1e-06) * key_width ** (-0.5)
    keys_in = keys_in * lax.rsqrt(lax.optimization_barrier(jnp.sum(keys_in * keys_in, axis=-1, keepdims=True)) + 1e-06)
    beta_rate = jax.nn.sigmoid(beta_lin) * live_mask[:, None]
    log_decay = -jnp.exp(log_rate)[None, :] * jax.nn.softplus(decay_lin + step_bias[None, :]) * live_mask[:, None]
    heads_out = delta_rule(queries, keys_in, values_in, beta_rate, log_decay, resets, BLOCK_LEN) * live_mask[:, None, None]
    scaled = heads_out * lax.rsqrt(lax.optimization_barrier(jnp.mean(heads_out * heads_out, axis=-1, keepdims=True)) + 1e-05)
    gated = scaled * norm_gain * jax.nn.silu(gate_out_lin.reshape(row_count, H, value_width))
    return gated.reshape(row_count, H * value_width)

def block_layer(block_x, starts_in, lengths_in, params):
    norm1_gain, q_weight, k_weight, v_weight, conv_weight, beta_weight, decay_weight, log_rate, step_bias, out_gate_weight, out_norm_gain, out_weight, norm2_gain, ffn_gate, ffn_up, ffn_down = params
    position, live_mask, resets = seq_layout(starts_in, lengths_in, block_x.shape[0], BLOCK_LEN)
    normed_in = low(rms_norm(block_x) * norm1_gain)
    q_lin = low_back(exact_dot(normed_in, q_weight))
    k_lin = low_back(exact_dot(normed_in, k_weight))
    v_lin = low_back(exact_dot(normed_in, v_weight))
    gate_out_lin = low_back(exact_dot(normed_in, out_gate_weight))
    beta_lin = low_back(exact_dot(normed_in, beta_weight))
    decay_lin = low_back(exact_dot(normed_in, decay_weight))
    mixed_out = low(mixer_core(q_lin, k_lin, v_lin, gate_out_lin, beta_lin, decay_lin, conv_weight, log_rate, step_bias, out_norm_gain, position, live_mask, resets))
    middle = block_x + low_back(exact_dot(mixed_out, out_weight))
    normed_mid = low(rms_norm(middle) * norm2_gain)
    gate_lin = low_back(exact_dot(normed_mid, ffn_gate))
    up_lin = low_back(exact_dot(normed_mid, ffn_up))
    hidden = low(jax.nn.silu(gate_lin) * up_lin)
    return middle + low_back(exact_dot(hidden, ffn_down))

def reference(tokens, cotangent, deal, offsets, lengths, norm1_gain, q_weight, k_weight, v_weight, conv_weight, beta_weight, decay_weight, log_rate, step_bias, out_gate_weight, out_norm_gain, out_weight, norm2_gain, ffn_gate, ffn_up, ffn_down):
    group_rows = N_SHARD * TOK_DEV
    dealt = deal.reshape(N_REP, group_rows)
    replica_ids = jnp.arange(N_REP, dtype=jnp.int32)[:, None]

    def to_blocks(tensor):
        grouped = tensor.astype(jnp.float32).reshape(N_REP, group_rows, D)
        return grouped[replica_ids, dealt].reshape(N_REP * N_SHARD, TOK_DEV, D)
    block_x = to_blocks(tokens)
    block_dy = to_blocks(cotangent)
    params = (norm1_gain.astype(jnp.float32), q_weight.astype(jnp.float32), k_weight.astype(jnp.float32), v_weight.astype(jnp.float32), conv_weight.astype(jnp.float32), beta_weight.astype(jnp.float32), decay_weight.astype(jnp.float32), log_rate.astype(jnp.float32), step_bias.astype(jnp.float32), out_gate_weight.astype(jnp.float32), out_norm_gain.astype(jnp.float32), out_weight.astype(jnp.float32), norm2_gain.astype(jnp.float32), ffn_gate.astype(jnp.float32), ffn_up.astype(jnp.float32), ffn_down.astype(jnp.float32))

    def whole(inputs_all, weights_all):

        def one_block(pieces):
            return block_layer(pieces[0], pieces[1], pieces[2], weights_all)
        return lax.map(jax.checkpoint(one_block), (inputs_all, offsets, lengths))
    outputs, pull_back = jax.vjp(whole, block_x, params)
    grad_x, grads = pull_back(block_dy)
    inverse = jnp.argsort(dealt, axis=1).astype(jnp.int32)

    def to_given(tensor):
        grouped = tensor.reshape(N_REP, group_rows, D)
        return grouped[replica_ids, inverse].reshape(N_REP * group_rows, D).astype(jnp.bfloat16)
    return (to_given(outputs), to_given(grad_x), grads[0], grads[1], grads[2], grads[3], grads[4], grads[5], grads[6], grads[7], grads[8], grads[9], grads[10], grads[11], grads[12], grads[13], grads[14], grads[15])
```

```python
import functools
import jax
import jax.numpy as jnp
from jax import lax
from jax.experimental import pallas as pl
from jax.experimental.pallas import tpu as pltpu
from jax.sharding import PartitionSpec as P

f32 = jnp.float32
bf16 = jnp.bfloat16
HEADS = 6
DK = 128
DVH = 256
KEYS = 768
VALS = 1536
QKV = 2 * KEYS + VALS
LANES = 128


def two_parts(a):
    hi = a.astype(bf16)
    return hi, (a - hi.astype(f32)).astype(bf16)


def dot(a, b, ca=1, cb=0):
    return lax.dot_general(a, b, (((ca,), (cb,)), ((), ())), preferred_element_type=f32)


def dot3(a, b, ca=1, cb=0):
    ah, al = a
    bh, bl = b
    return dot(ah, bh, ca, cb) + (dot(ah, bl, ca, cb) + dot(al, bh, ca, cb))


def tri_dot(tri, cols):
    hi = cols.astype(bf16)
    rest = cols - hi.astype(f32)
    mid = rest.astype(bf16)
    lo = (rest - mid.astype(f32)).astype(bf16)
    return dot(tri, hi) + (dot(tri, mid) + dot(tri, lo))


def sigm(a):
    return 1.0 / (1.0 + jnp.exp(-a))


def softplus(a):
    return jnp.maximum(a, 0.0) + jnp.log1p(jnp.exp(-jnp.abs(a)))


def layout_cols(offs, lens, n, shape, dim):
    row = lax.broadcasted_iota(jnp.int32, shape, dim)
    begin = jnp.zeros_like(row)
    extent = jnp.zeros_like(row)
    for i in range(len(offs)):
        inside = row >= offs[i]
        begin = jnp.where(inside, offs[i], begin)
        extent = jnp.where(inside, lens[i], extent)
    return begin, row - begin, (row - begin) < extent


def conv_chunk(x, taps, pos, cols):
    total = taps[0:1, cols] * x
    for t in range(1, 4):
        total = total + taps[t : t + 1, cols] * jnp.where(pos >= t, pltpu.roll(x, t, 0), 0.0)
    return total


def lane_pick(a, lane, index):
    return jnp.sum(jnp.where(lane == index, a, 0.0), axis=1, keepdims=True)


def pair_masks(n, begin_c, begin_r):
    i = lax.broadcasted_iota(jnp.int32, (n, n), 0)
    j = lax.broadcasted_iota(jnp.int32, (n, n), 1)
    same = begin_c == begin_r
    return i, j, (i >= j) & same


def mixer_forward(n, offs, lens, lin, taps, rate, bias, gain, act, cum, cum_t, tinv, fresh, heads_out, mixed):
    begin_c, pos, live = layout_cols(offs, lens, n, (n, 1), 0)
    begin_r, _, _ = layout_cols(offs, lens, n, (1, n), 1)
    live_f = live.astype(f32)
    width = 384

    def conv_step(step, carry):
        cols = pl.ds(pl.multiple_of(step * width, width), width)
        pre = conv_chunk(lin[:, cols], taps, pos, cols)
        act[:, cols] = pre * sigm(pre)
        return carry

    lax.fori_loop(0, QKV // width, conv_step, 0)
    lane = lax.broadcasted_iota(jnp.int32, (n, LANES), 1)
    bd = lin[:, QKV + VALS : QKV + VALS + LANES]
    beta = sigm(bd) * live_f
    decay = -jnp.exp(rate[...]) * softplus(bd + bias[...]) * live_f
    i, j, low = pair_masks(n, begin_c, begin_r)
    tri = (i >= j).astype(bf16)
    total = tri_dot(tri, decay)
    cum[...] = total
    cum_t[...] = total.T
    eye = (i == j).astype(f32)

    def one_head(h):
        kcols = pl.ds(pl.multiple_of(h * DK, DK), DK)
        ka = act[:, pl.ds(pl.multiple_of(KEYS + h * DK, DK), DK)]
        qa = act[:, kcols]
        vcols = pl.ds(pl.multiple_of(h * DVH, DVH), DVH)
        v = act[:, pl.ds(pl.multiple_of(2 * KEYS + h * DVH, DVH), DVH)]
        q = qa * (lax.rsqrt(jnp.sum(qa * qa, axis=1, keepdims=True) + 1e-6) * DK**-0.5)
        k = ka * lax.rsqrt(jnp.sum(ka * ka, axis=1, keepdims=True) + 1e-6)
        beta_c = lane_pick(beta, lane, h)
        cum_c = lane_pick(total, lane, HEADS + h)
        cum_r = cum_t[pl.ds(HEADS + h, 1), :]
        kk, qq = two_parts(k), two_parts(q)
        dec = jnp.where(low, jnp.exp(jnp.where(low, cum_c - cum_r, 0.0)), 0.0)
        system = jnp.where(i > j, beta_c * dot3(kk, kk, 1, 1) * dec, 0.0)
        inv = eye - jnp.where((i // 2) == (j // 2), system, 0.0)
        size = 2
        while size < n:
            off = jnp.where(((i // (2 * size)) == (j // (2 * size))) & ((i // size) != (j // size)), system, 0.0)
            parts = two_parts(inv)
            inv = inv - dot3(two_parts(dot3(parts, two_parts(off))), parts)
            size *= 2
        tinv[h] = inv
        u = dot3(two_parts(inv), two_parts(beta_c * v))
        fresh[:, vcols] = u
        o = dot3(two_parts(dot3(qq, kk, 1, 1) * dec), two_parts(u)) * live_f
        heads_out[:, vcols] = o
        gate = lin[:, pl.ds(pl.multiple_of(QKV + h * DVH, DVH), DVH)]
        scaled = o * lax.rsqrt(jnp.mean(o * o, axis=1, keepdims=True) + 1e-5)
        mixed[:, vcols] = (scaled * gain[...] * (gate * sigm(gate))).astype(bf16)

    def head_pair(step, carry):
        one_head(2 * step)
        one_head(2 * step + 1)
        return carry

    lax.fori_loop(0, HEADS // 2, head_pair, 0)


def mixer_backward(
    n, offs, lens, lin, taps, rate, bias, gain, act, cum, cum_t, tinv, fresh, heads_out, grad_mixed,
    dact, dcols, drows, lin_grad, tap_grad, gain_grad, rate_grad, bias_grad,
):
    begin_c, pos, live = layout_cols(offs, lens, n, (n, 1), 0)
    begin_r, _, _ = layout_cols(offs, lens, n, (1, n), 1)
    live_f = live.astype(f32)
    lane = lax.broadcasted_iota(jnp.int32, (n, LANES), 1)
    bd = lin[:, QKV + VALS : QKV + VALS + LANES]
    sig_b = sigm(bd)
    beta = sig_b * live_f
    i, j, low = pair_masks(n, begin_c, begin_r)
    strict = low & (i > j)
    gain_grad[...] = jnp.zeros_like(gain_grad)
    dcols[...] = jnp.zeros_like(dcols)
    drows[...] = jnp.zeros_like(drows)

    def one_head(h):
        kcols = pl.ds(pl.multiple_of(h * DK, DK), DK)
        kcols2 = pl.ds(pl.multiple_of(KEYS + h * DK, DK), DK)
        vcols = pl.ds(pl.multiple_of(h * DVH, DVH), DVH)
        vcols2 = pl.ds(pl.multiple_of(2 * KEYS + h * DVH, DVH), DVH)
        gcols = pl.ds(pl.multiple_of(QKV + h * DVH, DVH), DVH)
        ka = act[:, kcols2]
        qa = act[:, kcols]
        v = act[:, vcols2]
        o = heads_out[:, vcols]
        gate = lin[:, gcols]
        dm = grad_mixed[:, vcols]
        ro = lax.rsqrt(jnp.mean(o * o, axis=1, keepdims=True) + 1e-5)
        scaled = o * ro
        sg = sigm(gate)
        si = gate * sg
        gain_grad[...] += jnp.sum(dm * scaled * si, axis=0, keepdims=True)
        lin_grad[:, gcols] = (dm * scaled * gain[...] * (sg + si * (1.0 - sg))).astype(bf16)
        ds = dm * gain[...] * si
        d_o = two_parts(ro * (ds - scaled * jnp.mean(ds * scaled, axis=1, keepdims=True)) * live_f)
        rq = lax.rsqrt(jnp.sum(qa * qa, axis=1, keepdims=True) + 1e-6)
        rk = lax.rsqrt(jnp.sum(ka * ka, axis=1, keepdims=True) + 1e-6)
        qhat = qa * rq
        k = ka * rk
        kk, qq = two_parts(k), two_parts(qhat * DK**-0.5)
        beta_c = lane_pick(beta, lane, h)
        cum_c = lane_pick(cum[...], lane, HEADS + h)
        cum_r = cum_t[pl.ds(HEADS + h, 1), :]
        dec = jnp.where(low, jnp.exp(jnp.where(low, cum_c - cum_r, 0.0)), 0.0)
        gram = dot3(kk, kk, 1, 1)
        qk = dot3(qq, kk, 1, 1)
        uu = two_parts(fresh[:, vcols])
        du = dot3(two_parts(qk * dec), d_o, 0, 0)
        dp = dot3(d_o, uu, 1, 1) * dec
        db = dot3(two_parts(tinv[h]), two_parts(du), 0, 0)
        da = jnp.where(strict, -dot3(two_parts(db), uu, 1, 1), 0.0) * dec
        x = da * gram
        dbeta = jnp.sum(x, axis=1, keepdims=True) + jnp.sum(db * v, axis=1, keepdims=True)
        e = dp * qk + x * beta_c
        dcols[...] += jnp.where(lane == h, dbeta, 0.0) + jnp.where(
            lane == HEADS + h, jnp.sum(e, axis=1, keepdims=True), 0.0
        )
        drows[pl.ds(HEADS + h, 1), :] = jnp.sum(e, axis=0, keepdims=True)
        dact[:, vcols2] = beta_c * db
        dg = two_parts(da * beta_c)
        dpp = two_parts(dp)
        dq = dot3(dpp, kk)
        dk = dot3(dpp, qq, 0, 0) + dot3(dg, kk) + dot3(dg, kk, 0, 0)
        dact[:, kcols] = (rq * DK**-0.5) * (dq - qhat * jnp.sum(dq * qhat, axis=1, keepdims=True))
        dact[:, kcols2] = rk * (dk - k * jnp.sum(dk * k, axis=1, keepdims=True))

    def head_step(step, carry):
        one_head(2 * step)
        one_head(2 * step + 1)
        return carry

    lax.fori_loop(0, HEADS // 2, head_step, 0)

    dcum = jnp.where((lane >= HEADS) & (lane < 2 * HEADS), dcols[...] - drows[...].T, 0.0)
    ddecay = tri_dot((i <= j).astype(bf16), dcum)
    z = bd + bias[...]
    speed = -jnp.exp(rate[...]) * live_f
    dz = ddecay * speed * sigm(z)
    rate_grad[...] = jnp.sum(ddecay * speed * softplus(z), axis=0, keepdims=True)
    bias_grad[...] = jnp.sum(dz, axis=0, keepdims=True)
    dbeta_lin = dcols[...] * live_f * sig_b * (1.0 - sig_b)
    both = jnp.where(lane < HEADS, dbeta_lin, jnp.where(lane < 2 * HEADS, dz, 0.0))
    lin_grad[:, QKV + VALS : QKV + VALS + LANES] = both.astype(bf16)

    width = 384

    def conv_step(step, carry):
        cols = pl.ds(pl.multiple_of(step * width, width), width)
        x = lin[:, cols]
        pre = conv_chunk(x, taps, pos, cols)
        sg = sigm(pre)
        dc = dact[:, cols] * (sg + pre * sg * (1.0 - sg))
        dx = taps[0:1, cols] * dc
        tap_grad[0:1, cols] = jnp.sum(dc * x, axis=0, keepdims=True)
        for t in range(1, 4):
            masked = jnp.where(pos >= t, dc, 0.0)
            dx = dx + taps[t : t + 1, cols] * pltpu.roll(masked, n - t, 0)
            tap_grad[t : t + 1, cols] = jnp.sum(masked * pltpu.roll(x, t, 0), axis=0, keepdims=True)
        lin_grad[:, cols] = dx.astype(bf16)
        return carry

    lax.fori_loop(0, QKV // width, conv_step, 0)


MESH = pl.DeviceIdType.MESH


class Place:
    def __init__(self, n_shard, n_rep):
        self.n, self.reps = n_shard, n_rep
        self.ys = n_shard // 4
        self.r = lax.axis_index("rep")
        self.s = lax.axis_index("shard")
        self.c = self.s % 2
        self.x = (self.s // 2) % 2
        self.y = self.s // 4
        half = n_rep // 2
        low = self.r < half
        self.depth = jnp.where(low, self.r, n_rep - 1 - self.r)
        self.inner = jnp.where(low, self.r + 1, self.r - 1)
        self.outer = jnp.where(low, self.r - 1, self.r + 1)
        self.middle = self.depth == half - 1
        self.deep = self.depth > 0

    def shard_id(self, y, x, c):
        return (self.r, (y * 2 + x) * 2 + c)

    def core_peer(self):
        return self.shard_id(self.y, self.x, 1 - self.c)

    def x_peer(self):
        return self.shard_id(self.y, 1 - self.x, self.c)

    def y_of(self, step):
        return (self.y + step) % self.ys

    def y_peer(self, step):
        return self.shard_id(self.y_of(step), self.x, self.c)


def remote(src, dst, send, recv, device):
    return pltpu.make_async_remote_copy(
        src_ref=src, dst_ref=dst, send_sem=send, recv_sem=recv, device_id=device, device_id_type=MESH
    )


def greet(place, with_rep):
    barrier = pltpu.get_barrier_semaphore()
    n = place.n
    for step in range(1, n):
        pl.semaphore_signal(
            barrier, inc=1, device_id=(place.r, (place.s + step) % n), device_id_type=MESH
        )
    if not with_rep:
        pl.semaphore_wait(barrier, n - 1)
        return
    for step in range(1, place.reps):
        pl.semaphore_signal(
            barrier, inc=1, device_id=((place.r + step) % place.reps, place.s), device_id_type=MESH
        )
    pl.semaphore_wait(barrier, n - 1 + place.reps - 1)


def add_into(dst, idx, *others):
    total = dst[idx].astype(f32)
    for ref, at in others:
        total = total + ref[at].astype(f32)
    dst[idx] = total.astype(dst.dtype)


RING = 4


def halved(rows):
    return (rows // 2) // 16 * 16


class Ring:
    def __init__(self, n, rows, cols):
        self.n, self.rows, self.cols = n, rows, cols
        self.ys = n // 4
        self.count = 0

    def scratch(self):
        k, ys, cols = RING, self.ys, self.cols
        sems = pltpu.SemaphoreType.DMA
        per = 3 + 2 * (ys - 1)
        half = self.rows - halved(self.rows)
        return [
            pltpu.VMEM((k, ys, 2, 2, self.rows, cols), bf16),
            pltpu.VMEM((k, ys, 2, self.rows, cols), bf16),
            pltpu.VMEM((k, ys, half, cols), bf16),
            pltpu.VMEM((k, ys - 1, 2, half, cols), bf16),
            pltpu.VMEM((k, ys - 1, half, cols), bf16),
            pltpu.VMEM((k, half, cols), bf16),
            pltpu.VMEM((4, k, self.rows, cols), bf16),
            sems((k, per)),
            sems((k, per)),
            sems((k, 7)),
        ]

    def bind(self, refs):
        (self.own, self.r0, self.r1a, self.r1b, self.r2a, self.r2b, self.z, self.send, self.recv, self.zsem) = refs


class Piece:
    def __init__(self, ring, place, rows, cols, out, out_cols):
        self.ring, self.p, self.rows = ring, place, rows
        self.slot = ring.count % RING
        ring.count += 1
        self.w = pl.ds(0, cols)
        self.ra = halved(rows)
        self.rb = rows - self.ra
        self.all_rows = pl.ds(0, rows)
        self.out = out.at[:, pl.ds(out_cols, cols)]

    def own_view(self):
        return self.ring.own.at[self.slot, :, :, :, self.all_rows, self.w]

    def store_rows(self, value):
        ring = self.ring
        shaped = value.reshape(ring.ys, 2, 2, rinself.rows, value.shape[-1])
        ring.own[self.slot, :, :, :, self.all_rows, self.w] = shaped

    def send_core(self):
        g, p, k = self.ring, self.p, self.slot
        self.c0 = remote(
            g.own.at[k, :, :, 1 - p.c, self.all_rows, self.w], g.r0.at[k, :, :, self.all_rows, self.w],
            g.send.at[k, 0], g.recv.at[k, 0], p.core_peer(),
        )
        self.c0.start()

    def after_core(self):
        g, p, k, w = self.ring, self.p, self.slot, self.w
        rows = self.all_rows
        self.c0.wait()

        def step(q, carry):
            yy, xx = q // 2, q % 2
            add_into(g.own, (k, yy, xx, p.c, rows, w), (g.r0, (k, yy, xx, rows, w)))
            return carry

        lax.fori_loop(0, g.ys * 2, step, 0)
        top, low = pl.ds(0, self.ra), pl.ds(self.ra, self.rb)
        first, second = pl.ds(0, self.ra), pl.ds(0, self.rb)
        self.c1 = [
            remote(
                g.own.at[k, :, 1 - p.x, p.c, top, w], g.r1a.at[k, :, first, w],
                g.send.at[k, 1], g.recv.at[k, 1], p.x_peer(),
            )
        ]
        for d in range(1, g.ys):
            self.c1.append(
                remote(
                    g.own.at[k, p.y_of(d), :, p.c, low, w], g.r1b.at[k, d - 1, :, second, w],
                    g.send.at[k, 1 + d], g.recv.at[k, 1 + d], p.y_peer(d),
                )
            )
        for c in self.c1:
            c.start()

    def after_first(self):
        g, p, k, w = self.ring, self.p, self.slot, self.w
        top, low = pl.ds(0, self.ra), pl.ds(self.ra, self.rb)
        first, second = pl.ds(0, self.ra), pl.ds(0, self.rb)
        for c in self.c1:
            c.wait()
        for yy in range(g.ys):
            add_into(g.own, (k, yy, p.x, p.c, top, w), (g.r1a, (k, yy, first, w)))
        for xx in range(2):
            add_into(
                g.own, (k, p.y, xx, p.c, low, w),
                *[(g.r1b, (k, d, xx, second, w)) for d in range(g.ys - 1)],
            )
        self.c2 = [
            remote(
                g.own.at[k, p.y, 1 - p.x, p.c, low, w], g.r2b.at[k, second, w],
                g.send.at[k, 1 + g.ys], g.recv.at[k, 1 + g.ys], p.x_peer(),
            )
        ]
        for d in range(1, g.ys):
            self.c2.append(
                remote(
                    g.own.at[k, p.y_of(d), p.x, p.c, top, w], g.r2a.at[k, d - 1, first, w],
                    g.send.at[k, 1 + g.ys + d], g.recv.at[k, 1 + g.ys + d], p.y_peer(d),
                )
            )
        for c in self.c2:
            c.start()

    def after_second(self):
        g, p, k, w = self.ring, self.p, self.slot, self.w
        for c in self.c2:
            c.wait()
        total = g.own[k, p.y, p.x, p.c, 0 : self.ra, w].astype(f32)
        for d in range(g.ys - 1):
            total = total + g.r2a[k, d, 0 : self.ra, w].astype(f32)
        g.z[0, k, 0 : self.ra, w] = total.astype(bf16)
        total = g.own[k, p.y, p.x, p.c, self.ra : self.rows, w].astype(f32) + g.r2b[k, 0 : self.rb, w].astype(f32)
        g.z[0, k, self.ra : self.rows, w] = total.astype(bf16)
        z = lambda i: g.z.at[i, k, self.all_rows, w]
        target = lambda r: (r, p.s)
        sem = g.zsem
        self.up = remote(z(0), z(1), sem.at[k, 0], sem.at[k, 1], target(p.inner))
        self.meet = remote(z(0), z(2), sem.at[k, 2], sem.at[k, 3], target(p.inner))
        self.down = remote(z(3), z(2), sem.at[k, 4], sem.at[k, 3], target(p.outer))
        self.home = pltpu.make_async_copy(z(3), self.out, sem.at[k, 6])

        @pl.when(p.depth == 0)
        def _():
            self.send_inward()

    def send_inward(self):
        p = self.p

        @pl.when(p.middle)
        def _():
            self.meet.start()

        @pl.when(jnp.logical_not(p.middle))
        def _():
            self.up.start()

    def after_up(self):
        g, p, k, w = self.ring, self.p, self.slot, self.w

        @pl.when(p.deep)
        def _():
            self.up.wait_recv()
            add_into(g.z, (0, k, self.all_rows, w), (g.z, (1, k, self.all_rows, w)))
            self.send_inward()

    def finish(self, middle):
        g, p, k, w = self.ring, self.p, self.slot, self.w
        rows = self.all_rows

        @pl.when(p.middle if middle else jnp.logical_not(p.middle))
        def _():
            self.meet.wait_recv()
            if middle:
                both = g.z[0, k, rows, w].astype(f32) + g.z[2, k, rows, w].astype(f32)
                g.z[3, k, rows, w] = both.astype(bf16)
            else:
                g.z[3, k, rows, w] = g.z[2, k, rows, w]

            @pl.when(p.deep)
            def _():
                self.down.start()

            self.home.start()

    def close(self):
        p = self.p

        @pl.when(p.middle)
        def _():
            self.meet.wait_send()

        @pl.when(jnp.logical_not(p.middle))
        def _():
            self.up.wait_send()

        @pl.when(p.deep)
        def _():
            self.down.wait_send()

        self.home.wait()


def pump(pieces, index):
    stages = [
        (7, lambda q: q.close()),
        (6, lambda q: q.finish(False)),
        (5, lambda q: q.finish(True)),
        (4, lambda q: q.after_up()),
        (3, lambda q: q.after_second()),
        (2, lambda q: q.after_first()),
        (1, lambda q: q.after_core()),
    ]
    for lag, act in stages:
        if 0 <= index - lag < len(pieces):
            act(pieces[index - lag])


class Small:
    def __init__(self, n, reps, rows, cols):
        self.n, self.ys, self.reps = n, n // 4, reps
        self.sizes = (2, 2, self.ys, reps)
        self.rows, self.cols = rows, cols

    def scratch(self):
        total = sum(self.sizes)
        return [
            pltpu.VMEM((total, self.rows, self.cols), f32),
            pltpu.SemaphoreType.DMA((total,)),
            pltpu.SemaphoreType.DMA((total,)),
        ]

    def bind(self, refs):
        self.buf, self.send, self.recv = refs

    def begin(self, place, axis, value):
        base = sum(self.sizes[:axis])
        size = self.sizes[axis]
        p = place
        mine = (p.c, p.x, p.y, p.r)[axis]
        slot = self.buf.at[base + mine]
        slot[...] = value
        self.copies = []
        for d in range(1, size):
            at = (mine + d) % size
            device = (
                p.shard_id(p.y, p.x, at), p.shard_id(p.y, at, p.c), p.shard_id(at, p.x, p.c), (at, p.s),
            )[axis]
            self.copies.append(remote(slot, slot, self.send.at[base + d], self.recv.at[base + d], device))
        for c in self.copies:
            c.start()

    def end(self, axis):
        base = sum(self.sizes[:axis])
        for c in self.copies:
            c.wait()
        total = self.buf[base]
        for d in range(1, self.sizes[axis]):
            total = total + self.buf[base + d]
        return total


def columns(total, widths):
    cuts, at = [], 0
    while at < total:
        width = next(w for w in widths if w <= total - at)
        cuts.append((at, width))
        at += width
    return cuts


FFN_CUTS = ((0, 768), (768, 768), (1536, 640), (2176, 640))


def scatter_kernel(n, reps, rings, small, *refs):
    gg, gu, gd, go, gp, small_in = refs[:6]
    og, ou, od, oo, oq, ok, ov, ot, ob, small_out = refs[6:16]
    rest = refs[16:]
    ring_a, ring_b = rings
    load_sem = rest[0]
    rest = rest[1:]
    ring_a.bind(rest[:10])
    ring_b.bind(rest[10:20])
    small.bind(rest[20:23])
    place = Place(n, reps)
    greet(place, True)
    pieces = []
    loads = []
    rows_a = gg.shape[3]

    def add(ring, rows, cols, src, src_at, out, out_at):
        piece = Piece(ring, place, rows, cols, out, out_at)
        src_view = src.at[:, :, :, :, pl.ds(src_at, cols)]
        pieces.append(piece)
        loads.append(pltpu.make_async_copy(src_view, piece.own_view(), load_sem.at[len(pieces) % 2]))

    for src, out in ((gg, og), (gu, ou)):
        for at, width in FFN_CUTS:
            add(ring_a, rows_a, width, src, at, out, at)
    for at in range(0, 1024, 256):
        add(ring_b, gd.shape[3], 256, gd, at, od, at)
    for at in range(0, 1024, 256):
        add(ring_b, go.shape[3], 256, go, at, oo, at)
    at = 0
    for out in (oq, ok, ov, ot, ob):
        for inner, width in columns(out.shape[1], (768, 128)):
            add(ring_a, rows_a, width, gp, at, out, inner)
            at += width
    value = small_in[...]
    for index in range(len(pieces) + 7):
        if index < 4:
            small.begin(place, index, value)
        pump(pieces, index)
        if index < len(pieces):
            loads[index].start()
            loads[index].wait()
            pieces[index].send_core()
        if index < 4:
            value = small.end(index)
    small_out[...] = value


def scatter_sums(n, reps, gg, gu, gd, go, gp, small_in):
    rings = (Ring(n, gg.shape[0] // n, 768), Ring(n, gd.shape[0] // n, 256))
    small = Small(n, reps, *small_in.shape)
    anywhere = pl.BlockSpec(memory_space=pl.ANY)
    held = pl.BlockSpec(memory_space=pltpu.VMEM)
    rows = gg.shape[0] // n

    def shards(g):
        return g.reshape(n // 4, 2, 2, g.shape[0] // n, g.shape[1])

    shape = lambda r, c: jax.ShapeDtypeStruct((r, c), bf16)
    outs = [
        shape(rows, gg.shape[1]), shape(rows, gu.shape[1]), shape(gd.shape[0] // n, gd.shape[1]),
        shape(go.shape[0] // n, go.shape[1]), shape(rows, KEYS), shape(rows, KEYS), shape(rows, VALS),
        shape(rows, VALS), shape(rows, LANES), jax.ShapeDtypeStruct(small_in.shape, f32),
    ]
    return pl.pallas_call(
        functools.partial(scatter_kernel, n, reps, rings, small),
        out_shape=outs,
        in_specs=[anywhere] * 5 + [held],
        out_specs=[anywhere] * 9 + [held],
        scratch_shapes=[pltpu.SemaphoreType.DMA((2,))] + rings[0].scratch() + rings[1].scratch() + small.scratch(),
        compiler_params=pltpu.CompilerParams(collective_id=0, has_side_effects=True, vmem_limit_bytes=60 << 20),
    )(shards(gg), shards(gu), shards(gd), shards(go), shards(gp), small_in)


def forward_call(n, offs, lens, lin, taps, rate, bias, gain):
    held = pl.BlockSpec(memory_space=pltpu.VMEM)
    words = pl.BlockSpec(memory_space=pltpu.SMEM)

    def kernel(offs, lens, *refs):
        count = offs.shape[0]
        mixer_forward(n, [offs[i] for i in range(count)], [lens[i] for i in range(count)], *refs)

    sd = lambda s, d=f32: jax.ShapeDtypeStruct(s, d)
    return pl.pallas_call(
        kernel,
        in_specs=[words, words] + [held] * 5,
        out_specs=[held] * 7,
        out_shape=[sd((n, QKV)), sd((n, LANES)), sd((LANES, n)), sd((HEADS, n, n)), sd((n, VALS)), sd((n, VALS)), sd((n, VALS), bf16)],
        compiler_params=pltpu.CompilerParams(vmem_limit_bytes=56 << 20),
    )(offs, lens, lin, taps, rate, bias, gain)


def backward_call(n, offs, lens, lin, taps, rate, bias, gain, saved, grad_mixed):
    held = pl.BlockSpec(memory_space=pltpu.VMEM)
    words = pl.BlockSpec(memory_space=pltpu.SMEM)

    def kernel(offs, lens, *refs):
        count = offs.shape[0]
        mixer_backward(n, [offs[i] for i in range(count)], [lens[i] for i in range(count)], *refs)

    sd = lambda s, d=f32: jax.ShapeDtypeStruct(s, d)
    wide = QKV + VALS + LANES
    return pl.pallas_call(
        kernel,
        in_specs=[words, words] + [held] * 12,
        out_specs=[held] * 8,
        out_shape=[sd((n, QKV)), sd((n, LANES)), sd((LANES, n)), sd((n, wide), bf16), sd((4, QKV)), sd((1, DVH)), sd((1, LANES)), sd((1, LANES))],
        compiler_params=pltpu.CompilerParams(vmem_limit_bytes=56 << 20),
    )(offs, lens, lin, taps, rate, bias, gain, *saved, grad_mixed)


def mm(a, b):
    return jnp.dot(a, b, preferred_element_type=f32)


def local(
    reps, tokens, cotangent, deal, offsets, lengths, norm1_gain, q_weight, k_weight, v_weight, conv_weight,
    beta_weight, decay_weight, log_rate, step_bias, out_gate_weight, out_norm_gain, out_weight, norm2_gain,
    ffn_gate, ffn_up, ffn_down,
):
    rows, width = tokens.shape
    n = lax.axis_size("shard")
    per_peer = rows // n
    source = deal // rows
    local_row = deal % rows
    slot_order = jnp.argsort(source, stable=True)
    wanted = local_row[slot_order].reshape(n, per_peer)
    swap = functools.partial(lax.all_to_all, axis_name="shard", split_axis=0, concat_axis=0, tiled=True)
    asked = swap(wanted).reshape(rows)
    slot_place = jnp.argsort(slot_order)
    block_in = swap(tokens[asked].reshape(n, per_peer, width)).reshape(rows, width)[slot_place]
    block_dy = swap(cotangent[asked].reshape(n, per_peer, width)).reshape(rows, width)[slot_place]
    given_place = jnp.argsort(asked)
    gather = functools.partial(lax.all_gather, axis_name="shard", axis=0, tiled=True)
    pad = LANES - 2 * HEADS
    bd_weight = jnp.concatenate([beta_weight, decay_weight, jnp.zeros((beta_weight.shape[0], pad), bf16)], axis=1)
    proj = [gather(w) for w in (q_weight, k_weight, v_weight, out_gate_weight, bd_weight)]
    gain1, gain2, gain_o = [gather(g).astype(f32)[None, :] for g in (norm1_gain, norm2_gain, out_norm_gain)]
    taps = lax.all_gather(conv_weight, "shard", axis=1, tiled=True).astype(f32)
    w_out, w_gate, w_up, w_down = [gather(w) for w in (out_weight, ffn_gate, ffn_up, ffn_down)]
    lanes = lambda a: jnp.pad(a, (HEADS, LANES - 2 * HEADS))[None, :]
    rate, bias = lanes(log_rate), lanes(step_bias)

    x = block_in.astype(f32)
    r1 = lax.rsqrt(jnp.mean(x * x, axis=-1, keepdims=True) + 1e-5)
    normed_in = (x * r1 * gain1).astype(bf16)
    lin = jnp.concatenate([mm(normed_in, w) for w in proj], axis=1)
    saved = forward_call(rows, offsets[0], lengths[0], lin, taps, rate, bias, gain_o)
    mixed = saved[6]
    middle = x + mm(mixed, w_out)
    r2 = lax.rsqrt(jnp.mean(middle * middle, axis=-1, keepdims=True) + 1e-5)
    normed_mid = (middle * r2 * gain2).astype(bf16)
    gate, up = mm(normed_mid, w_gate), mm(normed_mid, w_up)
    sg = jax.nn.sigmoid(gate)
    hidden = (gate * sg * up).astype(bf16)
    result = (middle + mm(hidden, w_down)).astype(bf16)
    grad_down = mm(hidden.T, block_dy).astype(bf16)
    grad_hidden = mm(block_dy, w_down.T)
    grad_gate = (grad_hidden * up * (sg + gate * sg * (1.0 - sg))).astype(bf16)
    grad_up = (grad_hidden * gate * sg).astype(bf16)
    g_gate = mm(normed_mid.T, grad_gate).astype(bf16)
    g_up = mm(normed_mid.T, grad_up).astype(bf16)
    gnm = mm(grad_gate, w_gate.T) + mm(grad_up, w_up.T)
    g_norm2 = jnp.sum(gnm * middle * r2, axis=0)
    u = gnm * gain2
    grad_middle = block_dy.astype(f32) + r2 * (u - middle * (r2 * r2) * jnp.mean(u * middle, axis=-1, keepdims=True))
    branch = grad_middle.astype(bf16)
    g_out = mm(mixed.T, branch).astype(bf16)
    grad_mixed = mm(branch, w_out.T)
    back = backward_call(rows, offsets[0], lengths[0], lin, taps, rate, bias, gain_o, saved[:6], grad_mixed)
    lin_grad = back[3]
    g_proj = mm(normed_in.T, lin_grad).astype(bf16)
    grad_normed = mm(lin_grad, jnp.concatenate(proj, axis=1).T)
    g_norm1 = jnp.sum(grad_normed * x * r1, axis=0)
    u = grad_normed * gain1
    grad_in = (grad_middle + r1 * (u - x * (r1 * r1) * jnp.mean(u * x, axis=-1, keepdims=True))).astype(bf16)

    flat = jnp.concatenate([back[5][0], back[6][0], back[7][0]])
    small = jnp.concatenate(
        [
            back[4].reshape(-1, width), g_norm1[None], g_norm2[None],
            jnp.pad(flat, (0, width - flat.shape[0]))[None], jnp.zeros((1, width), f32),
        ],
        axis=0,
    )
    sums = scatter_sums(n, reps, g_gate, g_up, grad_down, g_out, g_proj, small)
    small = sums[9]
    s = lax.axis_index("shard")

    def part(a, dim=0):
        size = a.shape[dim] // n
        return lax.dynamic_slice_in_dim(a, s * size, size, dim)

    home = lambda a: swap(a[slot_order].reshape(n, per_peer, width)).reshape(rows, width)[given_place]
    f = lambda a: a.astype(f32)
    bd = sums[8]
    return (
        home(result), home(grad_in), part(small[12]), f(sums[4]), f(sums[5]), f(sums[6]),
        part(small[:12].reshape(4, QKV), 1), f(bd[:, :HEADS]), f(bd[:, HEADS : 2 * HEADS]),
        small[14, DVH + HEADS : DVH + 2 * HEADS], small[14, DVH + LANES + HEADS : DVH + LANES + 2 * HEADS],
        f(sums[7]), part(small[14, :DVH]), f(sums[3]), part(small[13]), f(sums[0]), f(sums[1]), f(sums[2]),
    )


def solution(mesh):
    rows2, shard0 = P(("rep", "shard"), None), P("shard", None)
    vec = P("shard")
    in_specs = (
        rows2, rows2, P(("rep", "shard")), rows2, rows2, vec, shard0, shard0, shard0, P(None, "shard"),
        shard0, shard0, P(), P(), shard0, vec, shard0, vec, shard0, shard0, shard0,
    )
    out_specs = (
        rows2, rows2, vec, shard0, shard0, shard0, P(None, "shard"), shard0, shard0, P(), P(), shard0,
        vec, shard0, vec, shard0, shard0, shard0,
    )
    body = functools.partial(local, mesh.shape["rep"])
    return jax.shard_map(body, mesh=mesh, in_specs=in_specs, out_specs=out_specs, check_vma=False)
```

```python
import functools
import jax
import jax.numpy as jnp
from jax import lax
from jax.experimental import pallas as pl
from jax.experimental.pallas import tpu as pltpu
from jax.sharding import PartitionSpec as P

f32 = jnp.float32
bf16 = jnp.bfloat16
HEADS = 6
DK = 128
DVH = 256
KEYS = 768
VALS = 1536
QKV = 2 * KEYS + VALS
LANES = 128


def two_parts(a):
    hi = a.astype(bf16)
    return hi, (a - hi.astype(f32)).astype(bf16)


def dot(a, b, ca=1, cb=0):
    return lax.dot_general(a, b, (((ca,), (cb,)), ((), ())), preferred_element_type=f32)


def dot3(a, b, ca=1, cb=0):
    ah, al = a
    bh, bl = b
    return dot(ah, bh, ca, cb) + (dot(ah, bl, ca, cb) + dot(al, bh, ca, cb))


def tri_dot(tri, cols):
    hi = cols.astype(bf16)
    rest = cols - hi.astype(f32)
    mid = rest.astype(bf16)
    lo = (rest - mid.astype(f32)).astype(bf16)
    return dot(tri, hi) + (dot(tri, mid) + dot(tri, lo))


def sigm(a):
    return 1.0 / (1.0 + jnp.exp(-a))


def softplus(a):
    return jnp.maximum(a, 0.0) + jnp.log1p(jnp.exp(-jnp.abs(a)))


def layout_cols(offs, lens, n, shape, dim):
    row = lax.broadcasted_iota(jnp.int32, shape, dim)
    begin = jnp.zeros_like(row)
    extent = jnp.zeros_like(row)
    for i in range(len(offs)):
        inside = row >= offs[i]
        begin = jnp.where(inside, offs[i], begin)
        extent = jnp.where(inside, lens[i], extent)
    return begin, row - begin, (row - begin) < extent


def conv_chunk(x, taps, pos, cols):
    total = taps[0:1, cols] * x
    for t in range(1, 4):
        total = total + taps[t : t + 1, cols] * jnp.where(pos >= t, pltpu.roll(x, t, 0), 0.0)
    return total


def lane_pick(a, lane, index):
    return jnp.sum(jnp.where(lane == index, a, 0.0), axis=1, keepdims=True)


def pair_masks(n, begin_c, begin_r):
    i = lax.broadcasted_iota(jnp.int32, (n, n), 0)
    j = lax.broadcasted_iota(jnp.int32, (n, n), 1)
    same = begin_c == begin_r
    return i, j, (i >= j) & same


def mixer_forward(n, offs, lens, lin, taps, rate, bias, gain, act, cum, cum_t, tinv, fresh, heads_out, mixed):
    begin_c, pos, live = layout_cols(offs, lens, n, (n, 1), 0)
    begin_r, _, _ = layout_cols(offs, lens, n, (1, n), 1)
    live_f = live.astype(f32)
    width = 384

    def conv_step(step, carry):
        cols = pl.ds(pl.multiple_of(step * width, width), width)
        pre = conv_chunk(lin[:, cols], taps, pos, cols)
        act[:, cols] = pre * sigm(pre)
        return carry

    lane = lax.broadcasted_iota(jnp.int32, (n, LANES), 1)
    bd = lin[:, QKV + VALS : QKV + VALS + LANES]
    beta = sigm(bd) * live_f
    decay = -jnp.exp(rate[...]) * softplus(bd + bias[...]) * live_f
    i, j, low = pair_masks(n, begin_c, begin_r)
    eye = (i == j).astype(f32)

    def convolve():
        lax.fori_loop(0, QKV // width, conv_step, 0)
        total = tri_dot((i >= j).astype(bf16), decay)
        cum[...] = total
        cum_t[...] = total.T

    def one_head(h):
        kcols = pl.ds(pl.multiple_of(h * DK, DK), DK)
        ka = act[:, pl.ds(pl.multiple_of(KEYS + h * DK, DK), DK)]
        qa = act[:, kcols]
        vcols = pl.ds(pl.multiple_of(h * DVH, DVH), DVH)
        v = act[:, pl.ds(pl.multiple_of(2 * KEYS + h * DVH, DVH), DVH)]
        q = qa * (lax.rsqrt(jnp.sum(qa * qa, axis=1, keepdims=True) + 1e-6) * DK**-0.5)
        k = ka * lax.rsqrt(jnp.sum(ka * ka, axis=1, keepdims=True) + 1e-6)
        beta_c = lane_pick(beta, lane, h)
        cum_c = lane_pick(cum[...], lane, HEADS + h)
        cum_r = cum_t[pl.ds(HEADS + h, 1), :]
        kk, qq = two_parts(k), two_parts(q)
        dec = jnp.where(low, jnp.exp(jnp.where(low, cum_c - cum_r, 0.0)), 0.0)
        system = jnp.where(i > j, beta_c * dot3(kk, kk, 1, 1) * dec, 0.0)
        inv = eye - jnp.where((i // 2) == (j // 2), system, 0.0)
        size = 2
        while size < n:
            off = jnp.where(((i // (2 * size)) == (j // (2 * size))) & ((i // size) != (j // size)), system, 0.0)
            parts = two_parts(inv)
            inv = inv - dot3(two_parts(dot3(parts, two_parts(off))), parts)
            size *= 2
        tinv[h] = inv
        u = dot3(two_parts(inv), two_parts(beta_c * v))
        fresh[:, vcols] = u
        o = dot3(two_parts(dot3(qq, kk, 1, 1) * dec), two_parts(u)) * live_f
        heads_out[:, vcols] = o
        gate = lin[:, pl.ds(pl.multiple_of(QKV + h * DVH, DVH), DVH)]
        scaled = o * lax.rsqrt(jnp.mean(o * o, axis=1, keepdims=True) + 1e-5)
        mixed[:, vcols] = (scaled * gain[...] * (gate * sigm(gate))).astype(bf16)

    def pair(step):
        def run():
            one_head(2 * step)
            one_head(2 * step + 1)

        return run

    return [convolve] + [pair(step) for step in range(HEADS // 2)]


def mixer_backward(
    n, offs, lens, lin, taps, rate, bias, gain, act, cum, cum_t, tinv, fresh, heads_out, grad_mixed,
    dact, dcols, drows, lin_grad, tap_grad, gain_grad, rate_grad, bias_grad,
):
    begin_c, pos, live = layout_cols(offs, lens, n, (n, 1), 0)
    begin_r, _, _ = layout_cols(offs, lens, n, (1, n), 1)
    live_f = live.astype(f32)
    lane = lax.broadcasted_iota(jnp.int32, (n, LANES), 1)
    bd = lin[:, QKV + VALS : QKV + VALS + LANES]
    sig_b = sigm(bd)
    beta = sig_b * live_f
    i, j, low = pair_masks(n, begin_c, begin_r)
    strict = low & (i > j)

    def clear():
        gain_grad[...] = jnp.zeros_like(gain_grad)
        dcols[...] = jnp.zeros_like(dcols)
        drows[...] = jnp.zeros_like(drows)

    def one_head(h):
        kcols = pl.ds(pl.multiple_of(h * DK, DK), DK)
        kcols2 = pl.ds(pl.multiple_of(KEYS + h * DK, DK), DK)
        vcols = pl.ds(pl.multiple_of(h * DVH, DVH), DVH)
        vcols2 = pl.ds(pl.multiple_of(2 * KEYS + h * DVH, DVH), DVH)
        gcols = pl.ds(pl.multiple_of(QKV + h * DVH, DVH), DVH)
        ka = act[:, kcols2]
        qa = act[:, kcols]
        v = act[:, vcols2]
        o = heads_out[:, vcols]
        gate = lin[:, gcols]
        dm = grad_mixed[:, vcols]
        ro = lax.rsqrt(jnp.mean(o * o, axis=1, keepdims=True) + 1e-5)
        scaled = o * ro
        sg = sigm(gate)
        si = gate * sg
        gain_grad[...] += jnp.sum(dm * scaled * si, axis=0, keepdims=True)
        lin_grad[:, gcols] = (dm * scaled * gain[...] * (sg + si * (1.0 - sg))).astype(bf16)
        ds = dm * gain[...] * si
        d_o = two_parts(ro * (ds - scaled * jnp.mean(ds * scaled, axis=1, keepdims=True)) * live_f)
        rq = lax.rsqrt(jnp.sum(qa * qa, axis=1, keepdims=True) + 1e-6)
        rk = lax.rsqrt(jnp.sum(ka * ka, axis=1, keepdims=True) + 1e-6)
        qhat = qa * rq
        k = ka * rk
        kk, qq = two_parts(k), two_parts(qhat * DK**-0.5)
        beta_c = lane_pick(beta, lane, h)
        cum_c = lane_pick(cum[...], lane, HEADS + h)
        cum_r = cum_t[pl.ds(HEADS + h, 1), :]
        dec = jnp.where(low, jnp.exp(jnp.where(low, cum_c - cum_r, 0.0)), 0.0)
        gram = dot3(kk, kk, 1, 1)
        qk = dot3(qq, kk, 1, 1)
        uu = two_parts(fresh[:, vcols])
        du = dot3(two_parts(qk * dec), d_o, 0, 0)
        dp = dot3(d_o, uu, 1, 1) * dec
        db = dot3(two_parts(tinv[h]), two_parts(du), 0, 0)
        da = jnp.where(strict, -dot3(two_parts(db), uu, 1, 1), 0.0) * dec
        x = da * gram
        dbeta = jnp.sum(x, axis=1, keepdims=True) + jnp.sum(db * v, axis=1, keepdims=True)
        e = dp * qk + x * beta_c
        dcols[...] += jnp.where(lane == h, dbeta, 0.0) + jnp.where(
            lane == HEADS + h, jnp.sum(e, axis=1, keepdims=True), 0.0
        )
        drows[pl.ds(HEADS + h, 1), :] = jnp.sum(e, axis=0, keepdims=True)
        dact[:, vcols2] = beta_c * db
        dg = two_parts(da * beta_c)
        dpp = two_parts(dp)
        dq = dot3(dpp, kk)
        dk = dot3(dpp, qq, 0, 0) + dot3(dg, kk) + dot3(dg, kk, 0, 0)
        dact[:, kcols] = (rq * DK**-0.5) * (dq - qhat * jnp.sum(dq * qhat, axis=1, keepdims=True))
        dact[:, kcols2] = rk * (dk - k * jnp.sum(dk * k, axis=1, keepdims=True))

    def rates():
        dcum = jnp.where((lane >= HEADS) & (lane < 2 * HEADS), dcols[...] - drows[...].T, 0.0)
        ddecay = tri_dot((i <= j).astype(bf16), dcum)
        z = bd + bias[...]
        speed = -jnp.exp(rate[...]) * live_f
        dz = ddecay * speed * sigm(z)
        rate_grad[...] = jnp.sum(ddecay * speed * softplus(z), axis=0, keepdims=True)
        bias_grad[...] = jnp.sum(dz, axis=0, keepdims=True)
        dbeta_lin = dcols[...] * live_f * sig_b * (1.0 - sig_b)
        both = jnp.where(lane < HEADS, dbeta_lin, jnp.where(lane < 2 * HEADS, dz, 0.0))
        lin_grad[:, QKV + VALS : QKV + VALS + LANES] = both.astype(bf16)

    width = 384

    def conv_step(step, carry):
        cols = pl.ds(pl.multiple_of(step * width, width), width)
        x = lin[:, cols]
        pre = conv_chunk(x, taps, pos, cols)
        sg = sigm(pre)
        dc = dact[:, cols] * (sg + pre * sg * (1.0 - sg))
        dx = taps[0:1, cols] * dc
        tap_grad[0:1, cols] = jnp.sum(dc * x, axis=0, keepdims=True)
        for t in range(1, 4):
            masked = jnp.where(pos >= t, dc, 0.0)
            dx = dx + taps[t : t + 1, cols] * pltpu.roll(masked, n - t, 0)
            tap_grad[t : t + 1, cols] = jnp.sum(masked * pltpu.roll(x, t, 0), axis=0, keepdims=True)
        lin_grad[:, cols] = dx.astype(bf16)
        return carry

    def convolve(first, last):
        return lambda: lax.fori_loop(first, last, conv_step, 0)

    heads = [functools.partial(one_head, h) for h in range(HEADS)]
    total = QKV // width
    return clear, heads, rates, [convolve(0, total // 2), convolve(total // 2, total)]


MESH = pl.DeviceIdType.MESH


class Place:
    def __init__(self, n_shard, n_rep):
        self.n, self.reps = n_shard, n_rep
        self.ys = n_shard // 4
        self.r = lax.axis_index("rep")
        self.s = lax.axis_index("shard")
        self.c = self.s % 2
        self.x = (self.s // 2) % 2
        self.y = self.s // 4
        half = n_rep // 2
        low = self.r < half
        self.depth = jnp.where(low, self.r, n_rep - 1 - self.r)
        self.inner = jnp.where(low, self.r + 1, self.r - 1)
        self.outer = jnp.where(low, self.r - 1, self.r + 1)
        self.middle = self.depth == half - 1
        self.deep = self.depth > 0

    def shard_id(self, y, x, c):
        return (self.r, (y * 2 + x) * 2 + c)

    def core_peer(self):
        return self.shard_id(self.y, self.x, 1 - self.c)

    def x_peer(self):
        return self.shard_id(self.y, 1 - self.x, self.c)

    def y_of(self, step):
        return (self.y + step) % self.ys

    def y_peer(self, step):
        return self.shard_id(self.y_of(step), self.x, self.c)


def remote(src, dst, send, recv, device):
    return pltpu.make_async_remote_copy(
        src_ref=src, dst_ref=dst, send_sem=send, recv_sem=recv, device_id=device, device_id_type=MESH
    )


def greet(place, with_rep):
    barrier = pltpu.get_barrier_semaphore()
    n = place.n
    for step in range(1, n):
        pl.semaphore_signal(
            barrier, inc=1, device_id=(place.r, (place.s + step) % n), device_id_type=MESH
        )
    if not with_rep:
        pl.semaphore_wait(barrier, n - 1)
        return
    for step in range(1, place.reps):
        pl.semaphore_signal(
            barrier, inc=1, device_id=((place.r + step) % place.reps, place.s), device_id_type=MESH
        )
    pl.semaphore_wait(barrier, n - 1 + place.reps - 1)


def add_into(dst, idx, *others):
    total = dst[idx].astype(f32)
    for ref, at in others:
        total = total + ref[at].astype(f32)
    dst[idx] = total.astype(dst.dtype)


RING = 4


def halved(rows):
    return (rows // 2) // 16 * 16


class Ring:
    def __init__(self, n, rows, cols):
        self.n, self.rows, self.cols = n, rows, cols
        self.ys = n // 4
        self.count = 0

    def scratch(self):
        k, ys, cols = RING, self.ys, self.cols
        sems = pltpu.SemaphoreType.DMA
        per = 3 + 2 * (ys - 1)
        half = self.rows - halved(self.rows)
        return [
            pltpu.VMEM((k, ys, 2, 2, self.rows, cols), bf16),
            pltpu.VMEM((k, ys, 2, self.rows, cols), bf16),
            pltpu.VMEM((k, ys, half, cols), bf16),
            pltpu.VMEM((k, ys - 1, 2, half, cols), bf16),
            pltpu.VMEM((k, ys - 1, half, cols), bf16),
            pltpu.VMEM((k, half, cols), bf16),
            pltpu.VMEM((4, k, self.rows, cols), bf16),
            sems((k, per)),
            sems((k, per)),
            sems((k, 7)),
        ]

    def bind(self, refs):
        (self.own, self.r0, self.r1a, self.r1b, self.r2a, self.r2b, self.z, self.send, self.recv, self.zsem) = refs


class Piece:
    def __init__(self, ring, place, rows, cols, out, out_cols):
        self.ring, self.p, self.rows = ring, place, rows
        self.slot = ring.count % RING
        ring.count += 1
        self.w = pl.ds(0, cols)
        self.ra = halved(rows)
        self.rb = rows - self.ra
        self.all_rows = pl.ds(0, rows)
        self.out = out.at[:, pl.ds(out_cols, cols)]

    def own_view(self):
        return self.ring.own.at[self.slot, :, :, :, self.all_rows, self.w]

    def store_rows(self, value):
        ring = self.ring
        shaped = value.reshape(ring.ys, 2, 2, rinself.rows, value.shape[-1])
        ring.own[self.slot, :, :, :, self.all_rows, self.w] = shaped

    def send_core(self):
        g, p, k = self.ring, self.p, self.slot
        self.c0 = remote(
            g.own.at[k, :, :, 1 - p.c, self.all_rows, self.w], g.r0.at[k, :, :, self.all_rows, self.w],
            g.send.at[k, 0], g.recv.at[k, 0], p.core_peer(),
        )
        self.c0.start()

    def after_core(self):
        g, p, k, w = self.ring, self.p, self.slot, self.w
        rows = self.all_rows
        self.c0.wait()

        def step(q, carry):
            yy, xx = q // 2, q % 2
            add_into(g.own, (k, yy, xx, p.c, rows, w), (g.r0, (k, yy, xx, rows, w)))
            return carry

        lax.fori_loop(0, g.ys * 2, step, 0)
        top, low = pl.ds(0, self.ra), pl.ds(self.ra, self.rb)
        first, second = pl.ds(0, self.ra), pl.ds(0, self.rb)
        self.c1 = [
            remote(
                g.own.at[k, :, 1 - p.x, p.c, top, w], g.r1a.at[k, :, first, w],
                g.send.at[k, 1], g.recv.at[k, 1], p.x_peer(),
            )
        ]
        for d in range(1, g.ys):
            self.c1.append(
                remote(
                    g.own.at[k, p.y_of(d), :, p.c, low, w], g.r1b.at[k, d - 1, :, second, w],
                    g.send.at[k, 1 + d], g.recv.at[k, 1 + d], p.y_peer(d),
                )
            )
        for c in self.c1:
            c.start()

    def after_first(self):
        g, p, k, w = self.ring, self.p, self.slot, self.w
        top, low = pl.ds(0, self.ra), pl.ds(self.ra, self.rb)
        first, second = pl.ds(0, self.ra), pl.ds(0, self.rb)
        for c in self.c1:
            c.wait()
        for yy in range(g.ys):
            add_into(g.own, (k, yy, p.x, p.c, top, w), (g.r1a, (k, yy, first, w)))
        for xx in range(2):
            add_into(
                g.own, (k, p.y, xx, p.c, low, w),
                *[(g.r1b, (k, d, xx, second, w)) for d in range(g.ys - 1)],
            )
        self.c2 = [
            remote(
                g.own.at[k, p.y, 1 - p.x, p.c, low, w], g.r2b.at[k, second, w],
                g.send.at[k, 1 + g.ys], g.recv.at[k, 1 + g.ys], p.x_peer(),
            )
        ]
        for d in range(1, g.ys):
            self.c2.append(
                remote(
                    g.own.at[k, p.y_of(d), p.x, p.c, top, w], g.r2a.at[k, d - 1, first, w],
                    g.send.at[k, 1 + g.ys + d], g.recv.at[k, 1 + g.ys + d], p.y_peer(d),
                )
            )
        for c in self.c2:
            c.start()

    def after_second(self):
        g, p, k, w = self.ring, self.p, self.slot, self.w
        for c in self.c2:
            c.wait()
        total = g.own[k, p.y, p.x, p.c, 0 : self.ra, w].astype(f32)
        for d in range(g.ys - 1):
            total = total + g.r2a[k, d, 0 : self.ra, w].astype(f32)
        g.z[0, k, 0 : self.ra, w] = total.astype(bf16)
        total = g.own[k, p.y, p.x, p.c, self.ra : self.rows, w].astype(f32) + g.r2b[k, 0 : self.rb, w].astype(f32)
        g.z[0, k, self.ra : self.rows, w] = total.astype(bf16)
        z = lambda i: g.z.at[i, k, self.all_rows, w]
        target = lambda r: (r, p.s)
        sem = g.zsem
        self.up = remote(z(0), z(1), sem.at[k, 0], sem.at[k, 1], target(p.inner))
        self.meet = remote(z(0), z(2), sem.at[k, 2], sem.at[k, 3], target(p.inner))
        self.down = remote(z(3), z(2), sem.at[k, 4], sem.at[k, 3], target(p.outer))
        self.home = pltpu.make_async_copy(z(3), self.out, sem.at[k, 6])

        @pl.when(p.depth == 0)
        def _():
            self.send_inward()

    def send_inward(self):
        p = self.p

        @pl.when(p.middle)
        def _():
            self.meet.start()

        @pl.when(jnp.logical_not(p.middle))
        def _():
            self.up.start()

    def after_up(self):
        g, p, k, w = self.ring, self.p, self.slot, self.w

        @pl.when(p.deep)
        def _():
            self.up.wait_recv()
            add_into(g.z, (0, k, self.all_rows, w), (g.z, (1, k, self.all_rows, w)))
            self.send_inward()

    def finish(self, middle):
        g, p, k, w = self.ring, self.p, self.slot, self.w
        rows = self.all_rows

        @pl.when(p.middle if middle else jnp.logical_not(p.middle))
        def _():
            self.meet.wait_recv()
            if middle:
                both = g.z[0, k, rows, w].astype(f32) + g.z[2, k, rows, w].astype(f32)
                g.z[3, k, rows, w] = both.astype(bf16)
            else:
                g.z[3, k, rows, w] = g.z[2, k, rows, w]

            @pl.when(p.deep)
            def _():
                self.down.start()

            self.home.start()

    def close(self):
        p = self.p

        @pl.when(p.middle)
        def _():
            self.meet.wait_send()

        @pl.when(jnp.logical_not(p.middle))
        def _():
            self.up.wait_send()

        @pl.when(p.deep)
        def _():
            self.down.wait_send()

        self.home.wait()


def pump(pieces, index):
    stages = [
        (7, lambda q: q.close()),
        (6, lambda q: q.finish(False)),
        (5, lambda q: q.finish(True)),
        (4, lambda q: q.after_up()),
        (3, lambda q: q.after_second()),
        (2, lambda q: q.after_first()),
        (1, lambda q: q.after_core()),
    ]
    for lag, act in stages:
        if 0 <= index - lag < len(pieces):
            act(pieces[index - lag])


class Small:
    def __init__(self, n, reps, rows, cols):
        self.n, self.ys, self.reps = n, n // 4, reps
        self.sizes = (2, 2, self.ys, reps)
        self.rows, self.cols = rows, cols

    def scratch(self):
        total = sum(self.sizes)
        return [
            pltpu.VMEM((total, self.rows, self.cols), f32),
            pltpu.SemaphoreType.DMA((total,)),
            pltpu.SemaphoreType.DMA((total,)),
        ]

    def bind(self, refs):
        self.buf, self.send, self.recv = refs

    def begin(self, place, axis, value):
        base = sum(self.sizes[:axis])
        size = self.sizes[axis]
        p = place
        mine = (p.c, p.x, p.y, p.r)[axis]
        slot = self.buf.at[base + mine]
        slot[...] = value
        self.copies = []
        for d in range(1, size):
            at = (mine + d) % size
            device = (
                p.shard_id(p.y, p.x, at), p.shard_id(p.y, at, p.c), p.shard_id(at, p.x, p.c), (at, p.s),
            )[axis]
            self.copies.append(remote(slot, slot, self.send.at[base + d], self.recv.at[base + d], device))
        for c in self.copies:
            c.start()

    def end(self, axis):
        base = sum(self.sizes[:axis])
        for c in self.copies:
            c.wait()
        total = self.buf[base]
        for d in range(1, self.sizes[axis]):
            total = total + self.buf[base + d]
        return total


class Flow:
    COUNT = staticmethod(lambda ys: 3 + 6 * (ys - 1))

    def __init__(self, place, src, src_at, cols, dst, dst_at, send, recv, base, mine):
        self.p, self.rows = place, src.shape[0]
        self.src = src.at[:, pl.ds(src_at, cols)]
        self.dst, self.cols = dst, pl.ds(dst_at, cols)
        self.send, self.recv, self.base, self.used = send, recv, base, 0
        self.ra = halved(self.rows)
        self.mine = pltpu.make_async_copy(self.src, self.region(place.y, place.x, place.c), mine)
        self.all = []

    def region(self, y, x, c, half=None):
        start = ((y * 2 + x) * 2 + c) * self.rows
        size = self.rows
        if half == 0:
            size = self.ra
        elif half == 1:
            start, size = start + self.ra, self.rows - self.ra
        return self.dst.at[pl.ds(pl.multiple_of(start, 16), size), self.cols]

    def copy(self, dst, device, src=None):
        at = self.base + self.used
        self.used += 1
        c = remote(dst if src is None else src, dst, self.send.at[at], self.recv.at[at], device)
        c.start()
        self.all.append(c)
        return c

    def begin(self):
        p = self.p
        own = self.region(p.y, p.x, p.c)
        self.mine.start()
        self.from_x = self.copy(own, p.x_peer(), self.src)
        self.from_y = [self.copy(own, p.y_peer(d), self.src) for d in range(1, p.ys)]
        self.from_core = [self.copy(own, p.core_peer(), self.src)]

    def forward(self):
        p = self.p
        steps = range(1, p.ys)
        self.from_x.wait_recv()
        self.diag = [self.copy(self.region(p.y, 1 - p.x, p.c, 0), p.y_peer(d)) for d in steps]
        self.from_core.append(self.copy(self.region(p.y, 1 - p.x, p.c), p.core_peer()))
        for d in steps:
            self.from_y[d - 1].wait_recv()
            back = p.y_of(p.ys - d)
            self.diag.append(self.copy(self.region(back, p.x, p.c, 1), p.x_peer()))
            self.from_core.append(self.copy(self.region(back, p.x, p.c), p.core_peer()))

    def relay(self):
        p = self.p
        for i, c in enumerate(self.diag):
            c.wait_recv()
            half, d = divmod(i, p.ys - 1)
            back = p.y_of(p.ys - d - 1)
            self.from_core.append(self.copy(self.region(back, 1 - p.x, p.c, half), p.core_peer()))

    def done(self):
        for c in self.from_core:
            c.wait_recv()
        self.mine.wait()

    def close(self):
        for c in self.all:
            c.wait_send()


FF_SPLIT = 1536
FTILE = 256


def one_hot_rows(values, count):
    return lax.broadcasted_iota(jnp.int32, (count, values.shape[1]), 0) == values


class Store:
    def __init__(self, sem):
        self.sem, self.all = sem, []

    def put(self, src, dst):
        c = pltpu.make_async_copy(src, dst, self.sem.at[len(self.all)])
        c.start()
        self.all.append(c)

    def wait(self):
        for c in self.all:
            c.wait()


FORWARD_SAVED = (
    ("xin", lambda n, d, f: ((n, d), bf16)),
    ("dy", lambda n, d, f: ((n, d), bf16)),
    ("normed_t", lambda n, d, f: ((d, n), bf16)),
    ("lin", lambda n, d, f: ((n, QKV + VALS + LANES), f32)),
    ("act", lambda n, d, f: ((n, QKV), f32)),
    ("cum", lambda n, d, f: ((n, LANES), f32)),
    ("cum_t", lambda n, d, f: ((LANES, n), f32)),
    ("tinv", lambda n, d, f: ((HEADS, n, n), f32)),
    ("fresh", lambda n, d, f: ((n, VALS), f32)),
    ("heads", lambda n, d, f: ((n, VALS), f32)),
    ("mixed_t", lambda n, d, f: ((VALS, n), bf16)),
    ("middle", lambda n, d, f: ((n, d), f32)),
    ("normed_mid_t", lambda n, d, f: ((d, n), bf16)),
    ("hidden", lambda n, d, f: ((n, f), bf16)),
    ("hidden_t", lambda n, d, f: ((f, n), bf16)),
    ("grads_gu", lambda n, d, f: ((n, 2 * f), bf16)),
    ("pick", lambda n, d, f: ((n, n), bf16)),
    ("place", lambda n, d, f: ((n, n), bf16)),
    ("params", lambda n, d, f: ((16, d), f32)),
    ("taps", lambda n, d, f: ((4, QKV), f32)),
)


def transposed(a):
    return a.T.astype(bf16)


def forward_kernel(n_shard, reps, *refs):
    take = iter(refs)
    get = lambda k: [next(take) for _ in range(k)]
    offs, lens, tokens, cot, deal, small_in, rate, bias = get(8)
    wq, wk, wv, wt, wb, wo, wg, wu, wd = get(9)
    gp, go, gg, gu, gd = get(5)
    outs = dict(zip([name for name, _ in FORWARD_SAVED], get(len(FORWARD_SAVED))))
    kept = dict(zip([name for name, _ in FORWARD_SAVED], get(len(FORWARD_SAVED))))
    (dealt, dsend, drecv, smalls, ssend, srecv, sent, come, tsend, trecv, wbuf, wobuf, wdbuf, load_sem, fsend, frecv,
     mine_sem, out_sem, normed, mixed, normed_mid) = get(21)
    rows, width = tokens.shape
    per = rows // n_shard
    place = Place(n_shard, reps)
    p = place
    greet(place, False)
    offsets = [offs[i] for i in range(offs.shape[0])]
    lengths = [lens[i] for i in range(lens.shape[0])]
    store = Store(out_sem)

    dealt[p.s] = deal[...]
    smalls[p.s] = small_in[...]
    first = []
    for d in range(1, n_shard):
        to = (p.r, (p.s + d) % n_shard)
        first.append(remote(dealt.at[p.s], dealt.at[p.s], dsend.at[d], drecv.at[d], to))
        first[-1].start()
    for d in range(1, n_shard):
        to = (p.r, (p.s + d) % n_shard)
        first.append(remote(smalls.at[p.s], smalls.at[p.s], ssend.at[d], srecv.at[d], to))
        first[-1].start()

    per_flow = Flow.COUNT(p.ys)
    made = []

    def flow(src, at, cols, dst, dst_at):
        k = len(made)
        made.append(Flow(place, src, at, cols, dst, dst_at, fsend, frecv, k * per_flow, mine_sem.at[k]))
        return made[-1]

    ff = wg.shape[1]
    stages = [
        [flow(wq, 0, KEYS, gp, 0), flow(wk, 0, KEYS, gp, KEYS)],
        [flow(wv, 0, VALS, gp, 2 * KEYS)],
        [flow(wt, 0, VALS, gp, QKV), flow(wb, 0, LANES, gp, QKV + VALS)],
        [flow(wo, 0, width, go, 0)],
        [flow(wd, 0, width // 2, gd, 0)],
        [flow(wd, width // 2, width // 2, gd, width // 2)],
        [flow(wg, 0, FF_SPLIT, gg, 0)],
        [flow(wu, 0, FF_SPLIT, gu, 0)],
        [flow(wg, FF_SPLIT, ff - FF_SPLIT, gg, FF_SPLIT)],
        [flow(wu, FF_SPLIT, ff - FF_SPLIT, gu, FF_SPLIT)],
    ]

    def advance(k):
        for lag, act in ((0, "begin"), (2, "forward"), (3, "relay"), (4, "done")):
            if 0 <= k - lag < len(stages):
                for f in stages[k - lag]:
                    getattr(f, act)()

    loads = {}

    def load(name, src, dst):
        loads[name] = pltpu.make_async_copy(src, dst, load_sem.at[len(loads)])
        loads[name].start()

    for c in first[: n_shard - 1]:
        c.wait_recv()
    i = lax.broadcasted_iota(jnp.int32, (rows, rows), 0)
    j = lax.broadcasted_iota(jnp.int32, (rows, rows), 1)
    upper = (i <= j).astype(bf16)
    everyone = dealt[:, 0, :]
    to_me = (everyone // rows) == p.s
    rank = dot(to_me.astype(f32).astype(bf16), upper).astype(jnp.int32) - 1
    rank = jnp.where(to_me, rank, -1)
    for b in range(n_shard):
        picked = one_hot_rows(rank[b : b + 1, :], per).astype(f32).astype(bf16)
        which = one_hot_rows(everyone[b : b + 1, :] % rows, rows).astype(f32).astype(bf16)
        kept["pick"][b * per : (b + 1) * per, :] = dot(picked, which, 1, 1).astype(bf16)
    pick = kept["pick"][...]
    exchange = []
    for a, src in enumerate((tokens, cot)):
        for at in range(0, width, 256):
            sent[a, :, at : at + 256] = dot(pick, src[:, at : at + 256]).astype(bf16)
        for d in range(1, n_shard):
            t = (p.s + d) % n_shard
            exchange.append(
                remote(
                    sent.at[a, pl.ds(pl.multiple_of(t * per, 16), per)],
                    come.at[a, pl.ds(pl.multiple_of(p.s * per, 16), per)],
                    tsend.at[a, d], trecv.at[a, d], (p.r, t),
                )
            )
            exchange[-1].start()
        if a == 0:
            advance(0)
            advance(1)
        here = pl.ds(pl.multiple_of(p.s * per, 16), per)
        come[a, here, :] = sent[a, here, :]
    mine = deal[0:1, :]
    source = mine // rows
    from_each = one_hot_rows(source, n_shard)
    cum = dot(from_each.astype(f32).astype(bf16), upper)
    slot = jnp.sum(jnp.where(from_each, cum, 0.0), axis=0, keepdims=True).astype(jnp.int32) - 1 + source * per
    kept["place"][...] = one_hot_rows(slot, rows).astype(f32).astype(bf16)
    store.put(kept["pick"], outs["pick"])
    store.put(kept["place"], outs["place"])

    for c in first[n_shard - 1 :]:
        c.wait_recv()
    total = smalls[0].astype(f32)
    for t in range(1, n_shard):
        total = total + smalls[t].astype(f32)
    kept["params"][...] = total
    for t in range(4):
        for g in range(QKV // width):
            row = t * (QKV // width) + g
            kept["taps"][t : t + 1, g * width : (g + 1) * width] = total[row : row + 1, :]
    gain1, gain2 = kept["params"].at[12:13, :], kept["params"].at[13:14, :]
    gain_o = kept["params"].at[14:15, 0:DVH]
    store.put(kept["params"], outs["params"])
    store.put(kept["taps"], outs["taps"])

    for a, name in enumerate(("xin", "dy")):
        for c in exchange[a * (n_shard - 1) : (a + 1) * (n_shard - 1)]:
            c.wait_recv()
        for at in range(0, width, 256):
            kept[name][:, at : at + 256] = dot(kept["place"][...], come[a, :, at : at + 256], 0, 0).astype(bf16)
        store.put(kept[name], outs[name])
    x = kept["xin"][...].astype(f32)
    norm = x * lax.rsqrt(jnp.mean(x * x, axis=1, keepdims=True) + 1e-5) * gain1[...]
    normed[...] = norm.astype(bf16)
    kept["normed_t"][...] = transposed(norm)
    store.put(kept["normed_t"], outs["normed_t"])

    def project(at, cols, tile):
        def step(k, carry):
            here = pl.ds(pl.multiple_of(at + k * tile, 128), tile)
            kept["lin"][:, here] = dot(normed[...], wbuf[:, here])
            return carry

        lax.fori_loop(0, cols // tile, step, 0)

    def fetch(name, at, cols):
        here = pl.ds(at, cols)
        load(name, gp.at[:, here], wbuf.at[:, here])

    advance(2)
    advance(3)
    advance(4)
    fetch("qk", 0, 2 * KEYS)
    advance(5)
    fetch("v", 2 * KEYS, VALS)
    loads["qk"].wait()
    project(0, 2 * KEYS, 256)
    advance(6)
    fetch("gb", QKV, VALS + LANES)
    loads["v"].wait()
    project(2 * KEYS, VALS, 256)
    loads["gb"].wait()
    project(QKV, VALS, 256)
    project(QKV + VALS, LANES, LANES)
    store.put(kept["lin"], outs["lin"])
    steps = mixer_forward(
        rows, offsets, lengths, kept["lin"], kept["taps"], rate, bias, gain_o, kept["act"], kept["cum"],
        kept["cum_t"], kept["tinv"], kept["fresh"], kept["heads"], mixed,
    )
    steps[0]()
    steps[1]()
    advance(7)
    load("out", go, wobuf)
    steps[2]()
    advance(8)
    steps[3]()
    for name in ("act", "cum", "cum_t", "tinv", "fresh", "heads"):
        store.put(kept[name], outs[name])
    advance(9)
    load("down", gd, wdbuf)
    loads["out"].wait()

    def out_step(k, carry):
        here = pl.ds(pl.multiple_of(k * 256, 256), 256)
        kept["middle"][:, here] = kept["xin"][:, here].astype(f32) + dot(mixed[...], wobuf[:, here])
        return carry

    lax.fori_loop(0, width // 256, out_step, 0)
    store.put(kept["middle"], outs["middle"])
    m = kept["middle"][...]
    norm = m * lax.rsqrt(jnp.mean(m * m, axis=1, keepdims=True) + 1e-5) * gain2[...]
    normed_mid[...] = norm.astype(bf16)
    kept["normed_mid_t"][...] = transposed(norm)
    store.put(kept["normed_mid_t"], outs["normed_mid_t"])
    kept["mixed_t"][...] = transposed(mixed[...].astype(f32))
    store.put(kept["mixed_t"], outs["mixed_t"])
    advance(10)

    def ffn(at, cols, up_at):
        def step(k, carry):
            here = pl.ds(pl.multiple_of(at + k * FTILE, FTILE), FTILE)
            there = pl.ds(pl.multiple_of(ff + at + k * FTILE, FTILE), FTILE)
            grad = dot(kept["dy"][...], wdbuf[here, :], 1, 1)
            gate = dot(normed_mid[...], wbuf[:, here])
            up = dot(normed_mid[...], wbuf[:, there])
            sg = sigm(gate)
            silu = gate * sg
            hid = silu * up
            kept["hidden"][:, here] = hid.astype(bf16)
            kept["hidden_t"][here, :] = transposed(hid)
            kept["grads_gu"][:, here] = (grad * up * (sg + silu * (1.0 - sg))).astype(bf16)
            kept["grads_gu"][:, there] = (grad * silu).astype(bf16)
            return carry

        lax.fori_loop(0, cols // FTILE, step, 0)

    low, high = pl.ds(0, FF_SPLIT), pl.ds(FF_SPLIT, ff - FF_SPLIT)
    shift = lambda s: pl.ds(ff + s.start, s.size)
    load("g0", gg.at[:, low], wbuf.at[:, low])
    advance(11)
    load("u0", gu.at[:, low], wbuf.at[:, shift(low)])
    advance(12)
    load("g1", gg.at[:, high], wbuf.at[:, high])
    for name in ("down", "g0", "u0"):
        loads[name].wait()
    ffn(0, FF_SPLIT, 0)
    advance(13)
    load("u1", gu.at[:, high], wbuf.at[:, shift(high)])
    loads["g1"].wait()
    loads["u1"].wait()
    ffn(FF_SPLIT, ff - FF_SPLIT, 0)
    for name in ("hidden", "hidden_t", "grads_gu"):
        store.put(kept[name], outs[name])
    for c in first + exchange:
        c.wait_send()
    for f in made:
        f.close()
    store.wait()


def forward_call(n_shard, reps, offs, lens, tokens, cot, deal, small_in, rate, bias, weights):
    anywhere = pl.BlockSpec(memory_space=pl.ANY)
    held = pl.BlockSpec(memory_space=pltpu.VMEM)
    words = pl.BlockSpec(memory_space=pltpu.SMEM)
    rows, width = tokens.shape
    ff = weights[6].shape[1]
    sd = jax.ShapeDtypeStruct
    wide = QKV + VALS + LANES
    vals_rows, ff_rows = weights[5].shape[0] * n_shard, weights[8].shape[0] * n_shard
    gathered = [
        sd((width, wide), bf16), sd((vals_rows, width), bf16), sd((width, ff), bf16), sd((width, ff), bf16),
        sd((ff_rows, width), bf16),
    ]
    shapes = [fn(rows, width, ff) for _, fn in FORWARD_SAVED]
    sems = pltpu.SemaphoreType.DMA
    flows = 12
    count = flows * Flow.COUNT(n_shard // 4)
    scratch = [pltpu.VMEM(s, d) for s, d in shapes] + [
        pltpu.VMEM((n_shard, 8, rows), jnp.int32), sems((n_shard,)), sems((n_shard,)),
        pltpu.VMEM((n_shard, 16, width), bf16), sems((n_shard,)), sems((n_shard,)),
        pltpu.VMEM((2, rows, width), bf16), pltpu.VMEM((2, rows, width), bf16), sems((2, n_shard)), sems((2, n_shard)),
        pltpu.VMEM((width, 2 * ff), bf16), pltpu.VMEM((vals_rows, width), bf16), pltpu.VMEM((ff_rows, width), bf16),
        sems((16,)), sems((count,)), sems((count,)), sems((flows,)), sems((len(shapes),)),
        pltpu.VMEM((rows, width), bf16), pltpu.VMEM((rows, VALS), bf16), pltpu.VMEM((rows, width), bf16),
    ]
    res = pl.pallas_call(
        functools.partial(forward_kernel, n_shard, reps),
        in_specs=[words, words] + [held] * 6 + [anywhere] * 9,
        out_specs=[anywhere] * (5 + len(shapes)),
        out_shape=gathered + [sd(s, d) for s, d in shapes],
        scratch_shapes=scratch,
        compiler_params=pltpu.CompilerParams(collective_id=1, has_side_effects=True, vmem_limit_bytes=62 << 20),
    )(offs, lens, tokens, cot, deal, small_in, rate, bias, *weights)
    return res[:5], dict(zip([name for name, _ in FORWARD_SAVED], res[5:]))


WIDE = 512
NARROW = 256


class Stream:
    def __init__(self, buf, sem, parts):
        self.buf, self.sem, self.parts, self.at = buf, sem, parts, 0
        self.copies = {}

    def start(self):
        self.issue(0)

    def issue(self, k):
        if k < len(self.parts):
            pairs = self.parts[k](self.buf.at[k % 2])
            self.copies[k] = [pltpu.make_async_copy(s, d, self.sem.at[k % 2, i]) for i, (s, d) in enumerate(pairs)]
            for c in self.copies[k]:
                c.start()

    def take(self):
        k = self.at
        self.at += 1
        self.issue(k + 1)
        for c in self.copies[k]:
            c.wait()
        return k, self.buf.at[k % 2]


BACK_KEPT = tuple(name for name, _ in FORWARD_SAVED if name not in ("hidden",))


def backward_kernel(n_shard, reps, rings, small, *refs):
    take = iter(refs)
    get = lambda k: [next(take) for _ in range(k)]
    offs, lens, rate, bias = get(4)
    gp, go, gg, gu, gd = get(5)
    given = dict(zip(BACK_KEPT, get(len(BACK_KEPT))))
    o_rows, o_grad, o_ffn, o_down, o_out, o_proj, o_small = get(7)
    kept = dict(zip(BACK_KEPT, get(len(BACK_KEPT))))
    ring_a, ring_b = rings
    ring_a.bind(get(10))
    ring_b.bind(get(10))
    small.bind(get(3))
    (load_sem, wbuf, wsem, nbuf, nsem, acc, middle_grad, branch, mix_grad, dcols, drows, lin_grad, tap_grad, gain_grad,
     rate_grad, bias_grad, small_v, sent, come, tsend, trecv, rows_out, out_sem) = get(23)
    rows, width = kept["xin"].shape
    ff = gg.shape[1]
    per = rows // n_shard
    place = Place(n_shard, reps)
    p = place
    offsets = [offs[i] for i in range(offs.shape[0])]
    lengths = [lens[i] for i in range(lens.shape[0])]
    loads = {}
    order = (
        "normed_mid_t", "grads_gu", "middle", "dy", "params", "hidden_t", "cum", "cum_t", "tinv", "fresh", "heads",
        "act", "lin", "taps", "mixed_t", "normed_t", "xin", "pick", "place",
    )
    for k, name in enumerate(order):
        loads[name] = pltpu.make_async_copy(given[name], kept[name], load_sem.at[k])
        loads[name].start()
    have = set()

    def need(*names):
        for name in names:
            if name not in have:
                have.add(name)
                loads[name].wait()

    greet(place, True)
    pieces = []

    def tick(piece=None, fill=None):
        index = tick.index
        tick.index += 1
        pump(pieces, index)
        if piece is not None:
            pieces.append(piece())
            fill(pieces[-1])
            pieces[-1].send_core()

    tick.index = 0

    def grad_piece(ring, size, left, right, cols, out, out_at):
        def fill(piece):
            def step(t, carry):
                c, q = t % 2, t // 2
                here = pl.ds(pl.multiple_of(t * size, 16), size)
                value = dot(left[here, :], right)
                ring.own[piece.slot, q // 2, q % 2, c, pl.ds(0, size), pl.ds(0, cols)] = value.astype(bf16)
                return carry

            lax.fori_loop(0, n_shard, step, 0)

        tick(lambda: Piece(ring, place, size, cols, out, out_at), fill)

    rows_a = width // n_shard

    def gu_piece(k):
        need("normed_mid_t", "grads_gu")
        at = k * WIDE
        grad_piece(ring_a, rows_a, kept["normed_mid_t"], kept["grads_gu"][:, at : at + WIDE], WIDE, o_ffn, at)

    def down_piece(k):
        need("hidden_t", "dy")
        at = k * NARROW
        grad_piece(ring_b, ff // n_shard, kept["hidden_t"], kept["dy"][:, at : at + NARROW], NARROW, o_down, at)

    def out_piece(k):
        need("mixed_t")
        at = k * NARROW
        grad_piece(ring_b, VALS // n_shard, kept["mixed_t"], branch[:, at : at + NARROW], NARROW, o_out, at)

    def proj_piece(at, cols):
        need("normed_t")
        grad_piece(ring_a, rows_a, kept["normed_t"], lin_grad[:, at : at + cols], cols, o_proj, at)

    def gu_part(k):
        cols = pl.ds(k * FTILE, FTILE)
        return lambda b: [(gg.at[:, cols], b.at[:, pl.ds(0, FTILE)]), (gu.at[:, cols], b.at[:, pl.ds(FTILE, FTILE)])]

    chunks = ff // FTILE
    gu_stream = Stream(wbuf, wsem, [gu_part(k) for k in range(chunks)])

    def gnm(count):
        need("grads_gu")
        for _ in range(count):
            k, buf = gu_stream.take()
            at = k * FTILE
            part = dot(kept["grads_gu"][:, at : at + FTILE], buf[:, 0:FTILE], 1, 1)
            part = part + dot(kept["grads_gu"][:, ff + at : ff + at + FTILE], buf[:, FTILE : 2 * FTILE], 1, 1)
            acc[...] = part if k == 0 else acc[...] + part

    def norm_back(values, gain, upstream):
        n = lax.rsqrt(jnp.mean(values * values, axis=1, keepdims=True) + 1e-5)
        u = upstream * gain
        gain_part = jnp.sum(upstream * values * n, axis=0, keepdims=True)
        return n * (u - values * (n * n) * jnp.mean(u * values, axis=1, keepdims=True)), gain_part

    def norm2():
        need("middle", "dy", "params")
        back, gain_part = norm_back(kept["middle"][...], kept["params"][13:14, :], acc[...])
        small_v[13:14, :] = gain_part
        total = kept["dy"][...].astype(f32) + back
        middle_grad[...] = total
        branch[...] = total.astype(bf16)

    def row_part(src, k):
        return lambda b: [(src.at[pl.ds(k * FTILE, FTILE), :], b)]

    out_stream = Stream(nbuf, nsem, [row_part(go, k) for k in range(VALS // FTILE)])
    down_stream = Stream(nbuf, nsem, [row_part(gd, k) for k in range(chunks)])

    def grad_mixed(count):
        for _ in range(count):
            k, buf = out_stream.take()
            mix_grad[:, k * FTILE : (k + 1) * FTILE] = dot(branch[...], buf[...], 1, 1)

    def result(count):
        need("hidden_t", "middle")
        for _ in range(count):
            k, buf = down_stream.take()
            part = dot(kept["hidden_t"][k * FTILE : (k + 1) * FTILE, :], buf[...], 0, 0)
            acc[...] = (kept["middle"][...] if k == 0 else acc[...]) + part

    exchange = {}

    def send_home(a, value):
        need("place")
        here = pl.ds(pl.multiple_of(p.s * per, 16), per)
        for at in range(0, width, 256):
            sent[a, :, at : at + 256] = dot(kept["place"][...], value[:, at : at + 256]).astype(bf16)
        exchange[a] = []
        for d in range(1, n_shard):
            t = (p.s + d) % n_shard
            exchange[a].append(
                remote(
                    sent.at[a, pl.ds(pl.multiple_of(t * per, 16), per)], come.at[a, here],
                    tsend.at[a, d], trecv.at[a, d], (p.r, t),
                )
            )
            exchange[a][-1].start()
        come[a, here, :] = sent[a, here, :]

    stores = []

    def arrive(a, out):
        need("pick")
        for c in exchange[a]:
            c.wait()
        for at in range(0, width, 256):
            rows_out[a, :, at : at + 256] = dot(kept["pick"][...], come[a, :, at : at + 256], 0, 0).astype(bf16)
        stores.append(pltpu.make_async_copy(rows_out.at[a], out, out_sem.at[a]))
        stores[-1].start()

    def wide_part(at, cols):
        return lambda b: [(gp.at[:, pl.ds(at, cols)], b.at[:, pl.ds(0, cols)])]

    proj_cuts = [(at, WIDE) for at in range(0, QKV + VALS, WIDE)] + [(QKV + VALS, LANES)]
    proj_stream = Stream(wbuf, wsem, [wide_part(at, cols) for at, cols in proj_cuts])

    def grad_normed(count):
        for _ in range(count):
            k, buf = proj_stream.take()
            at, cols = proj_cuts[k]
            part = dot(lin_grad[:, at : at + cols], buf[:, 0:cols], 1, 1)
            acc[...] = part if k == 0 else acc[...] + part

    def norm1():
        need("xin")
        back, gain_part = norm_back(kept["xin"][...].astype(f32), kept["params"][12:13, :], acc[...])
        small_v[12:13, :] = gain_part
        rows_out[1] = (middle_grad[...] + back).astype(bf16)

    def pack_small():
        small_v[14:16, :] = jnp.zeros((2, width), f32)
        for t in range(4):
            for g in range(QKV // width):
                row = t * (QKV // width) + g
                small_v[row : row + 1, :] = tap_grad[t : t + 1, g * width : (g + 1) * width]
        small_v[14:15, 0:DVH] = gain_grad[...]
        small_v[14:15, DVH : DVH + LANES] = rate_grad[...]
        small_v[14:15, DVH + LANES : DVH + 2 * LANES] = bias_grad[...]

    gu_stream.start()
    gu_piece(0)
    gnm(2)
    gu_piece(1)
    gnm(3)
    gu_piece(2)
    gnm(3)
    gu_piece(3)
    gnm(3)
    out_stream.start()
    gu_piece(4)
    norm2()
    gu_piece(5)
    grad_mixed(VALS // FTILE)
    need("cum", "cum_t", "tinv", "fresh", "heads", "act", "lin", "taps")
    clear, heads, rates, convs = mixer_backward(
        rows, offsets, lengths, kept["lin"], kept["taps"], rate, bias, kept["params"].at[14:15, 0:DVH], kept["act"],
        kept["cum"], kept["cum_t"], kept["tinv"], kept["fresh"], kept["heads"], mix_grad,
        kept["act"], dcols, drows, lin_grad, tap_grad, gain_grad, rate_grad, bias_grad,
    )
    clear()
    gu_piece(6)
    heads[0]()
    gu_piece(7)
    heads[1]()
    gu_piece(8)
    heads[2]()
    gu_piece(9)
    heads[3]()
    gu_piece(10)
    heads[4]()
    down_piece(0)
    heads[5]()
    down_piece(1)
    rates()
    convs[0]()
    down_piece(2)
    down_stream.start()
    convs[1]()
    down_piece(3)
    result(chunks // 2)
    out_piece(0)
    result(chunks - chunks // 2)
    rows_out[0] = acc[...].astype(bf16)
    send_home(0, rows_out.at[0])
    proj_stream.start()
    out_piece(1)
    grad_normed(5)
    out_piece(2)
    grad_normed(len(proj_cuts) - 5)
    out_piece(3)
    norm1()
    send_home(1, rows_out.at[1])
    pack_small()
    value = small_v[...]
    for k, (at, cols) in enumerate(proj_cuts[6:9] + proj_cuts[0:6] + proj_cuts[9:]):
        if 1 <= k <= 4:
            small.begin(place, k - 1, value)
        proj_piece(at, cols)
        if 1 <= k <= 4:
            value = small.end(k - 1)
        if k == 5:
            arrive(0, o_rows)
        if k == 7:
            arrive(1, o_grad)
    for _ in range(7):
        tick()
    o_small[...] = value
    for c in stores:
        c.wait()


def backward_call(n_shard, reps, offs, lens, rate, bias, gathered, saved):
    anywhere = pl.BlockSpec(memory_space=pl.ANY)
    held = pl.BlockSpec(memory_space=pltpu.VMEM)
    words = pl.BlockSpec(memory_space=pltpu.SMEM)
    rows, width = saved["xin"].shape
    ff = gathered[2].shape[1]
    sd = jax.ShapeDtypeStruct
    wide = QKV + VALS + LANES
    sems = pltpu.SemaphoreType.DMA
    rings = (Ring(n_shard, width // n_shard, WIDE), Ring(n_shard, ff // n_shard, NARROW))
    small = Small(n_shard, reps, 16, width)
    outs = [
        sd((rows, width), bf16), sd((rows, width), bf16), sd((width // n_shard, 2 * ff), bf16),
        sd((ff // n_shard, width), bf16), sd((VALS // n_shard, width), bf16), sd((width // n_shard, wide), bf16),
        sd((16, width), f32),
    ]
    vmem = pltpu.VMEM
    scratch = [vmem(saved[name].shape, saved[name].dtype) for name in BACK_KEPT]
    scratch += rings[0].scratch() + rings[1].scratch() + small.scratch()
    scratch += [
        sems((len(BACK_KEPT),)), vmem((2, width, WIDE), bf16), sems((2, 2)), vmem((2, FTILE, width), bf16), sems((2, 1)),
        vmem((rows, width), f32), vmem((rows, width), f32), vmem((rows, width), bf16), vmem((rows, VALS), f32),
        vmem((rows, LANES), f32), vmem((LANES, rows), f32), vmem((rows, wide), bf16), vmem((4, QKV), f32),
        vmem((1, DVH), f32), vmem((1, LANES), f32), vmem((1, LANES), f32), vmem((16, width), f32),
        vmem((2, rows, width), bf16), vmem((2, rows, width), bf16), sems((2, n_shard)), sems((2, n_shard)),
        vmem((2, rows, width), bf16), sems((2,)),
    ]
    return pl.pallas_call(
        functools.partial(backward_kernel, n_shard, reps, rings, small),
        in_specs=[words, words, held, held] + [anywhere] * (5 + len(BACK_KEPT)),
        out_specs=[anywhere] * 6 + [held],
        out_shape=outs,
        scratch_shapes=scratch,
        compiler_params=pltpu.CompilerParams(collective_id=0, has_side_effects=True, vmem_limit_bytes=63 << 20),
    )(offs, lens, rate, bias, *gathered, *[saved[name] for name in BACK_KEPT])


def local(
    reps, tokens, cotangent, deal, offsets, lengths, norm1_gain, q_weight, k_weight, v_weight, conv_weight,
    beta_weight, decay_weight, log_rate, step_bias, out_gate_weight, out_norm_gain, out_weight, norm2_gain,
    ffn_gate, ffn_up, ffn_down,
):
    rows, width = tokens.shape
    n = lax.axis_size("shard")
    s = lax.axis_index("shard")
    pad = LANES - 2 * HEADS
    bd_weight = jnp.concatenate([beta_weight, decay_weight, jnp.zeros((beta_weight.shape[0], pad), bf16)], axis=1)
    lanes = lambda a: jnp.pad(a, (HEADS, LANES - 2 * HEADS))[None, :]
    rate, bias = lanes(log_rate), lanes(step_bias)

    def spread(vector):
        size = vector.shape[0]
        wide = lax.dynamic_update_slice(jnp.zeros((size * n,), bf16), vector, (s * size,))
        return jnp.pad(wide, (0, width - size * n))[None]

    taps = lax.dynamic_update_slice(jnp.zeros((4, QKV), bf16), conv_weight, (0, s * conv_weight.shape[1]))
    small_in = jnp.concatenate(
        [taps.reshape(-1, width), spread(norm1_gain), spread(norm2_gain), spread(out_norm_gain), jnp.zeros((1, width), bf16)]
    )
    weights = (q_weight, k_weight, v_weight, out_gate_weight, bd_weight, out_weight, ffn_gate, ffn_up, ffn_down)
    deals = jnp.broadcast_to(deal[None, :], (8, rows))
    gathered, saved = forward_call(
        n, reps, offsets[0], lengths[0], tokens, cotangent, deals, small_in, rate, bias, weights
    )
    home_rows, home_grad, s_ffn, s_down, s_out, s_proj, small = backward_call(
        n, reps, offsets[0], lengths[0], rate, bias, gathered, saved
    )

    def part(a, dim=0):
        size = a.shape[dim] // n
        return lax.dynamic_slice_in_dim(a, s * size, size, dim)

    f = lambda a: a.astype(f32)
    ff = ffn_gate.shape[1]
    at = QKV + VALS
    return (
        home_rows, home_grad, part(small[12]), f(s_proj[:, :KEYS]), f(s_proj[:, KEYS : 2 * KEYS]),
        f(s_proj[:, 2 * KEYS : QKV]), part(small[:12].reshape(4, QKV), 1), f(s_proj[:, at : at + HEADS]),
        f(s_proj[:, at + HEADS : at + 2 * HEADS]), small[14, DVH + HEADS : DVH + 2 * HEADS],
        small[14, DVH + LANES + HEADS : DVH + LANES + 2 * HEADS], f(s_proj[:, QKV:at]), part(small[14, :DVH]),
        f(s_out), part(small[13]), f(s_ffn[:, :ff]), f(s_ffn[:, ff:]), f(s_down),
    )


def solution(mesh):
    rows2, shard0 = P(("rep", "shard"), None), P("shard", None)
    vec = P("shard")
    in_specs = (
        rows2, rows2, P(("rep", "shard")), rows2, rows2, vec, shard0, shard0, shard0, P(None, "shard"),
        shard0, shard0, P(), P(), shard0, vec, shard0, vec, shard0, shard0, shard0,
    )
    out_specs = (
        rows2, rows2, vec, shard0, shard0, shard0, P(None, "shard"), shard0, shard0, P(), P(), shard0,
        vec, shard0, vec, shard0, shard0, shard0,
    )
    body = functools.partial(local, mesh.shape["rep"])
    return jax.shard_map(body, mesh=mesh, in_specs=in_specs, out_specs=out_specs, check_vma=False)
```

```python
import functools
import jax
import jax.numpy as jnp
from jax import lax
from jax.experimental import pallas as pl
from jax.experimental.pallas import tpu as pltpu
from jax.sharding import PartitionSpec as P

f32 = jnp.float32
bf16 = jnp.bfloat16
HEADS = 6
DK = 128
DVH = 256
KEYS = 768
VALS = 1536
QKV = 2 * KEYS + VALS
LANES = 128


def two_parts(a):
    hi = a.astype(bf16)
    return hi, (a - hi.astype(f32)).astype(bf16)


def dot(a, b, ca=1, cb=0):
    return lax.dot_general(a, b, (((ca,), (cb,)), ((), ())), preferred_element_type=f32)


def dot3(a, b, ca=1, cb=0):
    ah, al = a
    bh, bl = b
    return dot(ah, bh, ca, cb) + (dot(ah, bl, ca, cb) + dot(al, bh, ca, cb))


def tri_dot(tri, cols):
    hi = cols.astype(bf16)
    rest = cols - hi.astype(f32)
    mid = rest.astype(bf16)
    lo = (rest - mid.astype(f32)).astype(bf16)
    return dot(tri, hi) + (dot(tri, mid) + dot(tri, lo))


def sigm(a):
    return 1.0 / (1.0 + jnp.exp(-a))


def softplus(a):
    return jnp.maximum(a, 0.0) + jnp.log1p(jnp.exp(-jnp.abs(a)))


def layout_cols(offs, lens, n, shape, dim):
    row = lax.broadcasted_iota(jnp.int32, shape, dim)
    begin = jnp.zeros_like(row)
    extent = jnp.zeros_like(row)
    for i in range(len(offs)):
        inside = row >= offs[i]
        begin = jnp.where(inside, offs[i], begin)
        extent = jnp.where(inside, lens[i], extent)
    return begin, row - begin, (row - begin) < extent


def conv_chunk(x, taps, pos, cols):
    total = taps[0:1, cols] * x
    for t in range(1, 4):
        total = total + taps[t : t + 1, cols] * jnp.where(pos >= t, pltpu.roll(x, t, 0), 0.0)
    return total


def lane_pick(a, lane, index):
    return jnp.sum(jnp.where(lane == index, a, 0.0), axis=1, keepdims=True)


def pair_masks(n, begin_c, begin_r):
    i = lax.broadcasted_iota(jnp.int32, (n, n), 0)
    j = lax.broadcasted_iota(jnp.int32, (n, n), 1)
    same = begin_c == begin_r
    return i, j, (i >= j) & same


def mixer_forward(n, offs, lens, lin, taps, rate, bias, gain, act, cum, cum_t, tinv, fresh, heads_out, mixed):
    begin_c, pos, live = layout_cols(offs, lens, n, (n, 1), 0)
    begin_r, _, _ = layout_cols(offs, lens, n, (1, n), 1)
    live_f = live.astype(f32)
    width = 384

    def conv_step(step, carry):
        cols = pl.ds(pl.multiple_of(step * width, width), width)
        pre = conv_chunk(lin[:, cols], taps, pos, cols)
        act[:, cols] = pre * sigm(pre)
        return carry

    lane = lax.broadcasted_iota(jnp.int32, (n, LANES), 1)
    bd = lin[:, QKV + VALS : QKV + VALS + LANES]
    beta = sigm(bd) * live_f
    decay = -jnp.exp(rate[...]) * softplus(bd + bias[...]) * live_f
    i, j, low = pair_masks(n, begin_c, begin_r)
    eye = (i == j).astype(f32)

    def convolve():
        lax.fori_loop(0, QKV // width, conv_step, 0)
        total = tri_dot((i >= j).astype(bf16), decay)
        cum[...] = total
        cum_t[...] = total.T

    def one_head(h):
        kcols = pl.ds(pl.multiple_of(h * DK, DK), DK)
        ka = act[:, pl.ds(pl.multiple_of(KEYS + h * DK, DK), DK)]
        qa = act[:, kcols]
        vcols = pl.ds(pl.multiple_of(h * DVH, DVH), DVH)
        v = act[:, pl.ds(pl.multiple_of(2 * KEYS + h * DVH, DVH), DVH)]
        q = qa * (lax.rsqrt(jnp.sum(qa * qa, axis=1, keepdims=True) + 1e-6) * DK**-0.5)
        k = ka * lax.rsqrt(jnp.sum(ka * ka, axis=1, keepdims=True) + 1e-6)
        beta_c = lane_pick(beta, lane, h)
        cum_c = lane_pick(cum[...], lane, HEADS + h)
        cum_r = cum_t[pl.ds(HEADS + h, 1), :]
        kk, qq = two_parts(k), two_parts(q)
        dec = jnp.where(low, jnp.exp(jnp.where(low, cum_c - cum_r, 0.0)), 0.0)
        system = jnp.where(i > j, beta_c * dot3(kk, kk, 1, 1) * dec, 0.0)
        inv = eye - jnp.where((i // 2) == (j // 2), system, 0.0)
        size = 2
        while size < n:
            off = jnp.where(((i // (2 * size)) == (j // (2 * size))) & ((i // size) != (j // size)), system, 0.0)
            parts = two_parts(inv)
            inv = inv - dot3(two_parts(dot3(parts, two_parts(off))), parts)
            size *= 2
        tinv[h] = inv
        u = dot3(two_parts(inv), two_parts(beta_c * v))
        fresh[:, vcols] = u
        o = dot3(two_parts(dot3(qq, kk, 1, 1) * dec), two_parts(u)) * live_f
        heads_out[:, vcols] = o
        gate = lin[:, pl.ds(pl.multiple_of(QKV + h * DVH, DVH), DVH)]
        scaled = o * lax.rsqrt(jnp.mean(o * o, axis=1, keepdims=True) + 1e-5)
        mixed[:, vcols] = (scaled * gain[...] * (gate * sigm(gate))).astype(bf16)

    return convolve, [functools.partial(one_head, h) for h in range(HEADS)]


def mixer_backward(
    n, offs, lens, lin, taps, rate, bias, gain, act, cum, cum_t, tinv, fresh, heads_out, grad_mixed,
    dact, dcols, drows, lin_grad, tap_grad, gain_grad, rate_grad, bias_grad,
):
    begin_c, pos, live = layout_cols(offs, lens, n, (n, 1), 0)
    begin_r, _, _ = layout_cols(offs, lens, n, (1, n), 1)
    live_f = live.astype(f32)
    lane = lax.broadcasted_iota(jnp.int32, (n, LANES), 1)
    bd = lin[:, QKV + VALS : QKV + VALS + LANES]
    sig_b = sigm(bd)
    beta = sig_b * live_f
    i, j, low = pair_masks(n, begin_c, begin_r)
    strict = low & (i > j)

    def clear():
        gain_grad[...] = jnp.zeros_like(gain_grad)
        dcols[...] = jnp.zeros_like(dcols)
        drows[...] = jnp.zeros_like(drows)

    def one_head(h):
        kcols = pl.ds(pl.multiple_of(h * DK, DK), DK)
        kcols2 = pl.ds(pl.multiple_of(KEYS + h * DK, DK), DK)
        vcols = pl.ds(pl.multiple_of(h * DVH, DVH), DVH)
        vcols2 = pl.ds(pl.multiple_of(2 * KEYS + h * DVH, DVH), DVH)
        gcols = pl.ds(pl.multiple_of(QKV + h * DVH, DVH), DVH)
        ka = act[:, kcols2]
        qa = act[:, kcols]
        v = act[:, vcols2]
        o = heads_out[:, vcols]
        gate = lin[:, gcols]
        dm = grad_mixed[:, vcols]
        ro = lax.rsqrt(jnp.mean(o * o, axis=1, keepdims=True) + 1e-5)
        scaled = o * ro
        sg = sigm(gate)
        si = gate * sg
        gain_grad[...] += jnp.sum(dm * scaled * si, axis=0, keepdims=True)
        lin_grad[:, gcols] = (dm * scaled * gain[...] * (sg + si * (1.0 - sg))).astype(bf16)
        ds = dm * gain[...] * si
        d_o = two_parts(ro * (ds - scaled * jnp.mean(ds * scaled, axis=1, keepdims=True)) * live_f)
        rq = lax.rsqrt(jnp.sum(qa * qa, axis=1, keepdims=True) + 1e-6)
        rk = lax.rsqrt(jnp.sum(ka * ka, axis=1, keepdims=True) + 1e-6)
        qhat = qa * rq
        k = ka * rk
        kk, qq = two_parts(k), two_parts(qhat * DK**-0.5)
        beta_c = lane_pick(beta, lane, h)
        cum_c = lane_pick(cum[...], lane, HEADS + h)
        cum_r = cum_t[pl.ds(HEADS + h, 1), :]
        dec = jnp.where(low, jnp.exp(jnp.where(low, cum_c - cum_r, 0.0)), 0.0)
        gram = dot3(kk, kk, 1, 1)
        qk = dot3(qq, kk, 1, 1)
        uu = two_parts(fresh[:, vcols])
        du = dot3(two_parts(qk * dec), d_o, 0, 0)
        dp = dot3(d_o, uu, 1, 1) * dec
        db = dot3(two_parts(tinv[h]), two_parts(du), 0, 0)
        da = jnp.where(strict, -dot3(two_parts(db), uu, 1, 1), 0.0) * dec
        x = da * gram
        dbeta = jnp.sum(x, axis=1, keepdims=True) + jnp.sum(db * v, axis=1, keepdims=True)
        e = dp * qk + x * beta_c
        dcols[...] += jnp.where(lane == h, dbeta, 0.0) + jnp.where(
            lane == HEADS + h, jnp.sum(e, axis=1, keepdims=True), 0.0
        )
        drows[pl.ds(HEADS + h, 1), :] = jnp.sum(e, axis=0, keepdims=True)
        dact[:, vcols2] = beta_c * db
        dg = two_parts(da * beta_c)
        dpp = two_parts(dp)
        dq = dot3(dpp, kk)
        dk = dot3(dpp, qq, 0, 0) + dot3(dg, kk) + dot3(dg, kk, 0, 0)
        dact[:, kcols] = (rq * DK**-0.5) * (dq - qhat * jnp.sum(dq * qhat, axis=1, keepdims=True))
        dact[:, kcols2] = rk * (dk - k * jnp.sum(dk * k, axis=1, keepdims=True))

    def rates():
        dcum = jnp.where((lane >= HEADS) & (lane < 2 * HEADS), dcols[...] - drows[...].T, 0.0)
        ddecay = tri_dot((i <= j).astype(bf16), dcum)
        z = bd + bias[...]
        speed = -jnp.exp(rate[...]) * live_f
        dz = ddecay * speed * sigm(z)
        rate_grad[...] = jnp.sum(ddecay * speed * softplus(z), axis=0, keepdims=True)
        bias_grad[...] = jnp.sum(dz, axis=0, keepdims=True)
        dbeta_lin = dcols[...] * live_f * sig_b * (1.0 - sig_b)
        both = jnp.where(lane < HEADS, dbeta_lin, jnp.where(lane < 2 * HEADS, dz, 0.0))
        lin_grad[:, QKV + VALS : QKV + VALS + LANES] = both.astype(bf16)

    width = 384

    def conv_step(step, carry):
        cols = pl.ds(pl.multiple_of(step * width, width), width)
        x = lin[:, cols]
        pre = conv_chunk(x, taps, pos, cols)
        sg = sigm(pre)
        dc = dact[:, cols] * (sg + pre * sg * (1.0 - sg))
        dx = taps[0:1, cols] * dc
        tap_grad[0:1, cols] = jnp.sum(dc * x, axis=0, keepdims=True)
        for t in range(1, 4):
            masked = jnp.where(pos >= t, dc, 0.0)
            dx = dx + taps[t : t + 1, cols] * pltpu.roll(masked, n - t, 0)
            tap_grad[t : t + 1, cols] = jnp.sum(masked * pltpu.roll(x, t, 0), axis=0, keepdims=True)
        lin_grad[:, cols] = dx.astype(bf16)
        return carry

    def convolve(first, last):
        return lambda: lax.fori_loop(first, last, conv_step, 0)

    heads = [functools.partial(one_head, h) for h in range(HEADS)]
    total = QKV // width
    return clear, heads, rates, [convolve(0, total // 2), convolve(total // 2, total)]


MESH = pl.DeviceIdType.MESH


class Place:
    def __init__(self, n_shard, n_rep):
        self.n, self.reps = n_shard, n_rep
        self.ys = n_shard // 4
        self.r = lax.axis_index("rep")
        self.s = lax.axis_index("shard")
        self.c = self.s % 2
        self.x = (self.s // 2) % 2
        self.y = self.s // 4
        half = n_rep // 2
        low = self.r < half
        self.depth = jnp.where(low, self.r, n_rep - 1 - self.r)
        self.inner = jnp.where(low, self.r + 1, self.r - 1)
        self.outer = jnp.where(low, self.r - 1, self.r + 1)
        self.middle = self.depth == half - 1
        self.deep = self.depth > 0

    def shard_id(self, y, x, c):
        return (self.r, (y * 2 + x) * 2 + c)

    def core_peer(self):
        return self.shard_id(self.y, self.x, 1 - self.c)

    def x_peer(self):
        return self.shard_id(self.y, 1 - self.x, self.c)

    def y_of(self, step):
        return (self.y + step) % self.ys

    def y_peer(self, step):
        return self.shard_id(self.y_of(step), self.x, self.c)


def remote(src, dst, send, recv, device):
    return pltpu.make_async_remote_copy(
        src_ref=src, dst_ref=dst, send_sem=send, recv_sem=recv, device_id=device, device_id_type=MESH
    )


def greet(place, with_rep):
    barrier = pltpu.get_barrier_semaphore()
    n = place.n
    for step in range(1, n):
        pl.semaphore_signal(
            barrier, inc=1, device_id=(place.r, (place.s + step) % n), device_id_type=MESH
        )
    if not with_rep:
        pl.semaphore_wait(barrier, n - 1)
        return
    for step in range(1, place.reps):
        pl.semaphore_signal(
            barrier, inc=1, device_id=((place.r + step) % place.reps, place.s), device_id_type=MESH
        )
    pl.semaphore_wait(barrier, n - 1 + place.reps - 1)


def add_into(dst, idx, *others):
    total = dst[idx].astype(f32)
    for ref, at in others:
        total = total + ref[at].astype(f32)
    dst[idx] = total.astype(dst.dtype)


RING = 4


def halved(rows):
    return (rows // 2) // 16 * 16


class Ring:
    def __init__(self, n, rows, cols):
        self.n, self.rows, self.cols = n, rows, cols
        self.ys = n // 4
        self.count = 0

    def scratch(self):
        k, ys, cols = RING, self.ys, self.cols
        sems = pltpu.SemaphoreType.DMA
        per = 3 + 2 * (ys - 1)
        half = self.rows - halved(self.rows)
        return [
            pltpu.VMEM((k, ys, 2, 2, self.rows, cols), bf16),
            pltpu.VMEM((k, ys, 2, self.rows, cols), bf16),
            pltpu.VMEM((k, ys, half, cols), bf16),
            pltpu.VMEM((k, ys - 1, 2, half, cols), bf16),
            pltpu.VMEM((k, ys - 1, half, cols), bf16),
            pltpu.VMEM((k, half, cols), bf16),
            pltpu.VMEM((4, k, self.rows, cols), bf16),
            sems((k, per)),
            sems((k, per)),
            sems((k, 7)),
        ]

    def bind(self, refs):
        (self.own, self.r0, self.r1a, self.r1b, self.r2a, self.r2b, self.z, self.send, self.recv, self.zsem) = refs


class Piece:
    def __init__(self, ring, place, rows, cols, out, out_cols):
        self.ring, self.p, self.rows = ring, place, rows
        self.slot = ring.count % RING
        ring.count += 1
        self.w = pl.ds(0, cols)
        self.ra = halved(rows)
        self.rb = rows - self.ra
        self.all_rows = pl.ds(0, rows)
        self.out = out.at[:, pl.ds(out_cols, cols)]

    def own_view(self):
        return self.ring.own.at[self.slot, :, :, :, self.all_rows, self.w]

    def store_rows(self, value):
        ring = self.ring
        shaped = value.reshape(ring.ys, 2, 2, rinself.rows, value.shape[-1])
        ring.own[self.slot, :, :, :, self.all_rows, self.w] = shaped

    def send_core(self):
        g, p, k = self.ring, self.p, self.slot
        self.c0 = remote(
            g.own.at[k, :, :, 1 - p.c, self.all_rows, self.w], g.r0.at[k, :, :, self.all_rows, self.w],
            g.send.at[k, 0], g.recv.at[k, 0], p.core_peer(),
        )
        self.c0.start()

    def after_core(self):
        g, p, k, w = self.ring, self.p, self.slot, self.w
        rows = self.all_rows
        self.c0.wait()

        def step(q, carry):
            yy, xx = q // 2, q % 2
            add_into(g.own, (k, yy, xx, p.c, rows, w), (g.r0, (k, yy, xx, rows, w)))
            return carry

        lax.fori_loop(0, g.ys * 2, step, 0)
        top, low = pl.ds(0, self.ra), pl.ds(self.ra, self.rb)
        first, second = pl.ds(0, self.ra), pl.ds(0, self.rb)
        self.c1 = [
            remote(
                g.own.at[k, :, 1 - p.x, p.c, top, w], g.r1a.at[k, :, first, w],
                g.send.at[k, 1], g.recv.at[k, 1], p.x_peer(),
            )
        ]
        for d in range(1, g.ys):
            self.c1.append(
                remote(
                    g.own.at[k, p.y_of(d), :, p.c, low, w], g.r1b.at[k, d - 1, :, second, w],
                    g.send.at[k, 1 + d], g.recv.at[k, 1 + d], p.y_peer(d),
                )
            )
        for c in self.c1:
            c.start()

    def after_first(self):
        g, p, k, w = self.ring, self.p, self.slot, self.w
        top, low = pl.ds(0, self.ra), pl.ds(self.ra, self.rb)
        first, second = pl.ds(0, self.ra), pl.ds(0, self.rb)
        for c in self.c1:
            c.wait()
        for yy in range(g.ys):
            add_into(g.own, (k, yy, p.x, p.c, top, w), (g.r1a, (k, yy, first, w)))
        for xx in range(2):
            add_into(
                g.own, (k, p.y, xx, p.c, low, w),
                *[(g.r1b, (k, d, xx, second, w)) for d in range(g.ys - 1)],
            )
        self.c2 = [
            remote(
                g.own.at[k, p.y, 1 - p.x, p.c, low, w], g.r2b.at[k, second, w],
                g.send.at[k, 1 + g.ys], g.recv.at[k, 1 + g.ys], p.x_peer(),
            )
        ]
        for d in range(1, g.ys):
            self.c2.append(
                remote(
                    g.own.at[k, p.y_of(d), p.x, p.c, top, w], g.r2a.at[k, d - 1, first, w],
                    g.send.at[k, 1 + g.ys + d], g.recv.at[k, 1 + g.ys + d], p.y_peer(d),
                )
            )
        for c in self.c2:
            c.start()

    def after_second(self):
        g, p, k, w = self.ring, self.p, self.slot, self.w
        for c in self.c2:
            c.wait()
        total = g.own[k, p.y, p.x, p.c, 0 : self.ra, w].astype(f32)
        for d in range(g.ys - 1):
            total = total + g.r2a[k, d, 0 : self.ra, w].astype(f32)
        g.z[0, k, 0 : self.ra, w] = total.astype(bf16)
        total = g.own[k, p.y, p.x, p.c, self.ra : self.rows, w].astype(f32) + g.r2b[k, 0 : self.rb, w].astype(f32)
        g.z[0, k, self.ra : self.rows, w] = total.astype(bf16)
        z = lambda i: g.z.at[i, k, self.all_rows, w]
        target = lambda r: (r, p.s)
        sem = g.zsem
        self.up = remote(z(0), z(1), sem.at[k, 0], sem.at[k, 1], target(p.inner))
        self.meet = remote(z(0), z(2), sem.at[k, 2], sem.at[k, 3], target(p.inner))
        self.down = remote(z(3), z(2), sem.at[k, 4], sem.at[k, 3], target(p.outer))
        self.home = pltpu.make_async_copy(z(3), self.out, sem.at[k, 6])

        @pl.when(p.depth == 0)
        def _():
            self.send_inward()

    def send_inward(self):
        p = self.p

        @pl.when(p.middle)
        def _():
            self.meet.start()

        @pl.when(jnp.logical_not(p.middle))
        def _():
            self.up.start()

    def after_up(self):
        g, p, k, w = self.ring, self.p, self.slot, self.w

        @pl.when(p.deep)
        def _():
            self.up.wait_recv()
            add_into(g.z, (0, k, self.all_rows, w), (g.z, (1, k, self.all_rows, w)))
            self.send_inward()

    def finish(self, middle):
        g, p, k, w = self.ring, self.p, self.slot, self.w
        rows = self.all_rows

        @pl.when(p.middle if middle else jnp.logical_not(p.middle))
        def _():
            self.meet.wait_recv()
            if middle:
                both = g.z[0, k, rows, w].astype(f32) + g.z[2, k, rows, w].astype(f32)
                g.z[3, k, rows, w] = both.astype(bf16)
            else:
                g.z[3, k, rows, w] = g.z[2, k, rows, w]

            @pl.when(p.deep)
            def _():
                self.down.start()

            self.home.start()

    def close(self):
        p = self.p

        @pl.when(p.middle)
        def _():
            self.meet.wait_send()

        @pl.when(jnp.logical_not(p.middle))
        def _():
            self.up.wait_send()

        @pl.when(p.deep)
        def _():
            self.down.wait_send()

        self.home.wait()


def pump(pieces, index):
    stages = [
        (1, lambda q: q.after_core()),
        (7, lambda q: q.close()),
        (6, lambda q: q.finish(False)),
        (5, lambda q: q.finish(True)),
        (4, lambda q: q.after_up()),
        (3, lambda q: q.after_second()),
        (2, lambda q: q.after_first()),
    ]
    for lag, act in stages:
        if 0 <= index - lag < len(pieces):
            act(pieces[index - lag])


class Small:
    def __init__(self, n, reps, rows, cols):
        self.n, self.ys, self.reps = n, n // 4, reps
        self.sizes = (2, 2, self.ys, reps)
        self.rows, self.cols = rows, cols

    def scratch(self):
        total = sum(self.sizes)
        return [
            pltpu.VMEM((total, self.rows, self.cols), f32),
            pltpu.SemaphoreType.DMA((total,)),
            pltpu.SemaphoreType.DMA((total,)),
        ]

    def bind(self, refs):
        self.buf, self.send, self.recv = refs

    def begin(self, place, axis, value):
        base = sum(self.sizes[:axis])
        size = self.sizes[axis]
        p = place
        mine = (p.c, p.x, p.y, p.r)[axis]
        slot = self.buf.at[base + mine]
        slot[...] = value
        self.copies = []
        for d in range(1, size):
            at = (mine + d) % size
            device = (
                p.shard_id(p.y, p.x, at), p.shard_id(p.y, at, p.c), p.shard_id(at, p.x, p.c), (at, p.s),
            )[axis]
            self.copies.append(remote(slot, slot, self.send.at[base + d], self.recv.at[base + d], device))
        for c in self.copies:
            c.start()

    def end(self, axis):
        base = sum(self.sizes[:axis])
        for c in self.copies:
            c.wait()
        total = self.buf[base]
        for d in range(1, self.sizes[axis]):
            total = total + self.buf[base + d]
        return total


class Flow:
    @staticmethod
    def count(ys, pair):
        return 5 + 12 * (ys - 1) if pair else 3 + 6 * (ys - 1)

    def __init__(self, place, src, src_at, cols, dst, dst_at, pair, send, recv, base, mine):
        self.p, self.rows, self.pair = place, src.shape[0], pair
        self.src_ref, self.src_at, self.dst, self.dst_at, self.width = src, src_at, dst, dst_at, cols
        self.send, self.recv, self.base, self.used = send, recv, base, 0
        self.ra = halved(self.rows)
        self.part = (place.r % 2) if pair else None
        whole = self.src_ref.at[:, pl.ds(src_at, cols)]
        self.mine = pltpu.make_async_copy(whole, self.region(place.y, place.x, place.c), mine)
        self.whole = whole
        self.all = []

    def columns(self, at, part):
        if part is None:
            return pl.ds(at, self.width)
        half = self.width // 2
        return pl.ds(pl.multiple_of(at + part * half, LANES), half)

    def region(self, y, x, c, half=None, part=None):
        start = ((y * 2 + x) * 2 + c) * self.rows
        size = self.rows
        if half == 0:
            size = self.ra
        elif half == 1:
            start, size = start + self.ra, self.rows - self.ra
        return self.dst.at[pl.ds(pl.multiple_of(start, 16), size), self.columns(self.dst_at, part)]

    def copy(self, dst, device, src=None):
        at = self.base + self.used
        self.used += 1
        c = remote(dst if src is None else src, dst, self.send.at[at], self.recv.at[at], device)
        c.start()
        self.all.append(c)
        return c

    def begin(self):
        p = self.p
        own = self.region(p.y, p.x, p.c, None, self.part)
        src = self.src_ref.at[:, self.columns(self.src_at, self.part)]
        self.mine.start()
        self.from_x = self.copy(own, p.x_peer(), src)
        self.from_y = [self.copy(own, p.y_peer(d), src) for d in range(1, p.ys)]
        self.from_core = [self.copy(self.region(p.y, p.x, p.c), p.core_peer(), self.whole)]
        self.from_z, self.z_regions = [], []

    def share(self, *where):
        p = self.p
        if self.pair:
            self.from_z.append(self.copy(self.region(*where, self.part), (p.r + 1 - 2 * (p.r % 2), p.s)))
            self.z_regions.append(where)
        self.from_core.append(self.copy(self.region(*where, self.part), p.core_peer()))

    def forward(self):
        p = self.p
        steps = range(1, p.ys)
        self.from_x.wait_recv()
        self.diag = [self.copy(self.region(p.y, 1 - p.x, p.c, 0, self.part), p.y_peer(d)) for d in steps]
        self.share(p.y, 1 - p.x, p.c, None)
        for d in steps:
            self.from_y[d - 1].wait_recv()
            back = p.y_of(p.ys - d)
            self.diag.append(self.copy(self.region(back, p.x, p.c, 1, self.part), p.x_peer()))
            self.share(back, p.x, p.c, None)

    def relay(self):
        p = self.p
        for i, c in enumerate(self.diag):
            c.wait_recv()
            half, d = divmod(i, p.ys - 1)
            self.share(p.y_of(p.ys - d - 1), 1 - p.x, p.c, half)

    def swap(self):
        for c, where in zip(self.from_z, self.z_regions):
            c.wait_recv()
            self.from_core.append(self.copy(self.region(*where, 1 - self.part), self.p.core_peer()))

    def done(self):
        for c in self.from_core:
            c.wait_recv()
        self.mine.wait()

    def close(self):
        for c in self.all:
            c.wait_send()


FF_SPLIT = 1536
FTILE = 256


def one_hot_rows(values, count):
    return lax.broadcasted_iota(jnp.int32, (count, values.shape[1]), 0) == values


class Store:
    def __init__(self, sem):
        self.sem, self.all = sem, []

    def put(self, src, dst):
        c = pltpu.make_async_copy(src, dst, self.sem.at[len(self.all)])
        c.start()
        self.all.append(c)

    def wait(self):
        for c in self.all:
            c.wait()


FORWARD_SAVED = (
    ("xin", lambda n, d, f: ((n, d), bf16)),
    ("dy", lambda n, d, f: ((n, d), bf16)),
    ("normed_t", lambda n, d, f: ((d, n), bf16)),
    ("lin", lambda n, d, f: ((n, QKV + VALS + LANES), f32)),
    ("act", lambda n, d, f: ((n, QKV), f32)),
    ("cum", lambda n, d, f: ((n, LANES), f32)),
    ("cum_t", lambda n, d, f: ((LANES, n), f32)),
    ("tinv", lambda n, d, f: ((HEADS, n, n), f32)),
    ("fresh", lambda n, d, f: ((n, VALS), f32)),
    ("heads", lambda n, d, f: ((n, VALS), f32)),
    ("mixed_t", lambda n, d, f: ((VALS, n), bf16)),
    ("middle", lambda n, d, f: ((n, d), f32)),
    ("normed_mid_t", lambda n, d, f: ((d, n), bf16)),
    ("hidden", lambda n, d, f: ((n, f), bf16)),
    ("hidden_t", lambda n, d, f: ((f, n), bf16)),
    ("grads_gu", lambda n, d, f: ((n, 2 * f), bf16)),
    ("pick", lambda n, d, f: ((n, n), bf16)),
    ("place", lambda n, d, f: ((n, n), bf16)),
    ("params", lambda n, d, f: ((16, d), f32)),
    ("taps", lambda n, d, f: ((4, QKV), f32)),
)


def transposed(a):
    return a.T.astype(bf16)


def forward_kernel(n_shard, reps, *refs):
    take = iter(refs)
    get = lambda k: [next(take) for _ in range(k)]
    offs, lens, tokens, cot, deal, small_in, rate, bias = get(8)
    wq, wk, wv, wt, wb, wo, wg, wu, wd = get(9)
    gp, go, gg, gu, gd = get(5)
    outs = dict(zip([name for name, _ in FORWARD_SAVED], get(len(FORWARD_SAVED))))
    kept = dict(zip([name for name, _ in FORWARD_SAVED], get(len(FORWARD_SAVED))))
    (dealt, dsend, drecv, smalls, ssend, srecv, sent, come, tsend, trecv, wbuf, wobuf, wdbuf, load_sem, fsend, frecv,
     mine_sem, out_sem, normed, mixed, normed_mid) = get(21)
    shards, shard_sem = get(9), get(1)[0]
    own_loads = []
    for k, (w, v) in enumerate(zip((wq, wk, wv, wt, wb, wo, wd, wg, wu), shards)):
        own_loads.append(pltpu.make_async_copy(w, v, shard_sem.at[k]))
        own_loads[-1].start()
    wq, wk, wv, wt, wb, wo, wd, wg, wu = shards
    rows, width = tokens.shape
    per = rows // n_shard
    place = Place(n_shard, reps)
    p = place
    greet(place, True)
    offsets = [offs[i] for i in range(offs.shape[0])]
    lengths = [lens[i] for i in range(lens.shape[0])]
    store = Store(out_sem)

    dealt[p.s] = deal[...]
    smalls[p.s] = small_in[...]
    first = []
    for d in range(1, n_shard):
        to = (p.r, (p.s + d) % n_shard)
        first.append(remote(dealt.at[p.s], dealt.at[p.s], dsend.at[d], drecv.at[d], to))
        first[-1].start()
    for d in range(1, n_shard):
        to = (p.r, (p.s + d) % n_shard)
        first.append(remote(smalls.at[p.s], smalls.at[p.s], ssend.at[d], srecv.at[d], to))
        first[-1].start()

    made = []

    def flow(src, at, cols, dst, dst_at, pair):
        k = len(made)
        base = sum(Flow.count(p.ys, f.pair) for f in made)
        made.append(Flow(place, src, at, cols, dst, dst_at, pair, fsend, frecv, base, mine_sem.at[k]))
        return made[-1]

    ff = wg.shape[1]
    stages = [
        [flow(wq, 0, KEYS, gp, 0, True), flow(wk, 0, KEYS, gp, KEYS, True), flow(wb, 0, LANES, gp, QKV + VALS, False)],
        [flow(wv, 0, VALS, gp, 2 * KEYS, True)],
        [flow(wt, 0, VALS, gp, QKV, False)],
        [flow(wo, 0, width, go, 0, True)],
        [flow(wd, 0, width // 2, gd, 0, True)],
        [flow(wd, width // 2, width // 2, gd, width // 2, False)],
        [flow(wg, 0, FF_SPLIT, gg, 0, True)],
        [flow(wu, 0, FF_SPLIT, gu, 0, False)],
        [flow(wg, FF_SPLIT, ff - FF_SPLIT, gg, FF_SPLIT, True)],
        [flow(wu, FF_SPLIT, ff - FF_SPLIT, gu, FF_SPLIT, True)],
    ]

    events = []
    for k in range(len(stages) + 5):
        for lag, act in ((0, "begin"), (2, "forward"), (3, "relay"), (4, "swap"), (5, "done")):
            if 0 <= k - lag < len(stages):
                events.append((act, k - lag))
    owned = set()

    def poll(count=1):
        for _ in range(count):
            if events:
                act, k = events.pop(0)
                for f in stages[k]:
                    if act == "begin" and id(f.src_ref) not in owned:
                        owned.add(id(f.src_ref))
                        own_loads[[id(v) for v in shards].index(id(f.src_ref))].wait()
                    getattr(f, act)()

    def until(act, k):
        while (act, k) in events:
            poll()

    until("begin", 1)

    loads = {}

    def load(name, src, dst):
        loads[name] = pltpu.make_async_copy(src, dst, load_sem.at[len(loads)])
        loads[name].start()

    for c in first[: n_shard - 1]:
        c.wait_recv()
    i = lax.broadcasted_iota(jnp.int32, (rows, rows), 0)
    j = lax.broadcasted_iota(jnp.int32, (rows, rows), 1)
    upper = (i <= j).astype(bf16)
    everyone = dealt[:, 0, :]
    to_me = (everyone // rows) == p.s
    rank = dot(to_me.astype(f32).astype(bf16), upper).astype(jnp.int32) - 1
    rank = jnp.where(to_me, rank, -1)
    for b in range(n_shard):
        picked = one_hot_rows(rank[b : b + 1, :], per).astype(f32).astype(bf16)
        which = one_hot_rows(everyone[b : b + 1, :] % rows, rows).astype(f32).astype(bf16)
        kept["pick"][b * per : (b + 1) * per, :] = dot(picked, which, 1, 1).astype(bf16)
    pick = kept["pick"][...]
    exchange = []
    for a, src in enumerate((tokens, cot)):
        for at in range(0, width, 256):
            sent[a, :, at : at + 256] = dot(pick, src[:, at : at + 256]).astype(bf16)
        for d in range(1, n_shard):
            t = (p.s + d) % n_shard
            exchange.append(
                remote(
                    sent.at[a, pl.ds(pl.multiple_of(t * per, 16), per)],
                    come.at[a, pl.ds(pl.multiple_of(p.s * per, 16), per)],
                    tsend.at[a, d], trecv.at[a, d], (p.r, t),
                )
            )
            exchange[-1].start()
        here = pl.ds(pl.multiple_of(p.s * per, 16), per)
        come[a, here, :] = sent[a, here, :]
    mine = deal[0:1, :]
    source = mine // rows
    from_each = one_hot_rows(source, n_shard)
    cum = dot(from_each.astype(f32).astype(bf16), upper)
    slot = jnp.sum(jnp.where(from_each, cum, 0.0), axis=0, keepdims=True).astype(jnp.int32) - 1 + source * per
    kept["place"][...] = one_hot_rows(slot, rows).astype(f32).astype(bf16)
    store.put(kept["pick"], outs["pick"])
    store.put(kept["place"], outs["place"])

    for c in first[n_shard - 1 :]:
        c.wait_recv()
    total = smalls[0].astype(f32)
    for t in range(1, n_shard):
        total = total + smalls[t].astype(f32)
    kept["params"][...] = total
    for t in range(4):
        for g in range(QKV // width):
            row = t * (QKV // width) + g
            kept["taps"][t : t + 1, g * width : (g + 1) * width] = total[row : row + 1, :]
    gain1, gain2 = kept["params"].at[12:13, :], kept["params"].at[13:14, :]
    gain_o = kept["params"].at[14:15, 0:DVH]
    store.put(kept["params"], outs["params"])
    store.put(kept["taps"], outs["taps"])

    for a, name in enumerate(("xin", "dy")):
        for c in exchange[a * (n_shard - 1) : (a + 1) * (n_shard - 1)]:
            c.wait_recv()
        for at in range(0, width, 256):
            kept[name][:, at : at + 256] = dot(kept["place"][...], come[a, :, at : at + 256], 0, 0).astype(bf16)
        store.put(kept[name], outs[name])
    x = kept["xin"][...].astype(f32)
    norm = x * lax.rsqrt(jnp.mean(x * x, axis=1, keepdims=True) + 1e-5) * gain1[...]
    normed[...] = norm.astype(bf16)
    kept["normed_t"][...] = transposed(norm)
    store.put(kept["normed_t"], outs["normed_t"])

    def project(at, cols, tile):
        def step(k, carry):
            here = pl.ds(pl.multiple_of(at + k * tile, 128), tile)
            kept["lin"][:, here] = dot(normed[...], wbuf[:, here])
            return carry

        lax.fori_loop(0, cols // tile, step, 0)

    def fetch(name, at, cols):
        here = pl.ds(at, cols)
        load(name, gp.at[:, here], wbuf.at[:, here])

    until("done", 0)
    fetch("qk", 0, 2 * KEYS)
    fetch("bd", QKV + VALS, LANES)
    until("done", 1)
    fetch("v", 2 * KEYS, VALS)
    loads["qk"].wait()
    loads["bd"].wait()
    project(0, 2 * KEYS, 256)
    project(QKV + VALS, LANES, LANES)
    poll(1)
    loads["v"].wait()
    project(2 * KEYS, VALS, 256)
    until("done", 2)
    fetch("gate", QKV, VALS)
    convolve, heads = mixer_forward(
        rows, offsets, lengths, kept["lin"], kept["taps"], rate, bias, gain_o, kept["act"], kept["cum"],
        kept["cum_t"], kept["tinv"], kept["fresh"], kept["heads"], mixed,
    )
    convolve()
    loads["gate"].wait()
    project(QKV, VALS, 256)
    store.put(kept["lin"], outs["lin"])
    for h, head in enumerate(heads):
        head()
        poll(3)
    until("done", 3)
    load("out", go, wobuf)
    for name in ("act", "cum", "cum_t", "tinv", "fresh", "heads"):
        store.put(kept[name], outs[name])
    loads["out"].wait()

    def out_step(k, carry):
        here = pl.ds(pl.multiple_of(k * 256, 256), 256)
        kept["middle"][:, here] = kept["xin"][:, here].astype(f32) + dot(mixed[...], wobuf[:, here])
        return carry

    lax.fori_loop(0, width // 256, out_step, 0)
    store.put(kept["middle"], outs["middle"])
    m = kept["middle"][...]
    norm = m * lax.rsqrt(jnp.mean(m * m, axis=1, keepdims=True) + 1e-5) * gain2[...]
    normed_mid[...] = norm.astype(bf16)
    kept["normed_mid_t"][...] = transposed(norm)
    store.put(kept["normed_mid_t"], outs["normed_mid_t"])
    kept["mixed_t"][...] = transposed(mixed[...].astype(f32))
    store.put(kept["mixed_t"], outs["mixed_t"])
    until("done", 5)
    load("down", gd, wdbuf)

    def ffn(at, cols, up_at):
        def step(k, carry):
            here = pl.ds(pl.multiple_of(at + k * FTILE, FTILE), FTILE)
            there = pl.ds(pl.multiple_of(ff + at + k * FTILE, FTILE), FTILE)
            grad = dot(kept["dy"][...], wdbuf[here, :], 1, 1)
            gate = dot(normed_mid[...], wbuf[:, here])
            up = dot(normed_mid[...], wbuf[:, there])
            sg = sigm(gate)
            silu = gate * sg
            hid = silu * up
            kept["hidden"][:, here] = hid.astype(bf16)
            kept["hidden_t"][here, :] = transposed(hid)
            kept["grads_gu"][:, here] = (grad * up * (sg + silu * (1.0 - sg))).astype(bf16)
            kept["grads_gu"][:, there] = (grad * silu).astype(bf16)
            return carry

        lax.fori_loop(0, cols // FTILE, step, 0)

    low, high = pl.ds(0, FF_SPLIT), pl.ds(FF_SPLIT, ff - FF_SPLIT)
    shift = lambda s: pl.ds(ff + s.start, s.size)
    until("done", 6)
    load("g0", gg.at[:, low], wbuf.at[:, low])
    until("done", 7)
    load("u0", gu.at[:, low], wbuf.at[:, shift(low)])
    poll(2)
    for name in ("down", "g0", "u0"):
        loads[name].wait()
    ffn(0, FF_SPLIT, 0)
    until("done", 8)
    load("g1", gg.at[:, high], wbuf.at[:, high])
    until("done", 9)
    load("u1", gu.at[:, high], wbuf.at[:, shift(high)])
    loads["g1"].wait()
    loads["u1"].wait()
    ffn(FF_SPLIT, ff - FF_SPLIT, 0)
    for name in ("hidden", "hidden_t", "grads_gu"):
        store.put(kept[name], outs[name])
    for c in first + exchange:
        c.wait_send()
    for f in made:
        f.close()
    store.wait()


def forward_call(n_shard, reps, offs, lens, tokens, cot, deal, small_in, rate, bias, weights):
    anywhere = pl.BlockSpec(memory_space=pl.ANY)
    held = pl.BlockSpec(memory_space=pltpu.VMEM)
    words = pl.BlockSpec(memory_space=pltpu.SMEM)
    rows, width = tokens.shape
    ff = weights[6].shape[1]
    sd = jax.ShapeDtypeStruct
    wide = QKV + VALS + LANES
    vals_rows, ff_rows = weights[5].shape[0] * n_shard, weights[8].shape[0] * n_shard
    gathered = [
        sd((width, wide), bf16), sd((vals_rows, width), bf16), sd((width, ff), bf16), sd((width, ff), bf16),
        sd((ff_rows, width), bf16),
    ]
    shapes = [fn(rows, width, ff) for _, fn in FORWARD_SAVED]
    sems = pltpu.SemaphoreType.DMA
    flows = 12
    count = flows * Flow.count(n_shard // 4, True)
    scratch = [pltpu.VMEM(s, d) for s, d in shapes] + [
        pltpu.VMEM((n_shard, 8, rows), jnp.int32), sems((n_shard,)), sems((n_shard,)),
        pltpu.VMEM((n_shard, 16, width), bf16), sems((n_shard,)), sems((n_shard,)),
        pltpu.VMEM((2, rows, width), bf16), pltpu.VMEM((2, rows, width), bf16), sems((2, n_shard)), sems((2, n_shard)),
        pltpu.VMEM((width, 2 * ff), bf16), pltpu.VMEM((vals_rows, width), bf16), pltpu.VMEM((ff_rows, width), bf16),
        sems((16,)), sems((count,)), sems((count,)), sems((flows,)), sems((len(shapes),)),
        pltpu.VMEM((rows, width), bf16), pltpu.VMEM((rows, VALS), bf16), pltpu.VMEM((rows, width), bf16),
    ]
    scratch += [pltpu.VMEM(weights[k].shape, bf16) for k in (0, 1, 2, 3, 4, 5, 8, 6, 7)] + [sems((9,))]
    res = pl.pallas_call(
        functools.partial(forward_kernel, n_shard, reps),
        in_specs=[words, words] + [held] * 6 + [anywhere] * 9,
        out_specs=[anywhere] * (5 + len(shapes)),
        out_shape=gathered + [sd(s, d) for s, d in shapes],
        scratch_shapes=scratch,
        compiler_params=pltpu.CompilerParams(collective_id=1, has_side_effects=True, vmem_limit_bytes=62 << 20),
    )(offs, lens, tokens, cot, deal, small_in, rate, bias, *weights)
    return res[:5], dict(zip([name for name, _ in FORWARD_SAVED], res[5:]))


WIDE = 512
NARROW = 256


class Stream:
    def __init__(self, buf, sem, parts):
        self.buf, self.sem, self.parts, self.at = buf, sem, parts, 0
        self.copies = {}

    def start(self):
        self.issue(0)

    def issue(self, k):
        if k < len(self.parts):
            pairs = self.parts[k](self.buf.at[k % 2])
            self.copies[k] = [pltpu.make_async_copy(s, d, self.sem.at[k % 2, i]) for i, (s, d) in enumerate(pairs)]
            for c in self.copies[k]:
                c.start()

    def take(self):
        k = self.at
        self.at += 1
        self.issue(k + 1)
        for c in self.copies[k]:
            c.wait()
        return k, self.buf.at[k % 2]


BACK_KEPT = tuple(name for name, _ in FORWARD_SAVED if name not in ("hidden",))


def backward_kernel(n_shard, reps, rings, small, *refs):
    take = iter(refs)
    get = lambda k: [next(take) for _ in range(k)]
    offs, lens, rate, bias = get(4)
    gp, go, gg, gu, gd = get(5)
    given = dict(zip(BACK_KEPT, get(len(BACK_KEPT))))
    o_rows, o_grad, o_ffn, o_down, o_out, o_proj, o_small = get(7)
    kept = dict(zip(BACK_KEPT, get(len(BACK_KEPT))))
    ring_a, ring_b = rings
    ring_a.bind(get(10))
    ring_b.bind(get(10))
    small.bind(get(3))
    (load_sem, wbuf, wsem, nbuf, nsem, acc, middle_grad, branch, mix_grad, dcols, drows, lin_grad, tap_grad, gain_grad,
     rate_grad, bias_grad, small_v, sent, come, tsend, trecv, rows_out, out_sem) = get(23)
    rows, width = kept["xin"].shape
    ff = gg.shape[1]
    per = rows // n_shard
    place = Place(n_shard, reps)
    p = place
    offsets = [offs[i] for i in range(offs.shape[0])]
    lengths = [lens[i] for i in range(lens.shape[0])]
    loads = {}
    order = (
        "normed_mid_t", "grads_gu", "middle", "dy", "params", "hidden_t", "cum", "cum_t", "tinv", "fresh", "heads",
        "act", "lin", "taps", "mixed_t", "normed_t", "xin", "pick", "place",
    )
    for k, name in enumerate(order):
        loads[name] = pltpu.make_async_copy(given[name], kept[name], load_sem.at[k])
        loads[name].start()
    have = set()

    def need(*names):
        for name in names:
            if name not in have:
                have.add(name)
                loads[name].wait()

    greet(place, True)
    pieces = []

    def tick(piece=None, fill=None):
        index = tick.index
        tick.index += 1
        pump(pieces, index)
        if piece is not None:
            pieces.append(piece())
            fill(pieces[-1])
            pieces[-1].send_core()

    tick.index = 0

    def grad_piece(ring, size, left, right_ref, right_at, cols, out, out_at):
        def fill(piece):
            tile = min(cols, 256)

            def step(t, carry):
                here = pl.ds(pl.multiple_of(t * tile, tile), tile)
                right = right_ref[:, pl.ds(pl.multiple_of(right_at + t * tile, LANES), tile)]
                value = dot(left[...], right).astype(bf16).reshape(ring.ys, 2, 2, size, tile)
                ring.own[piece.slot, :, :, :, pl.ds(0, size), here] = value
                return carry

            lax.fori_loop(0, cols // tile, step, 0)

        tick(lambda: Piece(ring, place, size, cols, out, out_at), fill)

    rows_a = width // n_shard

    def gu_piece(k):
        need("normed_mid_t", "grads_gu")
        at = k * WIDE
        grad_piece(ring_a, rows_a, kept["normed_mid_t"], kept["grads_gu"], at, WIDE, o_ffn, at)

    def down_piece(k):
        need("hidden_t", "dy")
        at = k * NARROW
        grad_piece(ring_b, ff // n_shard, kept["hidden_t"], kept["dy"], at, NARROW, o_down, at)

    def out_piece(k):
        need("mixed_t")
        at = k * NARROW
        grad_piece(ring_b, VALS // n_shard, kept["mixed_t"], branch, at, NARROW, o_out, at)

    def proj_piece(at, cols):
        need("normed_t")
        grad_piece(ring_a, rows_a, kept["normed_t"], lin_grad, at, cols, o_proj, at)

    def gu_part(k):
        cols = pl.ds(k * FTILE, FTILE)
        return lambda b: [(gg.at[:, cols], b.at[:, pl.ds(0, FTILE)]), (gu.at[:, cols], b.at[:, pl.ds(FTILE, FTILE)])]

    chunks = ff // FTILE
    gu_stream = Stream(wbuf, wsem, [gu_part(k) for k in range(chunks)])

    def gnm(count):
        need("grads_gu")
        for _ in range(count):
            k, buf = gu_stream.take()
            at = k * FTILE
            part = dot(kept["grads_gu"][:, at : at + FTILE], buf[:, 0:FTILE], 1, 1)
            part = part + dot(kept["grads_gu"][:, ff + at : ff + at + FTILE], buf[:, FTILE : 2 * FTILE], 1, 1)
            acc[...] = part if k == 0 else acc[...] + part

    def norm_back(values, gain, upstream):
        n = lax.rsqrt(jnp.mean(values * values, axis=1, keepdims=True) + 1e-5)
        u = upstream * gain
        gain_part = jnp.sum(upstream * values * n, axis=0, keepdims=True)
        return n * (u - values * (n * n) * jnp.mean(u * values, axis=1, keepdims=True)), gain_part

    def norm2():
        need("middle", "dy", "params")
        back, gain_part = norm_back(kept["middle"][...], kept["params"][13:14, :], acc[...])
        small_v[13:14, :] = gain_part
        total = kept["dy"][...].astype(f32) + back
        middle_grad[...] = total
        branch[...] = total.astype(bf16)

    def row_part(src, k):
        return lambda b: [(src.at[pl.ds(k * FTILE, FTILE), :], b)]

    out_stream = Stream(nbuf, nsem, [row_part(go, k) for k in range(VALS // FTILE)])
    down_stream = Stream(nbuf, nsem, [row_part(gd, k) for k in range(chunks)])

    def grad_mixed(count):
        for _ in range(count):
            k, buf = out_stream.take()
            mix_grad[:, k * FTILE : (k + 1) * FTILE] = dot(branch[...], buf[...], 1, 1)

    def result(count):
        need("hidden_t", "middle")
        for _ in range(count):
            k, buf = down_stream.take()
            part = dot(kept["hidden_t"][k * FTILE : (k + 1) * FTILE, :], buf[...], 0, 0)
            acc[...] = (kept["middle"][...] if k == 0 else acc[...]) + part

    exchange = {}

    def send_home(a, value):
        need("place")
        here = pl.ds(pl.multiple_of(p.s * per, 16), per)
        for at in range(0, width, 256):
            sent[a, :, at : at + 256] = dot(kept["place"][...], value[:, at : at + 256]).astype(bf16)
        exchange[a] = []
        for d in range(1, n_shard):
            t = (p.s + d) % n_shard
            exchange[a].append(
                remote(
                    sent.at[a, pl.ds(pl.multiple_of(t * per, 16), per)], come.at[a, here],
                    tsend.at[a, d], trecv.at[a, d], (p.r, t),
                )
            )
            exchange[a][-1].start()
        come[a, here, :] = sent[a, here, :]

    stores = []

    def arrive(a, out):
        need("pick")
        for c in exchange[a]:
            c.wait()
        for at in range(0, width, 256):
            rows_out[a, :, at : at + 256] = dot(kept["pick"][...], come[a, :, at : at + 256], 0, 0).astype(bf16)
        stores.append(pltpu.make_async_copy(rows_out.at[a], out, out_sem.at[a]))
        stores[-1].start()

    def wide_part(at, cols):
        return lambda b: [(gp.at[:, pl.ds(at, cols)], b.at[:, pl.ds(0, cols)])]

    proj_cuts = [(at, WIDE) for at in range(0, QKV + VALS, WIDE)] + [(QKV + VALS, LANES)]
    proj_stream = Stream(wbuf, wsem, [wide_part(at, cols) for at, cols in proj_cuts])

    def grad_normed(count):
        for _ in range(count):
            k, buf = proj_stream.take()
            at, cols = proj_cuts[k]
            part = dot(lin_grad[:, at : at + cols], buf[:, 0:cols], 1, 1)
            acc[...] = part if k == 0 else acc[...] + part

    def norm1():
        need("xin")
        back, gain_part = norm_back(kept["xin"][...].astype(f32), kept["params"][12:13, :], acc[...])
        small_v[12:13, :] = gain_part
        rows_out[1] = (middle_grad[...] + back).astype(bf16)

    def pack_small():
        small_v[14:16, :] = jnp.zeros((2, width), f32)
        for t in range(4):
            for g in range(QKV // width):
                row = t * (QKV // width) + g
                small_v[row : row + 1, :] = tap_grad[t : t + 1, g * width : (g + 1) * width]
        small_v[14:15, 0:DVH] = gain_grad[...]
        small_v[14:15, DVH : DVH + LANES] = rate_grad[...]
        small_v[14:15, DVH + LANES : DVH + 2 * LANES] = bias_grad[...]

    gu_stream.start()
    gu_piece(0)
    gnm(2)
    gu_piece(1)
    gnm(3)
    gu_piece(2)
    gnm(3)
    gu_piece(3)
    gnm(3)
    out_stream.start()
    gu_piece(4)
    norm2()
    gu_piece(5)
    grad_mixed(VALS // FTILE)
    need("cum", "cum_t", "tinv", "fresh", "heads", "act", "lin", "taps")
    clear, heads, rates, convs = mixer_backward(
        rows, offsets, lengths, kept["lin"], kept["taps"], rate, bias, kept["params"].at[14:15, 0:DVH], kept["act"],
        kept["cum"], kept["cum_t"], kept["tinv"], kept["fresh"], kept["heads"], mix_grad,
        kept["act"], dcols, drows, lin_grad, tap_grad, gain_grad, rate_grad, bias_grad,
    )
    clear()
    gu_piece(6)
    heads[0]()
    gu_piece(7)
    heads[1]()
    gu_piece(8)
    heads[2]()
    gu_piece(9)
    heads[3]()
    gu_piece(10)
    heads[4]()
    down_piece(0)
    heads[5]()
    down_piece(1)
    rates()
    convs[0]()
    down_piece(2)
    down_stream.start()
    convs[1]()
    down_piece(3)
    result(chunks // 2)
    out_piece(0)
    result(chunks - chunks // 2)
    rows_out[0] = acc[...].astype(bf16)
    send_home(0, rows_out.at[0])
    proj_stream.start()
    out_piece(1)
    grad_normed(5)
    out_piece(2)
    grad_normed(len(proj_cuts) - 5)
    out_piece(3)
    norm1()
    send_home(1, rows_out.at[1])
    pack_small()
    value = small_v[...]
    for k, (at, cols) in enumerate(proj_cuts[6:9] + proj_cuts[0:6] + proj_cuts[9:]):
        if 1 <= k <= 4:
            small.begin(place, k - 1, value)
        proj_piece(at, cols)
        if 1 <= k <= 4:
            value = small.end(k - 1)
        if k == 5:
            arrive(0, o_rows)
        if k == 7:
            arrive(1, o_grad)
    for _ in range(7):
        tick()
    o_small[...] = value
    for c in stores:
        c.wait()


def backward_call(n_shard, reps, offs, lens, rate, bias, gathered, saved):
    anywhere = pl.BlockSpec(memory_space=pl.ANY)
    held = pl.BlockSpec(memory_space=pltpu.VMEM)
    words = pl.BlockSpec(memory_space=pltpu.SMEM)
    rows, width = saved["xin"].shape
    ff = gathered[2].shape[1]
    sd = jax.ShapeDtypeStruct
    wide = QKV + VALS + LANES
    sems = pltpu.SemaphoreType.DMA
    rings = (Ring(n_shard, width // n_shard, WIDE), Ring(n_shard, ff // n_shard, NARROW))
    small = Small(n_shard, reps, 16, width)
    outs = [
        sd((rows, width), bf16), sd((rows, width), bf16), sd((width // n_shard, 2 * ff), bf16),
        sd((ff // n_shard, width), bf16), sd((VALS // n_shard, width), bf16), sd((width // n_shard, wide), bf16),
        sd((16, width), f32),
    ]
    vmem = pltpu.VMEM
    scratch = [vmem(saved[name].shape, saved[name].dtype) for name in BACK_KEPT]
    scratch += rings[0].scratch() + rings[1].scratch() + small.scratch()
    scratch += [
        sems((len(BACK_KEPT),)), vmem((2, width, WIDE), bf16), sems((2, 2)), vmem((2, FTILE, width), bf16), sems((2, 1)),
        vmem((rows, width), f32), vmem((rows, width), f32), vmem((rows, width), bf16), vmem((rows, VALS), f32),
        vmem((rows, LANES), f32), vmem((LANES, rows), f32), vmem((rows, wide), bf16), vmem((4, QKV), f32),
        vmem((1, DVH), f32), vmem((1, LANES), f32), vmem((1, LANES), f32), vmem((16, width), f32),
        vmem((2, rows, width), bf16), vmem((2, rows, width), bf16), sems((2, n_shard)), sems((2, n_shard)),
        vmem((2, rows, width), bf16), sems((2,)),
    ]
    return pl.pallas_call(
        functools.partial(backward_kernel, n_shard, reps, rings, small),
        in_specs=[words, words, held, held] + [anywhere] * (5 + len(BACK_KEPT)),
        out_specs=[anywhere] * 6 + [held],
        out_shape=outs,
        scratch_shapes=scratch,
        compiler_params=pltpu.CompilerParams(collective_id=0, has_side_effects=True, vmem_limit_bytes=63 << 20),
    )(offs, lens, rate, bias, *gathered, *[saved[name] for name in BACK_KEPT])


def local(
    reps, tokens, cotangent, deal, offsets, lengths, norm1_gain, q_weight, k_weight, v_weight, conv_weight,
    beta_weight, decay_weight, log_rate, step_bias, out_gate_weight, out_norm_gain, out_weight, norm2_gain,
    ffn_gate, ffn_up, ffn_down,
):
    rows, width = tokens.shape
    n = lax.axis_size("shard")
    s = lax.axis_index("shard")
    pad = LANES - 2 * HEADS
    bd_weight = jnp.concatenate([beta_weight, decay_weight, jnp.zeros((beta_weight.shape[0], pad), bf16)], axis=1)
    lanes = lambda a: jnp.pad(a, (HEADS, LANES - 2 * HEADS))[None, :]
    rate, bias = lanes(log_rate), lanes(step_bias)

    def spread(vector):
        size = vector.shape[0]
        wide = lax.dynamic_update_slice(jnp.zeros((size * n,), bf16), vector, (s * size,))
        return jnp.pad(wide, (0, width - size * n))[None]

    taps = lax.dynamic_update_slice(jnp.zeros((4, QKV), bf16), conv_weight, (0, s * conv_weight.shape[1]))
    small_in = jnp.concatenate(
        [taps.reshape(-1, width), spread(norm1_gain), spread(norm2_gain), spread(out_norm_gain), jnp.zeros((1, width), bf16)]
    )
    weights = (q_weight, k_weight, v_weight, out_gate_weight, bd_weight, out_weight, ffn_gate, ffn_up, ffn_down)
    deals = jnp.broadcast_to(deal[None, :], (8, rows))
    gathered, saved = forward_call(
        n, reps, offsets[0], lengths[0], tokens, cotangent, deals, small_in, rate, bias, weights
    )
    home_rows, home_grad, s_ffn, s_down, s_out, s_proj, small = backward_call(
        n, reps, offsets[0], lengths[0], rate, bias, gathered, saved
    )

    def part(a, dim=0):
        size = a.shape[dim] // n
        return lax.dynamic_slice_in_dim(a, s * size, size, dim)

    f = lambda a: a.astype(f32)
    ff = ffn_gate.shape[1]
    at = QKV + VALS
    return (
        home_rows, home_grad, part(small[12]), f(s_proj[:, :KEYS]), f(s_proj[:, KEYS : 2 * KEYS]),
        f(s_proj[:, 2 * KEYS : QKV]), part(small[:12].reshape(4, QKV), 1), f(s_proj[:, at : at + HEADS]),
        f(s_proj[:, at + HEADS : at + 2 * HEADS]), small[14, DVH + HEADS : DVH + 2 * HEADS],
        small[14, DVH + LANES + HEADS : DVH + LANES + 2 * HEADS], f(s_proj[:, QKV:at]), part(small[14, :DVH]),
        f(s_out), part(small[13]), f(s_ffn[:, :ff]), f(s_ffn[:, ff:]), f(s_down),
    )


def solution(mesh):
    rows2, shard0 = P(("rep", "shard"), None), P("shard", None)
    vec = P("shard")
    in_specs = (
        rows2, rows2, P(("rep", "shard")), rows2, rows2, vec, shard0, shard0, shard0, P(None, "shard"),
        shard0, shard0, P(), P(), shard0, vec, shard0, vec, shard0, shard0, shard0,
    )
    out_specs = (
        rows2, rows2, vec, shard0, shard0, shard0, P(None, "shard"), shard0, shard0, P(), P(), shard0,
        vec, shard0, vec, shard0, shard0, shard0,
    )
    body = functools.partial(local, mesh.shape["rep"])
    return jax.shard_map(body, mesh=mesh, in_specs=in_specs, out_specs=out_specs, check_vma=False)
```

```python
import functools
import jax
import jax.numpy as jnp
from jax import lax
from jax.experimental import pallas as pl
from jax.experimental.pallas import tpu as pltpu
from jax.sharding import PartitionSpec as P

f32 = jnp.float32
bf16 = jnp.bfloat16
HEADS = 6
DK = 128
DVH = 256
KEYS = 768
VALS = 1536
QKV = 2 * KEYS + VALS
LANES = 128


def two_parts(a):
    hi = a.astype(bf16)
    return hi, (a - hi.astype(f32)).astype(bf16)


def dot(a, b, ca=1, cb=0):
    return lax.dot_general(a, b, (((ca,), (cb,)), ((), ())), preferred_element_type=f32)


def dot3(a, b, ca=1, cb=0):
    ah, al = a
    bh, bl = b
    return dot(ah, bh, ca, cb) + (dot(ah, bl, ca, cb) + dot(al, bh, ca, cb))


def tri_dot(tri, cols):
    hi = cols.astype(bf16)
    rest = cols - hi.astype(f32)
    mid = rest.astype(bf16)
    lo = (rest - mid.astype(f32)).astype(bf16)
    return dot(tri, hi) + (dot(tri, mid) + dot(tri, lo))


def sigm(a):
    return 1.0 / (1.0 + jnp.exp(-a))


def softplus(a):
    return jnp.maximum(a, 0.0) + jnp.log1p(jnp.exp(-jnp.abs(a)))


def layout_cols(offs, lens, n, shape, dim):
    row = lax.broadcasted_iota(jnp.int32, shape, dim)
    begin = jnp.zeros_like(row)
    extent = jnp.zeros_like(row)
    for i in range(len(offs)):
        inside = row >= offs[i]
        begin = jnp.where(inside, offs[i], begin)
        extent = jnp.where(inside, lens[i], extent)
    return begin, row - begin, (row - begin) < extent


def conv_chunk(x, taps, pos, cols):
    total = taps[0:1, cols] * x
    for t in range(1, 4):
        total = total + taps[t : t + 1, cols] * jnp.where(pos >= t, pltpu.roll(x, t, 0), 0.0)
    return total


def lane_pick(a, lane, index):
    return jnp.sum(jnp.where(lane == index, a, 0.0), axis=1, keepdims=True)


def pair_masks(n, begin_c, begin_r):
    i = lax.broadcasted_iota(jnp.int32, (n, n), 0)
    j = lax.broadcasted_iota(jnp.int32, (n, n), 1)
    same = begin_c == begin_r
    return i, j, (i >= j) & same


def mixer_forward(n, offs, lens, lin, taps, rate, bias, gain, act, cum, cum_t, tinv, fresh, heads_out, mixed):
    begin_c, pos, live = layout_cols(offs, lens, n, (n, 1), 0)
    begin_r, _, _ = layout_cols(offs, lens, n, (1, n), 1)
    live_f = live.astype(f32)
    width = 384

    def conv_step(step, carry):
        cols = pl.ds(pl.multiple_of(step * width, width), width)
        pre = conv_chunk(lin[:, cols], taps, pos, cols)
        act[:, cols] = pre * sigm(pre)
        return carry

    lane = lax.broadcasted_iota(jnp.int32, (n, LANES), 1)
    bd = lin[:, QKV + VALS : QKV + VALS + LANES]
    beta = sigm(bd) * live_f
    decay = -jnp.exp(rate[...]) * softplus(bd + bias[...]) * live_f
    i, j, low = pair_masks(n, begin_c, begin_r)
    eye = (i == j).astype(f32)

    def convolve():
        lax.fori_loop(0, QKV // width, conv_step, 0)
        total = tri_dot((i >= j).astype(bf16), decay)
        cum[...] = total
        cum_t[...] = total.T

    def one_head(h):
        kcols = pl.ds(pl.multiple_of(h * DK, DK), DK)
        ka = act[:, pl.ds(pl.multiple_of(KEYS + h * DK, DK), DK)]
        qa = act[:, kcols]
        vcols = pl.ds(pl.multiple_of(h * DVH, DVH), DVH)
        v = act[:, pl.ds(pl.multiple_of(2 * KEYS + h * DVH, DVH), DVH)]
        q = qa * (lax.rsqrt(jnp.sum(qa * qa, axis=1, keepdims=True) + 1e-6) * DK**-0.5)
        k = ka * lax.rsqrt(jnp.sum(ka * ka, axis=1, keepdims=True) + 1e-6)
        beta_c = lane_pick(beta, lane, h)
        cum_c = lane_pick(cum[...], lane, HEADS + h)
        cum_r = cum_t[pl.ds(HEADS + h, 1), :]
        kk, qq = two_parts(k), two_parts(q)
        dec = jnp.where(low, jnp.exp(jnp.where(low, cum_c - cum_r, 0.0)), 0.0)
        system = jnp.where(i > j, beta_c * dot3(kk, kk, 1, 1) * dec, 0.0)
        inv = eye - jnp.where((i // 2) == (j // 2), system, 0.0)
        size = 2
        while size < n:
            off = jnp.where(((i // (2 * size)) == (j // (2 * size))) & ((i // size) != (j // size)), system, 0.0)
            parts = two_parts(inv)
            inv = inv - dot3(two_parts(dot3(parts, two_parts(off))), parts)
            size *= 2
        tinv[h] = inv
        u = dot3(two_parts(inv), two_parts(beta_c * v))
        fresh[:, vcols] = u
        o = dot3(two_parts(dot3(qq, kk, 1, 1) * dec), two_parts(u)) * live_f
        heads_out[:, vcols] = o
        gate = lin[:, pl.ds(pl.multiple_of(QKV + h * DVH, DVH), DVH)]
        scaled = o * lax.rsqrt(jnp.mean(o * o, axis=1, keepdims=True) + 1e-5)
        mixed[:, vcols] = (scaled * gain[...] * (gate * sigm(gate))).astype(bf16)

    return convolve, [functools.partial(one_head, h) for h in range(HEADS)]


def mixer_backward(
    n, offs, lens, lin, taps, rate, bias, gain, act, cum, cum_t, tinv, fresh, heads_out, grad_mixed,
    dact, dcols, drows, lin_grad, tap_grad, gain_grad, rate_grad, bias_grad,
):
    begin_c, pos, live = layout_cols(offs, lens, n, (n, 1), 0)
    begin_r, _, _ = layout_cols(offs, lens, n, (1, n), 1)
    live_f = live.astype(f32)
    lane = lax.broadcasted_iota(jnp.int32, (n, LANES), 1)
    bd = lin[:, QKV + VALS : QKV + VALS + LANES]
    sig_b = sigm(bd)
    beta = sig_b * live_f
    i, j, low = pair_masks(n, begin_c, begin_r)
    strict = low & (i > j)

    def clear():
        gain_grad[...] = jnp.zeros_like(gain_grad)
        dcols[...] = jnp.zeros_like(dcols)
        drows[...] = jnp.zeros_like(drows)

    def one_head(h):
        kcols = pl.ds(pl.multiple_of(h * DK, DK), DK)
        kcols2 = pl.ds(pl.multiple_of(KEYS + h * DK, DK), DK)
        vcols = pl.ds(pl.multiple_of(h * DVH, DVH), DVH)
        vcols2 = pl.ds(pl.multiple_of(2 * KEYS + h * DVH, DVH), DVH)
        gcols = pl.ds(pl.multiple_of(QKV + h * DVH, DVH), DVH)
        ka = act[:, kcols2]
        qa = act[:, kcols]
        v = act[:, vcols2]
        o = heads_out[:, vcols]
        gate = lin[:, gcols]
        dm = grad_mixed[:, vcols]
        ro = lax.rsqrt(jnp.mean(o * o, axis=1, keepdims=True) + 1e-5)
        scaled = o * ro
        sg = sigm(gate)
        si = gate * sg
        gain_grad[...] += jnp.sum(dm * scaled * si, axis=0, keepdims=True)
        lin_grad[:, gcols] = (dm * scaled * gain[...] * (sg + si * (1.0 - sg))).astype(bf16)
        ds = dm * gain[...] * si
        d_o = two_parts(ro * (ds - scaled * jnp.mean(ds * scaled, axis=1, keepdims=True)) * live_f)
        rq = lax.rsqrt(jnp.sum(qa * qa, axis=1, keepdims=True) + 1e-6)
        rk = lax.rsqrt(jnp.sum(ka * ka, axis=1, keepdims=True) + 1e-6)
        qhat = qa * rq
        k = ka * rk
        kk, qq = two_parts(k), two_parts(qhat * DK**-0.5)
        beta_c = lane_pick(beta, lane, h)
        cum_c = lane_pick(cum[...], lane, HEADS + h)
        cum_r = cum_t[pl.ds(HEADS + h, 1), :]
        dec = jnp.where(low, jnp.exp(jnp.where(low, cum_c - cum_r, 0.0)), 0.0)
        gram = dot3(kk, kk, 1, 1)
        qk = dot3(qq, kk, 1, 1)
        uu = two_parts(fresh[:, vcols])
        du = dot3(two_parts(qk * dec), d_o, 0, 0)
        dp = dot3(d_o, uu, 1, 1) * dec
        db = dot3(two_parts(tinv[h]), two_parts(du), 0, 0)
        da = jnp.where(strict, -dot3(two_parts(db), uu, 1, 1), 0.0) * dec
        x = da * gram
        dbeta = jnp.sum(x, axis=1, keepdims=True) + jnp.sum(db * v, axis=1, keepdims=True)
        e = dp * qk + x * beta_c
        dcols[...] += jnp.where(lane == h, dbeta, 0.0) + jnp.where(
            lane == HEADS + h, jnp.sum(e, axis=1, keepdims=True), 0.0
        )
        drows[pl.ds(HEADS + h, 1), :] = jnp.sum(e, axis=0, keepdims=True)
        dact[:, vcols2] = beta_c * db
        dg = two_parts(da * beta_c)
        dpp = two_parts(dp)
        dq = dot3(dpp, kk)
        dk = dot3(dpp, qq, 0, 0) + dot3(dg, kk) + dot3(dg, kk, 0, 0)
        dact[:, kcols] = (rq * DK**-0.5) * (dq - qhat * jnp.sum(dq * qhat, axis=1, keepdims=True))
        dact[:, kcols2] = rk * (dk - k * jnp.sum(dk * k, axis=1, keepdims=True))

    def rates():
        dcum = jnp.where((lane >= HEADS) & (lane < 2 * HEADS), dcols[...] - drows[...].T, 0.0)
        ddecay = tri_dot((i <= j).astype(bf16), dcum)
        z = bd + bias[...]
        speed = -jnp.exp(rate[...]) * live_f
        dz = ddecay * speed * sigm(z)
        rate_grad[...] = jnp.sum(ddecay * speed * softplus(z), axis=0, keepdims=True)
        bias_grad[...] = jnp.sum(dz, axis=0, keepdims=True)
        dbeta_lin = dcols[...] * live_f * sig_b * (1.0 - sig_b)
        both = jnp.where(lane < HEADS, dbeta_lin, jnp.where(lane < 2 * HEADS, dz, 0.0))
        lin_grad[:, QKV + VALS : QKV + VALS + LANES] = both.astype(bf16)

    width = 384

    def conv_step(step, carry):
        cols = pl.ds(pl.multiple_of(step * width, width), width)
        x = lin[:, cols]
        pre = conv_chunk(x, taps, pos, cols)
        sg = sigm(pre)
        dc = dact[:, cols] * (sg + pre * sg * (1.0 - sg))
        dx = taps[0:1, cols] * dc
        tap_grad[0:1, cols] = jnp.sum(dc * x, axis=0, keepdims=True)
        for t in range(1, 4):
            masked = jnp.where(pos >= t, dc, 0.0)
            dx = dx + taps[t : t + 1, cols] * pltpu.roll(masked, n - t, 0)
            tap_grad[t : t + 1, cols] = jnp.sum(masked * pltpu.roll(x, t, 0), axis=0, keepdims=True)
        lin_grad[:, cols] = dx.astype(bf16)
        return carry

    def convolve(first, last):
        return lambda: lax.fori_loop(first, last, conv_step, 0)

    heads = [functools.partial(one_head, h) for h in range(HEADS)]
    total = QKV // width
    return clear, heads, rates, [convolve(0, total // 2), convolve(total // 2, total)]


MESH = pl.DeviceIdType.MESH


class Place:
    def __init__(self, n_shard, n_rep):
        self.n, self.reps = n_shard, n_rep
        self.ys = n_shard // 4
        self.r = lax.axis_index("rep")
        self.s = lax.axis_index("shard")
        self.c = self.s % 2
        self.x = (self.s // 2) % 2
        self.y = self.s // 4
        half = n_rep // 2
        low = self.r < half
        self.depth = jnp.where(low, self.r, n_rep - 1 - self.r)
        self.inner = jnp.where(low, self.r + 1, self.r - 1)
        self.outer = jnp.where(low, self.r - 1, self.r + 1)
        self.middle = self.depth == half - 1
        self.deep = self.depth > 0
        self.half = self.depth % 2

    def partner(self):
        return (self.r + 1 - 2 * (self.r % 2), self.s)

    def shard_id(self, y, x, c):
        return (self.r, (y * 2 + x) * 2 + c)

    def core_peer(self):
        return self.shard_id(self.y, self.x, 1 - self.c)

    def x_peer(self):
        return self.shard_id(self.y, 1 - self.x, self.c)

    def y_of(self, step):
        return (self.y + step) % self.ys

    def y_peer(self, step):
        return self.shard_id(self.y_of(step), self.x, self.c)


def remote(src, dst, send, recv, device):
    return pltpu.make_async_remote_copy(
        src_ref=src, dst_ref=dst, send_sem=send, recv_sem=recv, device_id=device, device_id_type=MESH
    )


def greet(place, with_rep):
    barrier = pltpu.get_barrier_semaphore()
    n = place.n
    for step in range(1, n):
        pl.semaphore_signal(
            barrier, inc=1, device_id=(place.r, (place.s + step) % n), device_id_type=MESH
        )
    if not with_rep:
        pl.semaphore_wait(barrier, n - 1)
        return
    for step in range(1, place.reps):
        pl.semaphore_signal(
            barrier, inc=1, device_id=((place.r + step) % place.reps, place.s), device_id_type=MESH
        )
    pl.semaphore_wait(barrier, n - 1 + place.reps - 1)


def add_into(dst, idx, *others):
    total = dst[idx].astype(f32)
    for ref, at in others:
        total = total + ref[at].astype(f32)
    dst[idx] = total.astype(dst.dtype)


RING = 10
ZRING = 12


def halved(rows):
    return (rows // 2) // 16 * 16


class Ring:
    def __init__(self, n, rows, cols, twins=1):
        self.n, self.rows, self.cols, self.twins = n, rows, cols, twins
        self.ys = n // 4
        self.count = 0

    def scratch(self):
        k, ys, cols = RING, self.ys, self.cols
        sems = pltpu.SemaphoreType.DMA
        per = 3 + 2 * (ys - 1)
        half = self.rows - halved(self.rows)
        return [
            pltpu.VMEM((k, ys, 2, 2, self.rows, cols), bf16),
            pltpu.VMEM((k, ys, 2, self.rows, cols), bf16),
            pltpu.VMEM((k, ys, half, cols), bf16),
            pltpu.VMEM((k, ys - 1, 2, half, cols), bf16),
            pltpu.VMEM((k, ys - 1, half, cols), bf16),
            pltpu.VMEM((k, half, cols), bf16),
            pltpu.VMEM((4, ZRING, self.twins, self.rows, cols), bf16),
            sems((k, per)),
            sems((k, per)),
            sems((ZRING, 6 + self.twins)),
        ]

    def bind(self, refs):
        (self.own, self.r0, self.r1a, self.r1b, self.r2a, self.r2b, self.z, self.send, self.recv, self.zsem) = refs


class Piece:
    def __init__(self, ring, place, rows, cols, out, out_cols):
        self.ring, self.p, self.rows = ring, place, rows
        self.twin = len(out_cols) == 2
        self.side = pl.ds(0, len(out_cols))
        self.slot, self.zslot = ring.count % RING, ring.count % ZRING
        ring.count += 1
        self.w = pl.ds(0, cols)
        self.ra = halved(rows)
        self.rb = rows - self.ra
        self.all_rows = pl.ds(0, rows)
        self.outs = [out.at[:, pl.ds(at, cols)] for at in out_cols]

    def own_view(self):
        return self.ring.own.at[self.slot, :, :, :, self.all_rows, self.w]

    def store_rows(self, value):
        ring = self.ring
        shaped = value.reshape(ring.ys, 2, 2, rinself.rows, value.shape[-1])
        ring.own[self.slot, :, :, :, self.all_rows, self.w] = shaped

    def send_core(self):
        g, p, k = self.ring, self.p, self.slot
        self.c0 = remote(
            g.own.at[k, :, :, 1 - p.c, self.all_rows, self.w], g.r0.at[k, :, :, self.all_rows, self.w],
            g.send.at[k, 0], g.recv.at[k, 0], p.core_peer(),
        )
        self.c0.start()

    def after_core(self):
        g, p, k, w = self.ring, self.p, self.slot, self.w
        rows = self.all_rows
        self.c0.wait()

        def step(q, carry):
            yy, xx = q // 2, q % 2
            add_into(g.own, (k, yy, xx, p.c, rows, w), (g.r0, (k, yy, xx, rows, w)))
            return carry

        lax.fori_loop(0, g.ys * 2, step, 0)
        top, low = pl.ds(0, self.ra), pl.ds(self.ra, self.rb)
        first, second = pl.ds(0, self.ra), pl.ds(0, self.rb)
        self.c1 = [
            remote(
                g.own.at[k, :, 1 - p.x, p.c, top, w], g.r1a.at[k, :, first, w],
                g.send.at[k, 1], g.recv.at[k, 1], p.x_peer(),
            )
        ]
        for d in range(1, g.ys):
            self.c1.append(
                remote(
                    g.own.at[k, p.y_of(d), :, p.c, low, w], g.r1b.at[k, d - 1, :, second, w],
                    g.send.at[k, 1 + d], g.recv.at[k, 1 + d], p.y_peer(d),
                )
            )
        for c in self.c1:
            c.start()

    def after_first(self):
        g, p, k, w = self.ring, self.p, self.slot, self.w
        top, low = pl.ds(0, self.ra), pl.ds(self.ra, self.rb)
        first, second = pl.ds(0, self.ra), pl.ds(0, self.rb)
        for c in self.c1:
            c.wait()
        for yy in range(g.ys):
            add_into(g.own, (k, yy, p.x, p.c, top, w), (g.r1a, (k, yy, first, w)))
        for xx in range(2):
            add_into(
                g.own, (k, p.y, xx, p.c, low, w),
                *[(g.r1b, (k, d, xx, second, w)) for d in range(g.ys - 1)],
            )
        self.c2 = [
            remote(
                g.own.at[k, p.y, 1 - p.x, p.c, low, w], g.r2b.at[k, second, w],
                g.send.at[k, 1 + g.ys], g.recv.at[k, 1 + g.ys], p.x_peer(),
            )
        ]
        for d in range(1, g.ys):
            self.c2.append(
                remote(
                    g.own.at[k, p.y_of(d), p.x, p.c, top, w], g.r2a.at[k, d - 1, first, w],
                    g.send.at[k, 1 + g.ys + d], g.recv.at[k, 1 + g.ys + d], p.y_peer(d),
                )
            )
        for c in self.c2:
            c.start()

    def after_second(self):
        g, p, k, w = self.ring, self.p, self.slot, self.w
        zk = self.zslot
        for c in self.c2:
            c.wait()
        top, low = pl.ds(0, self.ra), pl.ds(self.ra, self.rb)
        total = g.own[k, p.y, p.x, p.c, top, w].astype(f32)
        for d in range(g.ys - 1):
            total = total + g.r2a[k, d, 0 : self.ra, w].astype(f32)
        side = p.half if self.twin else 0
        g.z[0, zk, side, top, w] = total.astype(bf16)
        total = g.own[k, p.y, p.x, p.c, low, w].astype(f32) + g.r2b[k, 0 : self.rb, w].astype(f32)
        g.z[0, zk, side, low, w] = total.astype(bf16)
        if self.twin:
            g.z[0, zk, 1 - side, self.all_rows, w] = jnp.zeros((self.rows, w.size), bf16)
        z = lambda i: g.z.at[i, zk, self.side, self.all_rows, w]
        target = lambda r: (r, p.s)
        sem = g.zsem
        self.up = remote(z(0), z(1), sem.at[zk, 0], sem.at[zk, 1], target(p.inner))
        self.meet = remote(z(0), z(2), sem.at[zk, 2], sem.at[zk, 3], target(p.inner))
        self.down = remote(z(3), z(2), sem.at[zk, 4], sem.at[zk, 3], target(p.outer))
        self.home = [
            pltpu.make_async_copy(g.z.at[3, zk, i, self.all_rows, w], out, sem.at[zk, 6 + i])
            for i, out in enumerate(self.outs)
        ]

        @pl.when(p.depth == 0)
        def _():
            self.send_inward()

    def send_inward(self):
        p = self.p

        @pl.when(p.middle)
        def _():
            self.meet.start()

        @pl.when(jnp.logical_not(p.middle))
        def _():
            self.up.start()

    def after_up(self):
        g, p, zk, w = self.ring, self.p, self.zslot, self.w

        @pl.when(p.deep)
        def _():
            self.up.wait_recv()
            for i in range(len(self.outs)):
                add_into(g.z, (0, zk, i, self.all_rows, w), (g.z, (1, zk, i, self.all_rows, w)))
            self.send_inward()

    def finish(self, middle):
        g, p, zk, w = self.ring, self.p, self.zslot, self.w
        rows = self.all_rows

        @pl.when(p.middle if middle else jnp.logical_not(p.middle))
        def _():
            self.meet.wait_recv()
            for i in range(len(self.outs)):
                if middle:
                    both = g.z[0, zk, i, rows, w].astype(f32) + g.z[2, zk, i, rows, w].astype(f32)
                    g.z[3, zk, i, rows, w] = both.astype(bf16)
                else:
                    g.z[3, zk, i, rows, w] = g.z[2, zk, i, rows, w]

            @pl.when(p.deep)
            def _():
                self.down.start()

            for c in self.home:
                c.start()

    def close(self):
        p = self.p

        @pl.when(p.middle)
        def _():
            self.meet.wait_send()

        @pl.when(jnp.logical_not(p.middle))
        def _():
            self.up.wait_send()

        @pl.when(p.deep)
        def _():
            self.down.wait_send()

        for c in self.home:
            c.wait()


def pump(pieces, index):
    stages = [
        (2, lambda q: q.after_core()),
        (18, lambda q: q.close()),
        (17, lambda q: q.finish(False)),
        (14, lambda q: q.finish(True)),
        (11, lambda q: q.after_up()),
        (8, lambda q: q.after_second()),
        (5, lambda q: q.after_first()),
    ]
    for lag, act in stages:
        if 0 <= index - lag < len(pieces):
            act(pieces[index - lag])


class Small:
    def __init__(self, n, reps, rows, cols):
        self.n, self.ys, self.reps = n, n // 4, reps
        self.sizes = (2, 2, self.ys, reps)
        self.rows, self.cols = rows, cols

    def scratch(self):
        total = sum(self.sizes)
        return [
            pltpu.VMEM((total, self.rows, self.cols), f32),
            pltpu.SemaphoreType.DMA((total,)),
            pltpu.SemaphoreType.DMA((total,)),
        ]

    def bind(self, refs):
        self.buf, self.send, self.recv = refs

    def begin(self, place, axis, value):
        base = sum(self.sizes[:axis])
        size = self.sizes[axis]
        p = place
        mine = (p.c, p.x, p.y, p.r)[axis]
        slot = self.buf.at[base + mine]
        slot[...] = value
        self.copies = []
        for d in range(1, size):
            at = (mine + d) % size
            device = (
                p.shard_id(p.y, p.x, at), p.shard_id(p.y, at, p.c), p.shard_id(at, p.x, p.c), (at, p.s),
            )[axis]
            self.copies.append(remote(slot, slot, self.send.at[base + d], self.recv.at[base + d], device))
        for c in self.copies:
            c.start()

    def end(self, axis):
        base = sum(self.sizes[:axis])
        for c in self.copies:
            c.wait()
        total = self.buf[base]
        for d in range(1, self.sizes[axis]):
            total = total + self.buf[base + d]
        return total


class Flow:
    @staticmethod
    def count(ys, pair):
        return 5 + 12 * (ys - 1) if pair else 3 + 6 * (ys - 1)

    def __init__(self, place, src, src_at, cols, dst, dst_at, pair, send, recv, base, mine):
        self.p, self.rows, self.pair = place, src.shape[0], pair
        self.src_ref, self.src_at, self.dst, self.dst_at, self.width = src, src_at, dst, dst_at, cols
        self.send, self.recv, self.base, self.used = send, recv, base, 0
        self.ra = halved(self.rows)
        self.part = (place.r % 2) if pair else None
        whole = self.src_ref.at[:, self.columns(src_at, None)]
        self.mine = pltpu.make_async_copy(whole, self.region(place.y, place.x, place.c), mine)
        self.whole = whole
        self.all = []

    def columns(self, at, part):
        if part is None:
            return pl.ds(at if isinstance(at, int) else pl.multiple_of(at, LANES), self.width)
        half = self.width // 2
        return pl.ds(pl.multiple_of(at + part * half, LANES), half)

    def region(self, y, x, c, half=None, part=None):
        start = ((y * 2 + x) * 2 + c) * self.rows
        size = self.rows
        if half == 0:
            size = self.ra
        elif half == 1:
            start, size = start + self.ra, self.rows - self.ra
        return self.dst.at[pl.ds(pl.multiple_of(start, 16), size), self.columns(self.dst_at, part)]

    def copy(self, dst, device, src=None):
        at = self.base + self.used
        self.used += 1
        c = remote(dst if src is None else src, dst, self.send.at[at], self.recv.at[at], device)
        c.start()
        self.all.append(c)
        return c

    def begin(self):
        p = self.p
        own = self.region(p.y, p.x, p.c, None, self.part)
        src = self.src_ref.at[:, self.columns(self.src_at, self.part)]
        self.mine.start()
        self.from_x = self.copy(own, p.x_peer(), src)
        self.from_y = [self.copy(own, p.y_peer(d), src) for d in range(1, p.ys)]
        self.from_core = [self.copy(self.region(p.y, p.x, p.c), p.core_peer(), self.whole)]
        self.from_z, self.z_regions = [], []

    def share(self, *where):
        p = self.p
        if self.pair:
            self.from_z.append(self.copy(self.region(*where, self.part), (p.r + 1 - 2 * (p.r % 2), p.s)))
            self.z_regions.append(where)
        self.from_core.append(self.copy(self.region(*where, self.part), p.core_peer()))

    def forward(self):
        p = self.p
        steps = range(1, p.ys)
        self.from_x.wait_recv()
        self.diag = [self.copy(self.region(p.y, 1 - p.x, p.c, 0, self.part), p.y_peer(d)) for d in steps]
        self.share(p.y, 1 - p.x, p.c, None)
        for d in steps:
            self.from_y[d - 1].wait_recv()
            back = p.y_of(p.ys - d)
            self.diag.append(self.copy(self.region(back, p.x, p.c, 1, self.part), p.x_peer()))
            self.share(back, p.x, p.c, None)

    def relay(self):
        p = self.p
        for i, c in enumerate(self.diag):
            c.wait_recv()
            half, d = divmod(i, p.ys - 1)
            self.share(p.y_of(p.ys - d - 1), 1 - p.x, p.c, half)

    def swap(self):
        for c, where in zip(self.from_z, self.z_regions):
            c.wait_recv()
            self.from_core.append(self.copy(self.region(*where, 1 - self.part), self.p.core_peer()))

    def done(self):
        for c in self.from_core:
            c.wait_recv()
        self.mine.wait()

    def close(self):
        for c in self.all:
            c.wait_send()


FTILE = 256
FF_TILE = 512


def cuts(total, step):
    return [(at, min(step, total - at)) for at in range(0, total, step)]


def one_hot_rows(values, count):
    return lax.broadcasted_iota(jnp.int32, (count, values.shape[1]), 0) == values


class Store:
    def __init__(self, sem):
        self.sem, self.all = sem, []

    def put(self, src, dst):
        c = pltpu.make_async_copy(src, dst, self.sem.at[len(self.all)])
        c.start()
        self.all.append(c)

    def wait(self):
        for c in self.all:
            c.wait()


FORWARD_SAVED = (
    ("xin", lambda n, d, f: ((n, d), bf16)),
    ("dy", lambda n, d, f: ((2 * n, d), bf16)),
    ("normed_t", lambda n, d, f: ((d, n), bf16)),
    ("lin", lambda n, d, f: ((n, QKV + VALS + LANES), f32)),
    ("act", lambda n, d, f: ((n, QKV), f32)),
    ("cum", lambda n, d, f: ((n, LANES), f32)),
    ("cum_t", lambda n, d, f: ((LANES, n), f32)),
    ("tinv", lambda n, d, f: ((HEADS, n, n), f32)),
    ("fresh", lambda n, d, f: ((n, VALS), f32)),
    ("heads", lambda n, d, f: ((n, VALS), f32)),
    ("mixed_t", lambda n, d, f: ((VALS, n), bf16)),
    ("middle", lambda n, d, f: ((n, d), f32)),
    ("normed_mid_t", lambda n, d, f: ((d, 2 * n), bf16)),
    ("hidden_t", lambda n, d, f: ((f // 2, 2 * n), bf16)),
    ("grads_gu", lambda n, d, f: ((2 * n, f), bf16)),
    ("pick", lambda n, d, f: ((n, n), bf16)),
    ("place", lambda n, d, f: ((n, n), bf16)),
    ("params", lambda n, d, f: ((16, d), f32)),
    ("taps", lambda n, d, f: ((4, QKV), f32)),
)


def transposed(a):
    return a.T.astype(bf16)


def forward_kernel(n_shard, reps, *refs):
    take = iter(refs)
    get = lambda k: [next(take) for _ in range(k)]
    offs, lens, tokens, cot, deal, small_in, rate, bias = get(8)
    wq, wk, wv, wt, wb, wo, wg, wu, wd = get(9)
    gp, go, gg, gu, gd = get(5)
    outs = dict(zip([name for name, _ in FORWARD_SAVED], get(len(FORWARD_SAVED))))
    kept = dict(zip([name for name, _ in FORWARD_SAVED], get(len(FORWARD_SAVED))))
    (dealt, dsend, drecv, smalls, ssend, srecv, sent, come, tsend, trecv, wbuf, wobuf, wdbuf, load_sem, fsend, frecv,
     mine_sem, out_sem, normed, mixed, normed_mid) = get(21)
    shards, shard_sem, zsend, zrecv = get(9), *get(3)
    own_loads = []
    for k, (w, v) in enumerate(zip((wq, wk, wv, wt, wb, wo, wd, wg, wu), shards)):
        own_loads.append(pltpu.make_async_copy(w, v, shard_sem.at[k]))
        own_loads[-1].start()
    wq, wk, wv, wt, wb, wo, wd, wg, wu = shards
    rows, width = tokens.shape
    per = rows // n_shard
    place = Place(n_shard, reps)
    p = place
    greet(place, True)
    offsets = [offs[i] for i in range(offs.shape[0])]
    lengths = [lens[i] for i in range(lens.shape[0])]
    store = Store(out_sem)

    dealt[p.s] = deal[...]
    smalls[p.s] = small_in[...]
    first = []
    for d in range(1, n_shard):
        to = (p.r, (p.s + d) % n_shard)
        first.append(remote(dealt.at[p.s], dealt.at[p.s], dsend.at[d], drecv.at[d], to))
        first[-1].start()
    for d in range(1, n_shard):
        to = (p.r, (p.s + d) % n_shard)
        first.append(remote(smalls.at[p.s], smalls.at[p.s], ssend.at[d], srecv.at[d], to))
        first[-1].start()

    made = []

    def flow(src, at, cols, dst, dst_at, pair):
        k = len(made)
        base = sum(Flow.count(p.ys, f.pair) for f in made)
        made.append(Flow(place, src, at, cols, dst, dst_at, pair, fsend, frecv, base, mine_sem.at[k]))
        return made[-1]

    ff = wg.shape[1]
    half = ff // 2
    ff_cuts = cuts(half, FF_TILE)
    stages = [
        [flow(wq, 0, KEYS, gp, 0, True), flow(wk, 0, KEYS, gp, KEYS, True), flow(wb, 0, LANES, gp, QKV + VALS, False)],
        [flow(wv, 0, VALS, gp, 2 * KEYS, True)],
        [flow(wt, 0, VALS, gp, QKV, False)],
        [flow(wo, 0, width, go, 0, True)],
        [flow(wd, 0, width // 2, gd, 0, False)],
        [flow(wd, width // 2, width // 2, gd, width // 2, False)],
    ]
    for at, cols in ff_cuts:
        stages.append([flow(wg, p.half * half + at, cols, gg, at, False), flow(wu, p.half * half + at, cols, gu, at, False)])
    last = len(stages) - 1

    events = []
    for k in range(len(stages) + 5):
        for lag, act in ((0, "begin"), (2, "forward"), (3, "relay"), (4, "swap"), (5, "done")):
            if 0 <= k - lag < len(stages):
                events.append((act, k - lag))
    owned = set()

    def poll(count=1):
        for _ in range(count):
            if events:
                act, k = events.pop(0)
                for f in stages[k]:
                    if act == "begin" and id(f.src_ref) not in owned:
                        owned.add(id(f.src_ref))
                        own_loads[[id(v) for v in shards].index(id(f.src_ref))].wait()
                    getattr(f, act)()

    def until(act, k):
        while (act, k) in events:
            poll()

    until("begin", 1)

    loads = {}

    def load(name, src, dst):
        loads[name] = pltpu.make_async_copy(src, dst, load_sem.at[len(loads)])
        loads[name].start()

    for c in first[: n_shard - 1]:
        c.wait_recv()
    i = lax.broadcasted_iota(jnp.int32, (rows, rows), 0)
    j = lax.broadcasted_iota(jnp.int32, (rows, rows), 1)
    upper = (i <= j).astype(bf16)
    everyone = dealt[:, 0, :]
    to_me = (everyone // rows) == p.s
    rank = dot(to_me.astype(f32).astype(bf16), upper).astype(jnp.int32) - 1
    rank = jnp.where(to_me, rank, -1)
    for b in range(n_shard):
        picked = one_hot_rows(rank[b : b + 1, :], per).astype(f32).astype(bf16)
        which = one_hot_rows(everyone[b : b + 1, :] % rows, rows).astype(f32).astype(bf16)
        kept["pick"][b * per : (b + 1) * per, :] = dot(picked, which, 1, 1).astype(bf16)
    pick = kept["pick"][...]
    exchange = []
    here = pl.ds(pl.multiple_of(p.s * per, 16), per)

    def pack(a, src):
        for at in range(0, width, 256):
            sent[a, :, at : at + 256] = dot(pick, src[:, at : at + 256]).astype(bf16)
        for d in range(1, n_shard):
            t = (p.s + d) % n_shard
            exchange.append(
                remote(
                    sent.at[a, pl.ds(pl.multiple_of(t * per, 16), per)], come.at[a, here],
                    tsend.at[a, d], trecv.at[a, d], (p.r, t),
                )
            )
            exchange[-1].start()
        come[a, here, :] = sent[a, here, :]

    def unpack(a, name):
        for c in exchange[a * (n_shard - 1) : (a + 1) * (n_shard - 1)]:
            c.wait_recv()
        for at in range(0, width, 256):
            kept[name][0:rows, at : at + 256] = dot(kept["place"][...], come[a, :, at : at + 256], 0, 0).astype(bf16)

    def swap_rows(ref, k):
        c = remote(ref.at[pl.ds(0, rows)], ref.at[pl.ds(rows, rows)], zsend.at[k], zrecv.at[k], p.partner())
        c.start()
        return c

    pack(0, tokens)
    poll(2)
    mine = deal[0:1, :]
    source = mine // rows
    from_each = one_hot_rows(source, n_shard)
    cum = dot(from_each.astype(f32).astype(bf16), upper)
    slot = jnp.sum(jnp.where(from_each, cum, 0.0), axis=0, keepdims=True).astype(jnp.int32) - 1 + source * per
    kept["place"][...] = one_hot_rows(slot, rows).astype(f32).astype(bf16)
    store.put(kept["pick"], outs["pick"])
    store.put(kept["place"], outs["place"])

    for c in first[n_shard - 1 :]:
        c.wait_recv()
    total = smalls[0].astype(f32)
    for t in range(1, n_shard):
        total = total + smalls[t].astype(f32)
    kept["params"][...] = total
    for t in range(4):
        for g in range(QKV // width):
            row = t * (QKV // width) + g
            kept["taps"][t : t + 1, g * width : (g + 1) * width] = total[row : row + 1, :]
    gain1, gain2 = kept["params"].at[12:13, :], kept["params"].at[13:14, :]
    gain_o = kept["params"].at[14:15, 0:DVH]
    store.put(kept["params"], outs["params"])
    store.put(kept["taps"], outs["taps"])

    unpack(0, "xin")
    store.put(kept["xin"], outs["xin"])
    x = kept["xin"][...].astype(f32)
    norm = x * lax.rsqrt(jnp.mean(x * x, axis=1, keepdims=True) + 1e-5) * gain1[...]
    normed[...] = norm.astype(bf16)
    pack(1, cot)

    def project(at, cols, tile):
        def step(k, carry):
            here = pl.ds(pl.multiple_of(at + k * tile, 128), tile)
            kept["lin"][:, here] = dot(normed[...], wbuf[:, here])
            return carry

        lax.fori_loop(0, cols // tile, step, 0)

    def fetch(name, at, cols):
        here = pl.ds(at, cols)
        load(name, gp.at[:, here], wbuf.at[:, here])

    until("done", 0)
    fetch("qk", 0, 2 * KEYS)
    fetch("bd", QKV + VALS, LANES)
    until("done", 1)
    fetch("v", 2 * KEYS, VALS)
    loads["qk"].wait()
    loads["bd"].wait()
    project(0, 2 * KEYS, 256)
    project(QKV + VALS, LANES, LANES)
    poll(1)
    loads["v"].wait()
    project(2 * KEYS, VALS, 256)
    until("done", 2)
    fetch("gate", QKV, VALS)
    convolve, heads = mixer_forward(
        rows, offsets, lengths, kept["lin"], kept["taps"], rate, bias, gain_o, kept["act"], kept["cum"],
        kept["cum_t"], kept["tinv"], kept["fresh"], kept["heads"], mixed,
    )
    convolve()
    poll(2)
    unpack(1, "dy")
    dy_swap = swap_rows(kept["dy"], 0)
    loads["gate"].wait()
    project(QKV, VALS, 256)
    store.put(kept["lin"], outs["lin"])
    for h in range(0, HEADS, 2):
        heads[h]()
        heads[h + 1]()
        poll(6)
    until("done", 3)
    load("out", go, wobuf)
    for name in ("act", "cum", "cum_t", "tinv", "fresh", "heads"):
        store.put(kept[name], outs[name])
    loads["out"].wait()

    def out_step(k, carry):
        here = pl.ds(pl.multiple_of(k * 256, 256), 256)
        kept["middle"][:, here] = kept["xin"][:, here].astype(f32) + dot(mixed[...], wobuf[:, here])
        return carry

    lax.fori_loop(0, width // 256, out_step, 0)
    store.put(kept["middle"], outs["middle"])
    m = kept["middle"][...]
    norm = m * lax.rsqrt(jnp.mean(m * m, axis=1, keepdims=True) + 1e-5) * gain2[...]
    normed_mid[0:rows, :] = norm.astype(bf16)
    mid_swap = swap_rows(normed_mid, 1)
    kept["normed_mid_t"][:, 0:rows] = transposed(norm)
    kept["mixed_t"][...] = transposed(mixed[...].astype(f32))
    store.put(kept["mixed_t"], outs["mixed_t"])
    until("done", 5)
    load("down", gd.at[pl.ds(pl.multiple_of(p.half * half, LANES), half)], wdbuf)

    def ffn(k, at, cols):
        some = slice(k * rows, (k + 1) * rows)
        here, there = slice(at, at + cols), slice(half + at, half + at + cols)
        grad = dot(kept["dy"][some, :], wdbuf[here, :], 1, 1)
        gate = dot(normed_mid[some, :], wbuf[:, here])
        up = dot(normed_mid[some, :], wbuf[:, there])
        sg = sigm(gate)
        silu = gate * sg
        hid = silu * up
        kept["hidden_t"][here, some] = transposed(hid)
        kept["grads_gu"][some, here] = (grad * up * (sg + silu * (1.0 - sg))).astype(bf16)
        kept["grads_gu"][some, there] = (grad * silu).astype(bf16)

    loads["down"].wait()
    for i, (at, cols) in enumerate(ff_cuts):
        until("done", last - len(ff_cuts) + 1 + i)
        load(("g", i), gg.at[:, pl.ds(at, cols)], wbuf.at[:, pl.ds(at, cols)])
        load(("u", i), gu.at[:, pl.ds(at, cols)], wbuf.at[:, pl.ds(half + at, cols)])
        poll(2)
        loads[("g", i)].wait()
        loads[("u", i)].wait()
        ffn(0, at, cols)
    kept["normed_t"][...] = transposed(normed[...].astype(f32))
    store.put(kept["normed_t"], outs["normed_t"])
    dy_swap.wait()
    mid_swap.wait()
    store.put(kept["dy"], outs["dy"])
    for at, cols in ff_cuts:
        ffn(1, at, cols)
    kept["normed_mid_t"][:, rows : 2 * rows] = transposed(normed_mid[rows : 2 * rows, :].astype(f32))
    store.put(kept["normed_mid_t"], outs["normed_mid_t"])
    for name in ("hidden_t", "grads_gu"):
        store.put(kept[name], outs[name])
    for c in first + exchange:
        c.wait_send()
    for f in made:
        f.close()
    store.wait()


def forward_call(n_shard, reps, offs, lens, tokens, cot, deal, small_in, rate, bias, weights):
    anywhere = pl.BlockSpec(memory_space=pl.ANY)
    held = pl.BlockSpec(memory_space=pltpu.VMEM)
    words = pl.BlockSpec(memory_space=pltpu.SMEM)
    rows, width = tokens.shape
    ff = weights[6].shape[1]
    sd = jax.ShapeDtypeStruct
    wide = QKV + VALS + LANES
    vals_rows, ff_rows = weights[5].shape[0] * n_shard, weights[8].shape[0] * n_shard
    gathered = [
        sd((width, wide), bf16), sd((vals_rows, width), bf16), sd((width, ff // 2), bf16), sd((width, ff // 2), bf16),
        sd((ff_rows, width), bf16),
    ]
    shapes = [fn(rows, width, ff) for _, fn in FORWARD_SAVED]
    sems = pltpu.SemaphoreType.DMA
    flows = 8 + 2 * len(cuts(ff // 2, FF_TILE))
    count = flows * Flow.count(n_shard // 4, True)
    scratch = [pltpu.VMEM(s, d) for s, d in shapes] + [
        pltpu.VMEM((n_shard, 8, rows), jnp.int32), sems((n_shard,)), sems((n_shard,)),
        pltpu.VMEM((n_shard, 16, width), bf16), sems((n_shard,)), sems((n_shard,)),
        pltpu.VMEM((2, rows, width), bf16), pltpu.VMEM((2, rows, width), bf16), sems((2, n_shard)), sems((2, n_shard)),
        pltpu.VMEM((width, wide), bf16), pltpu.VMEM((vals_rows, width), bf16), pltpu.VMEM((ff_rows // 2, width), bf16),
        sems((16,)), sems((count,)), sems((count,)), sems((flows,)), sems((len(shapes),)),
        pltpu.VMEM((rows, width), bf16), pltpu.VMEM((rows, VALS), bf16), pltpu.VMEM((2 * rows, width), bf16),
    ]
    scratch += [pltpu.VMEM(weights[k].shape, bf16) for k in (0, 1, 2, 3, 4, 5, 8, 6, 7)] + [sems((9,)), sems((2,)), sems((2,))]
    res = pl.pallas_call(
        functools.partial(forward_kernel, n_shard, reps),
        in_specs=[words, words] + [held] * 6 + [anywhere] * 9,
        out_specs=[anywhere] * (5 + len(shapes)),
        out_shape=gathered + [sd(s, d) for s, d in shapes],
        scratch_shapes=scratch,
        compiler_params=pltpu.CompilerParams(collective_id=1, has_side_effects=True, vmem_limit_bytes=62 << 20),
    )(offs, lens, tokens, cot, deal, small_in, rate, bias, *weights)
    return res[:5], dict(zip([name for name, _ in FORWARD_SAVED], res[5:]))


WIDE = 512
PIECE = 256


class Stream:
    def __init__(self, buf, sem, parts):
        self.buf, self.sem, self.parts, self.at = buf, sem, parts, 0
        self.copies = {}

    def start(self):
        self.issue(0)

    def issue(self, k):
        if k < len(self.parts):
            pairs = self.parts[k](self.buf.at[k % 2])
            self.copies[k] = [pltpu.make_async_copy(s, d, self.sem.at[k % 2, i]) for i, (s, d) in enumerate(pairs)]
            for c in self.copies[k]:
                c.start()

    def take(self):
        k = self.at
        self.at += 1
        self.issue(k + 1)
        for c in self.copies[k]:
            c.wait()
        return k, self.buf.at[k % 2]


BACK_KEPT = tuple(name for name, _ in FORWARD_SAVED)


def backward_kernel(n_shard, reps, rings, small, *refs):
    take = iter(refs)
    get = lambda k: [next(take) for _ in range(k)]
    offs, lens, rate, bias = get(4)
    gp, go, gg, gu, gd = get(5)
    given = dict(zip(BACK_KEPT, get(len(BACK_KEPT))))
    o_rows, o_grad, o_ffn, o_down, o_out, o_proj, o_small = get(7)
    kept = dict(zip(BACK_KEPT, get(len(BACK_KEPT))))
    (ring,) = rings
    ring.bind(get(10))
    small.bind(get(3))
    (load_sem, wbuf, wsem, nbuf, nsem, acc, middle_grad, branch, mix_grad, dcols, drows, lin_grad, tap_grad, gain_grad,
     rate_grad, bias_grad, small_v, sent, come, tsend, trecv, rows_out, out_sem, swaps, zsend, zrecv, block) = get(27)
    rows, width = kept["xin"].shape
    half = gg.shape[1]
    ff = 2 * half
    per = rows // n_shard
    place = Place(n_shard, reps)
    p = place
    offsets = [offs[i] for i in range(offs.shape[0])]
    lengths = [lens[i] for i in range(lens.shape[0])]
    loads = {}
    order = (
        "normed_mid_t", "grads_gu", "middle", "dy", "params", "hidden_t", "cum", "cum_t", "tinv", "fresh", "heads",
        "act", "lin", "taps", "mixed_t", "normed_t", "xin", "pick", "place",
    )
    for k, name in enumerate(order):
        loads[name] = pltpu.make_async_copy(given[name], kept[name], load_sem.at[k])
        loads[name].start()
    have = set()

    def need(*names):
        for name in names:
            if name not in have:
                have.add(name)
                loads[name].wait()

    greet(place, True)
    pieces = []

    def tick(piece=None, fill=None):
        index = tick.index
        tick.index += 1
        pump(pieces, index)
        if piece is not None:
            pieces.append(piece())
            fill(pieces[-1])
            pieces[-1].send_core()

    tick.index = 0

    size = width // n_shard

    def wide_piece(left, right, right_at, cols, out, out_at):
        def fill(piece):
            value = dot(left[...], right[:, right_at : right_at + cols]).astype(bf16)
            ring.own[piece.slot, :, :, :, :, 0:cols] = value.reshape(ring.ys, 2, 2, size, cols)

        tick(lambda: Piece(ring, place, size, cols, out, out_at), fill)

    def block_piece(left, right, at, cols, first, count, out):
        total = left.shape[0]
        long = out.shape[0]
        held = total // long
        ys = held // 4

        def fill(piece):
            if first == 0:
                block[0:total, 0:cols] = dot(left[...], right[:, at : at + cols]).astype(bf16)
            for t in range(held):
                y = t // 4 if held == n_shard else p.half * ys + t // 4
                part = block[t * long + first : t * long + first + count, 0:cols]
                ring.own[piece.slot, y, (t // 2) % 2, t % 2, 0:count, 0:cols] = part
            if held < n_shard:
                for t in range(held):
                    y = (1 - p.half) * ys + t // 4
                    ring.own[piece.slot, y, (t // 2) % 2, t % 2, 0:count, 0:cols] = jnp.zeros((count, cols), bf16)

        tick(lambda: Piece(ring, place, count, cols, out.at[pl.ds(first, count)], (at,)), fill)

    queue = []

    def run(count=1):
        for _ in range(count):
            queue.pop(0)()

    gu_cuts = [(side, at, cols) for side in (0, 1) for at, cols in cuts(half, WIDE)]

    def gu_piece(side, at, cols):
        need("normed_mid_t", "grads_gu")
        outs = (side * ff + at, side * ff + half + at)
        wide_piece(kept["normed_mid_t"], kept["grads_gu"], side * half + at, cols, o_ffn, outs)

    def down_piece(at, first, count):
        need("hidden_t", "dy")
        block_piece(kept["hidden_t"], kept["dy"], at, PIECE, first, count, o_down)

    def out_piece(at, first, count):
        need("mixed_t")
        block_piece(kept["mixed_t"], branch, at, PIECE, first, count, o_out)

    def proj_piece(at, cols):
        need("normed_t")
        wide_piece(kept["normed_t"], lin_grad, at, cols, o_proj, (at,))

    def blocks(fn, out):
        return [
            functools.partial(fn, at, first, count) for at, _ in cuts(width, PIECE) for first, count in cuts(out.shape[0], size)
        ]

    sided = [functools.partial(gu_piece, side, at, cols) for side in (0, 1) for at, cols in cuts(half, PIECE)]
    downs = blocks(down_piece, o_down)
    while sided or downs:
        queue.extend(sided[:1] + downs[:1])
        del sided[:1], downs[:1]
    queue.extend(blocks(out_piece, o_out))
    wide = cuts(QKV + VALS, PIECE)
    late = QKV // PIECE
    for at, cols in wide[late:] + wide[:late] + [(QKV + VALS, LANES)]:
        queue.append(functools.partial(proj_piece, at, cols))

    def gu_part(k):
        side, at, cols = gu_cuts[k]
        return lambda b: [((gg, gu)[side].at[:, pl.ds(at, cols)], b.at[:, pl.ds(0, cols)])]

    gu_stream = Stream(wbuf, wsem, [gu_part(k) for k in range(len(gu_cuts))])

    def gnm(count):
        need("grads_gu")
        for _ in range(count):
            k, buf = gu_stream.take()
            side, at, cols = gu_cuts[k]
            at = side * half + at
            part = dot(kept["grads_gu"][:, at : at + cols], buf[:, 0:cols], 1, 1)
            acc[...] = part if k == 0 else acc[...] + part

    def to_partner(k):
        swaps[0] = acc[rows : 2 * rows, :].astype(bf16)
        c = remote(swaps.at[0], swaps.at[1 + k], zsend.at[k], zrecv.at[k], p.partner())
        c.start()
        return c

    def norm_back(values, gain, upstream):
        n = lax.rsqrt(jnp.mean(values * values, axis=1, keepdims=True) + 1e-5)
        u = upstream * gain
        gain_part = jnp.sum(upstream * values * n, axis=0, keepdims=True)
        return n * (u - values * (n * n) * jnp.mean(u * values, axis=1, keepdims=True)), gain_part

    def norm2():
        need("middle", "dy", "params")
        mid_swap.wait()
        upstream = acc[0:rows, :] + swaps[1].astype(f32)
        back, gain_part = norm_back(kept["middle"][...], kept["params"][13:14, :], upstream)
        small_v[13:14, :] = gain_part
        total = kept["dy"][0:rows, :].astype(f32) + back
        middle_grad[...] = total
        branch[...] = total.astype(bf16)

    def row_part(src, k):
        return lambda b: [(src.at[pl.ds(k * FTILE, FTILE), :], b)]

    out_stream = Stream(nbuf, nsem, [row_part(go, k) for k in range(VALS // FTILE)])
    down_cuts = cuts(half, FTILE)

    def down_part(at, size):
        start = pl.multiple_of(p.half * half + at, LANES)
        return lambda b: [(gd.at[pl.ds(start, size), :], b.at[pl.ds(0, size)])]

    down_stream = Stream(nbuf, nsem, [down_part(at, size) for at, size in down_cuts])

    def grad_mixed(count):
        for _ in range(count):
            k, buf = out_stream.take()
            mix_grad[:, k * FTILE : (k + 1) * FTILE] = dot(branch[...], buf[...], 1, 1)

    def result(count):
        need("hidden_t", "middle")
        for _ in range(count):
            k, buf = down_stream.take()
            at, size = down_cuts[k]
            part = dot(kept["hidden_t"][at : at + size, :], buf[0:size, :], 0, 0)
            acc[...] = part if k == 0 else acc[...] + part

    exchange = {}

    def send_home(a, value):
        need("place")
        here = pl.ds(pl.multiple_of(p.s * per, 16), per)
        for at in range(0, width, 256):
            sent[a, :, at : at + 256] = dot(kept["place"][...], value[:, at : at + 256]).astype(bf16)
        exchange[a] = []
        for d in range(1, n_shard):
            t = (p.s + d) % n_shard
            exchange[a].append(
                remote(
                    sent.at[a, pl.ds(pl.multiple_of(t * per, 16), per)], come.at[a, here],
                    tsend.at[a, d], trecv.at[a, d], (p.r, t),
                )
            )
            exchange[a][-1].start()
        come[a, here, :] = sent[a, here, :]

    stores = []

    def arrive(a, out):
        need("pick")
        for c in exchange[a]:
            c.wait()
        for at in range(0, width, 256):
            rows_out[a, :, at : at + 256] = dot(kept["pick"][...], come[a, :, at : at + 256], 0, 0).astype(bf16)
        stores.append(pltpu.make_async_copy(rows_out.at[a], out, out_sem.at[a]))
        stores[-1].start()

    def wide_part(at, cols):
        return lambda b: [(gp.at[:, pl.ds(at, cols)], b.at[:, pl.ds(0, cols)])]

    proj_cuts = [(at, WIDE) for at in range(0, QKV + VALS, WIDE)] + [(QKV + VALS, LANES)]
    proj_stream = Stream(wbuf, wsem, [wide_part(at, cols) for at, cols in proj_cuts])

    def grad_normed(count):
        for _ in range(count):
            k, buf = proj_stream.take()
            at, cols = proj_cuts[k]
            part = dot(lin_grad[:, at : at + cols], buf[:, 0:cols], 1, 1)
            acc[0:rows, :] = part if k == 0 else acc[0:rows, :] + part

    def norm1():
        need("xin")
        back, gain_part = norm_back(kept["xin"][...].astype(f32), kept["params"][12:13, :], acc[0:rows, :])
        small_v[12:13, :] = gain_part
        rows_out[1] = (middle_grad[...] + back).astype(bf16)

    def pack_small():
        small_v[14:16, :] = jnp.zeros((2, width), f32)
        for t in range(4):
            for g in range(QKV // width):
                row = t * (QKV // width) + g
                small_v[row : row + 1, :] = tap_grad[t : t + 1, g * width : (g + 1) * width]
        small_v[14:15, 0:DVH] = gain_grad[...]
        small_v[14:15, DVH : DVH + LANES] = rate_grad[...]
        small_v[14:15, DVH + LANES : DVH + 2 * LANES] = bias_grad[...]

    gu_stream.start()
    out_stream.start()
    for _ in gu_cuts:
        run()
        gnm(1)
    mid_swap = to_partner(0)
    run(6)
    need("cum", "cum_t", "tinv", "fresh", "heads", "act", "lin", "taps")
    clear, heads, rates, convs = mixer_backward(
        rows, offsets, lengths, kept["lin"], kept["taps"], rate, bias, kept["params"].at[14:15, 0:DVH], kept["act"],
        kept["cum"], kept["cum_t"], kept["tinv"], kept["fresh"], kept["heads"], mix_grad,
        kept["act"], dcols, drows, lin_grad, tap_grad, gain_grad, rate_grad, bias_grad,
    )
    clear()
    norm2()
    run()
    grad_mixed(3)
    run()
    grad_mixed(3)
    down_stream.start()
    for h in range(0, HEADS, 2):
        run(4)
        heads[h]()
        heads[h + 1]()
    for step in [rates] + convs:
        run()
        step()
    while len(queue) > len(wide) + 1:
        run()
    result(3)
    run()
    result(len(down_cuts) - 3)
    result_swap = to_partner(1)
    proj_stream.start()
    run(4)
    result_swap.wait()
    rows_out[0] = (kept["middle"][...] + acc[0:rows, :] + swaps[2].astype(f32)).astype(bf16)
    send_home(0, rows_out.at[0])
    run()
    for count in (3, 3, len(proj_cuts) - 6):
        grad_normed(count)
        run()
    norm1()
    send_home(1, rows_out.at[1])
    pack_small()
    value = small_v[...]
    for k in range(4):
        small.begin(place, k, value)
        run()
        value = small.end(k)
    arrive(0, o_rows)
    run()
    arrive(1, o_grad)
    run(len(queue))
    for _ in range(18):
        tick()
    o_small[...] = value
    for c in stores:
        c.wait()


def backward_call(n_shard, reps, offs, lens, rate, bias, gathered, saved):
    anywhere = pl.BlockSpec(memory_space=pl.ANY)
    held = pl.BlockSpec(memory_space=pltpu.VMEM)
    words = pl.BlockSpec(memory_space=pltpu.SMEM)
    rows, width = saved["xin"].shape
    ff = 2 * gathered[2].shape[1]
    sd = jax.ShapeDtypeStruct
    wide = QKV + VALS + LANES
    sems = pltpu.SemaphoreType.DMA
    rings = (Ring(n_shard, width // n_shard, PIECE, 2),)
    small = Small(n_shard, reps, 16, width)
    outs = [
        sd((rows, width), bf16), sd((rows, width), bf16), sd((width // n_shard, 2 * ff), bf16),
        sd((ff // n_shard, width), bf16), sd((VALS // n_shard, width), bf16), sd((width // n_shard, wide), bf16),
        sd((16, width), f32),
    ]
    vmem = pltpu.VMEM
    scratch = [vmem(saved[name].shape, saved[name].dtype) for name in BACK_KEPT]
    scratch += rings[0].scratch() + small.scratch()
    scratch += [
        sems((len(BACK_KEPT),)), vmem((2, width, WIDE), bf16), sems((2, 2)), vmem((2, FTILE, width), bf16), sems((2, 1)),
        vmem((2 * rows, width), f32), vmem((rows, width), f32), vmem((rows, width), bf16), vmem((rows, VALS), f32),
        vmem((rows, LANES), f32), vmem((LANES, rows), f32), vmem((rows, wide), bf16), vmem((4, QKV), f32),
        vmem((1, DVH), f32), vmem((1, LANES), f32), vmem((1, LANES), f32), vmem((16, width), f32),
        vmem((2, rows, width), bf16), vmem((2, rows, width), bf16), sems((2, n_shard)), sems((2, n_shard)),
        vmem((2, rows, width), bf16), sems((2,)), vmem((3, rows, width), bf16), sems((2,)), sems((2,)),
        vmem((max(VALS, ff // 2), PIECE), bf16),
    ]
    return pl.pallas_call(
        functools.partial(backward_kernel, n_shard, reps, rings, small),
        in_specs=[words, words, held, held] + [anywhere] * (5 + len(BACK_KEPT)),
        out_specs=[anywhere] * 6 + [held],
        out_shape=outs,
        scratch_shapes=scratch,
        compiler_params=pltpu.CompilerParams(collective_id=0, has_side_effects=True, vmem_limit_bytes=63 << 20),
    )(offs, lens, rate, bias, *gathered, *[saved[name] for name in BACK_KEPT])


def local(
    reps, tokens, cotangent, deal, offsets, lengths, norm1_gain, q_weight, k_weight, v_weight, conv_weight,
    beta_weight, decay_weight, log_rate, step_bias, out_gate_weight, out_norm_gain, out_weight, norm2_gain,
    ffn_gate, ffn_up, ffn_down,
):
    rows, width = tokens.shape
    n = lax.axis_size("shard")
    s = lax.axis_index("shard")
    pad = LANES - 2 * HEADS
    bd_weight = jnp.concatenate([beta_weight, decay_weight, jnp.zeros((beta_weight.shape[0], pad), bf16)], axis=1)
    lanes = lambda a: jnp.pad(a, (HEADS, LANES - 2 * HEADS))[None, :]
    rate, bias = lanes(log_rate), lanes(step_bias)

    def spread(vector):
        size = vector.shape[0]
        wide = lax.dynamic_update_slice(jnp.zeros((size * n,), bf16), vector, (s * size,))
        return jnp.pad(wide, (0, width - size * n))[None]

    taps = lax.dynamic_update_slice(jnp.zeros((4, QKV), bf16), conv_weight, (0, s * conv_weight.shape[1]))
    small_in = jnp.concatenate(
        [taps.reshape(-1, width), spread(norm1_gain), spread(norm2_gain), spread(out_norm_gain), jnp.zeros((1, width), bf16)]
    )
    weights = (q_weight, k_weight, v_weight, out_gate_weight, bd_weight, out_weight, ffn_gate, ffn_up, ffn_down)
    deals = jnp.broadcast_to(deal[None, :], (8, rows))
    gathered, saved = forward_call(
        n, reps, offsets[0], lengths[0], tokens, cotangent, deals, small_in, rate, bias, weights
    )
    home_rows, home_grad, s_ffn, s_down, s_out, s_proj, small = backward_call(
        n, reps, offsets[0], lengths[0], rate, bias, gathered, saved
    )

    def part(a, dim=0):
        size = a.shape[dim] // n
        return lax.dynamic_slice_in_dim(a, s * size, size, dim)

    f = lambda a: a.astype(f32)
    ff = ffn_gate.shape[1]
    at = QKV + VALS
    return (
        home_rows, home_grad, part(small[12]), f(s_proj[:, :KEYS]), f(s_proj[:, KEYS : 2 * KEYS]),
        f(s_proj[:, 2 * KEYS : QKV]), part(small[:12].reshape(4, QKV), 1), f(s_proj[:, at : at + HEADS]),
        f(s_proj[:, at + HEADS : at + 2 * HEADS]), small[14, DVH + HEADS : DVH + 2 * HEADS],
        small[14, DVH + LANES + HEADS : DVH + LANES + 2 * HEADS], f(s_proj[:, QKV:at]), part(small[14, :DVH]),
        f(s_out), part(small[13]), f(s_ffn[:, :ff]), f(s_ffn[:, ff:]), f(s_down),
    )


def solution(mesh):
    rows2, shard0 = P(("rep", "shard"), None), P("shard", None)
    vec = P("shard")
    in_specs = (
        rows2, rows2, P(("rep", "shard")), rows2, rows2, vec, shard0, shard0, shard0, P(None, "shard"),
        shard0, shard0, P(), P(), shard0, vec, shard0, vec, shard0, shard0, shard0,
    )
    out_specs = (
        rows2, rows2, vec, shard0, shard0, shard0, P(None, "shard"), shard0, shard0, P(), P(), shard0,
        vec, shard0, vec, shard0, shard0, shard0,
    )
    body = functools.partial(local, mesh.shape["rep"])
    return jax.shard_map(body, mesh=mesh, in_specs=in_specs, out_specs=out_specs, check_vma=False)
```

```python
import functools
import jax
import jax.numpy as jnp
from jax import lax
from jax.experimental import pallas as pl
from jax.experimental.pallas import tpu as pltpu
from jax.sharding import PartitionSpec as P

f32 = jnp.float32
bf16 = jnp.bfloat16
HEADS = 6
DK = 128
DVH = 256
KEYS = 768
VALS = 1536
QKV = 2 * KEYS + VALS
LANES = 128


def two_parts(a):
    hi = a.astype(bf16)
    return hi, (a - hi.astype(f32)).astype(bf16)


def dot(a, b, ca=1, cb=0):
    return lax.dot_general(a, b, (((ca,), (cb,)), ((), ())), preferred_element_type=f32)


def dot3(a, b, ca=1, cb=0):
    ah, al = a
    bh, bl = b
    return dot(ah, bh, ca, cb) + (dot(ah, bl, ca, cb) + dot(al, bh, ca, cb))


def tri_dot(tri, cols):
    hi = cols.astype(bf16)
    rest = cols - hi.astype(f32)
    mid = rest.astype(bf16)
    lo = (rest - mid.astype(f32)).astype(bf16)
    return dot(tri, hi) + (dot(tri, mid) + dot(tri, lo))


def sigm(a):
    return 1.0 / (1.0 + jnp.exp(-a))


def softplus(a):
    return jnp.maximum(a, 0.0) + jnp.log1p(jnp.exp(-jnp.abs(a)))


def layout_cols(offs, lens, n, shape, dim):
    row = lax.broadcasted_iota(jnp.int32, shape, dim)
    begin = jnp.zeros_like(row)
    extent = jnp.zeros_like(row)
    for i in range(len(offs)):
        inside = row >= offs[i]
        begin = jnp.where(inside, offs[i], begin)
        extent = jnp.where(inside, lens[i], extent)
    return begin, row - begin, (row - begin) < extent


def conv_chunk(x, taps, pos, cols):
    total = taps[0:1, cols] * x
    for t in range(1, 4):
        total = total + taps[t : t + 1, cols] * jnp.where(pos >= t, pltpu.roll(x, t, 0), 0.0)
    return total


def lane_pick(a, lane, index):
    return jnp.sum(jnp.where(lane == index, a, 0.0), axis=1, keepdims=True)


def pair_masks(n, begin_c, begin_r):
    i = lax.broadcasted_iota(jnp.int32, (n, n), 0)
    j = lax.broadcasted_iota(jnp.int32, (n, n), 1)
    same = begin_c == begin_r
    return i, j, (i >= j) & same


def mixer_forward(n, offs, lens, lin, taps, rate, bias, gain, act, cum, cum_t, tinv, fresh, heads_out, mixed):
    begin_c, pos, live = layout_cols(offs, lens, n, (n, 1), 0)
    begin_r, _, _ = layout_cols(offs, lens, n, (1, n), 1)
    live_f = live.astype(f32)
    width = 384

    def conv_step(step, carry):
        cols = pl.ds(pl.multiple_of(step * width, width), width)
        pre = conv_chunk(lin[:, cols], taps, pos, cols)
        act[:, cols] = pre * sigm(pre)
        return carry

    lane = lax.broadcasted_iota(jnp.int32, (n, LANES), 1)
    bd = lin[:, QKV + VALS : QKV + VALS + LANES]
    beta = sigm(bd) * live_f
    decay = -jnp.exp(rate[...]) * softplus(bd + bias[...]) * live_f
    i, j, low = pair_masks(n, begin_c, begin_r)
    eye = (i == j).astype(f32)

    def convolve():
        lax.fori_loop(0, QKV // width, conv_step, 0)
        total = tri_dot((i >= j).astype(bf16), decay)
        cum[...] = total
        cum_t[...] = total.T

    def one_head(h):
        kcols = pl.ds(pl.multiple_of(h * DK, DK), DK)
        ka = act[:, pl.ds(pl.multiple_of(KEYS + h * DK, DK), DK)]
        qa = act[:, kcols]
        vcols = pl.ds(pl.multiple_of(h * DVH, DVH), DVH)
        v = act[:, pl.ds(pl.multiple_of(2 * KEYS + h * DVH, DVH), DVH)]
        q = qa * (lax.rsqrt(jnp.sum(qa * qa, axis=1, keepdims=True) + 1e-6) * DK**-0.5)
        k = ka * lax.rsqrt(jnp.sum(ka * ka, axis=1, keepdims=True) + 1e-6)
        beta_c = lane_pick(beta, lane, h)
        cum_c = lane_pick(cum[...], lane, HEADS + h)
        cum_r = cum_t[pl.ds(HEADS + h, 1), :]
        kk, qq = two_parts(k), two_parts(q)
        dec = jnp.where(low, jnp.exp(jnp.where(low, cum_c - cum_r, 0.0)), 0.0)
        system = jnp.where(i > j, beta_c * dot3(kk, kk, 1, 1) * dec, 0.0)
        inv = eye - jnp.where((i // 2) == (j // 2), system, 0.0)
        size = 2
        while size < n:
            off = jnp.where(((i // (2 * size)) == (j // (2 * size))) & ((i // size) != (j // size)), system, 0.0)
            parts = two_parts(inv)
            inv = inv - dot3(two_parts(dot3(parts, two_parts(off))), parts)
            size *= 2
        tinv[h] = inv
        u = dot3(two_parts(inv), two_parts(beta_c * v))
        fresh[:, vcols] = u
        o = dot3(two_parts(dot3(qq, kk, 1, 1) * dec), two_parts(u)) * live_f
        heads_out[:, vcols] = o
        gate = lin[:, pl.ds(pl.multiple_of(QKV + h * DVH, DVH), DVH)]
        scaled = o * lax.rsqrt(jnp.mean(o * o, axis=1, keepdims=True) + 1e-5)
        mixed[:, vcols] = (scaled * gain[...] * (gate * sigm(gate))).astype(bf16)

    return convolve, [functools.partial(one_head, h) for h in range(HEADS)]


def mixer_backward(
    n, offs, lens, lin, taps, rate, bias, gain, act, cum, cum_t, tinv, fresh, heads_out, grad_mixed,
    dact, dcols, drows, lin_grad, tap_grad, gain_grad, rate_grad, bias_grad,
):
    begin_c, pos, live = layout_cols(offs, lens, n, (n, 1), 0)
    begin_r, _, _ = layout_cols(offs, lens, n, (1, n), 1)
    live_f = live.astype(f32)
    lane = lax.broadcasted_iota(jnp.int32, (n, LANES), 1)
    bd = lin[:, QKV + VALS : QKV + VALS + LANES]
    sig_b = sigm(bd)
    beta = sig_b * live_f
    i, j, low = pair_masks(n, begin_c, begin_r)
    strict = low & (i > j)

    def clear():
        gain_grad[...] = jnp.zeros_like(gain_grad)
        dcols[...] = jnp.zeros_like(dcols)
        drows[...] = jnp.zeros_like(drows)

    def one_head(h):
        kcols = pl.ds(pl.multiple_of(h * DK, DK), DK)
        kcols2 = pl.ds(pl.multiple_of(KEYS + h * DK, DK), DK)
        vcols = pl.ds(pl.multiple_of(h * DVH, DVH), DVH)
        vcols2 = pl.ds(pl.multiple_of(2 * KEYS + h * DVH, DVH), DVH)
        gcols = pl.ds(pl.multiple_of(QKV + h * DVH, DVH), DVH)
        ka = act[:, kcols2]
        qa = act[:, kcols]
        v = act[:, vcols2]
        o = heads_out[:, vcols]
        gate = lin[:, gcols]
        dm = grad_mixed[:, vcols]
        ro = lax.rsqrt(jnp.mean(o * o, axis=1, keepdims=True) + 1e-5)
        scaled = o * ro
        sg = sigm(gate)
        si = gate * sg
        gain_grad[...] += jnp.sum(dm * scaled * si, axis=0, keepdims=True)
        lin_grad[:, gcols] = (dm * scaled * gain[...] * (sg + si * (1.0 - sg))).astype(bf16)
        ds = dm * gain[...] * si
        d_o = two_parts(ro * (ds - scaled * jnp.mean(ds * scaled, axis=1, keepdims=True)) * live_f)
        rq = lax.rsqrt(jnp.sum(qa * qa, axis=1, keepdims=True) + 1e-6)
        rk = lax.rsqrt(jnp.sum(ka * ka, axis=1, keepdims=True) + 1e-6)
        qhat = qa * rq
        k = ka * rk
        kk, qq = two_parts(k), two_parts(qhat * DK**-0.5)
        beta_c = lane_pick(beta, lane, h)
        cum_c = lane_pick(cum[...], lane, HEADS + h)
        cum_r = cum_t[pl.ds(HEADS + h, 1), :]
        dec = jnp.where(low, jnp.exp(jnp.where(low, cum_c - cum_r, 0.0)), 0.0)
        gram = dot3(kk, kk, 1, 1)
        qk = dot3(qq, kk, 1, 1)
        uu = two_parts(fresh[:, vcols])
        du = dot3(two_parts(qk * dec), d_o, 0, 0)
        dp = dot3(d_o, uu, 1, 1) * dec
        db = dot3(two_parts(tinv[h]), two_parts(du), 0, 0)
        da = jnp.where(strict, -dot3(two_parts(db), uu, 1, 1), 0.0) * dec
        x = da * gram
        dbeta = jnp.sum(x, axis=1, keepdims=True) + jnp.sum(db * v, axis=1, keepdims=True)
        e = dp * qk + x * beta_c
        dcols[...] += jnp.where(lane == h, dbeta, 0.0) + jnp.where(
            lane == HEADS + h, jnp.sum(e, axis=1, keepdims=True), 0.0
        )
        drows[pl.ds(HEADS + h, 1), :] = jnp.sum(e, axis=0, keepdims=True)
        dact[:, vcols2] = beta_c * db
        dg = two_parts(da * beta_c)
        dpp = two_parts(dp)
        dq = dot3(dpp, kk)
        dk = dot3(dpp, qq, 0, 0) + dot3(dg, kk) + dot3(dg, kk, 0, 0)
        dact[:, kcols] = (rq * DK**-0.5) * (dq - qhat * jnp.sum(dq * qhat, axis=1, keepdims=True))
        dact[:, kcols2] = rk * (dk - k * jnp.sum(dk * k, axis=1, keepdims=True))

    def rates():
        dcum = jnp.where((lane >= HEADS) & (lane < 2 * HEADS), dcols[...] - drows[...].T, 0.0)
        ddecay = tri_dot((i <= j).astype(bf16), dcum)
        z = bd + bias[...]
        speed = -jnp.exp(rate[...]) * live_f
        dz = ddecay * speed * sigm(z)
        rate_grad[...] = jnp.sum(ddecay * speed * softplus(z), axis=0, keepdims=True)
        bias_grad[...] = jnp.sum(dz, axis=0, keepdims=True)
        dbeta_lin = dcols[...] * live_f * sig_b * (1.0 - sig_b)
        both = jnp.where(lane < HEADS, dbeta_lin, jnp.where(lane < 2 * HEADS, dz, 0.0))
        lin_grad[:, QKV + VALS : QKV + VALS + LANES] = both.astype(bf16)

    width = 384

    def conv_step(step, carry):
        cols = pl.ds(pl.multiple_of(step * width, width), width)
        x = lin[:, cols]
        pre = conv_chunk(x, taps, pos, cols)
        sg = sigm(pre)
        dc = dact[:, cols] * (sg + pre * sg * (1.0 - sg))
        dx = taps[0:1, cols] * dc
        tap_grad[0:1, cols] = jnp.sum(dc * x, axis=0, keepdims=True)
        for t in range(1, 4):
            masked = jnp.where(pos >= t, dc, 0.0)
            dx = dx + taps[t : t + 1, cols] * pltpu.roll(masked, n - t, 0)
            tap_grad[t : t + 1, cols] = jnp.sum(masked * pltpu.roll(x, t, 0), axis=0, keepdims=True)
        lin_grad[:, cols] = dx.astype(bf16)
        return carry

    def convolve(first, last):
        return lambda: lax.fori_loop(first, last, conv_step, 0)

    heads = [functools.partial(one_head, h) for h in range(HEADS)]
    total = QKV // width
    return clear, heads, rates, [convolve(0, total // 2), convolve(total // 2, total)]


MESH = pl.DeviceIdType.MESH


class Place:
    def __init__(self, n_shard, n_rep):
        self.n, self.reps = n_shard, n_rep
        self.ys = n_shard // 4
        self.r = lax.axis_index("rep")
        self.s = lax.axis_index("shard")
        self.c = self.s % 2
        self.x = (self.s // 2) % 2
        self.y = self.s // 4
        half = n_rep // 2
        low = self.r < half
        self.depth = jnp.where(low, self.r, n_rep - 1 - self.r)
        self.inner = jnp.where(low, self.r + 1, self.r - 1)
        self.outer = jnp.where(low, self.r - 1, self.r + 1)
        self.middle = self.depth == half - 1
        self.deep = self.depth > 0
        self.half = self.depth % 2

    def partner(self):
        return (self.r + 1 - 2 * (self.r % 2), self.s)

    def shard_id(self, y, x, c):
        return (self.r, (y * 2 + x) * 2 + c)

    def core_peer(self):
        return self.shard_id(self.y, self.x, 1 - self.c)

    def x_peer(self):
        return self.shard_id(self.y, 1 - self.x, self.c)

    def y_of(self, step):
        return (self.y + step) % self.ys

    def y_peer(self, step):
        return self.shard_id(self.y_of(step), self.x, self.c)


def remote(src, dst, send, recv, device):
    return pltpu.make_async_remote_copy(
        src_ref=src, dst_ref=dst, send_sem=send, recv_sem=recv, device_id=device, device_id_type=MESH
    )


def greet(place, with_rep):
    barrier = pltpu.get_barrier_semaphore()
    n = place.n
    for step in range(1, n):
        pl.semaphore_signal(
            barrier, inc=1, device_id=(place.r, (place.s + step) % n), device_id_type=MESH
        )
    if not with_rep:
        pl.semaphore_wait(barrier, n - 1)
        return
    for step in range(1, place.reps):
        pl.semaphore_signal(
            barrier, inc=1, device_id=((place.r + step) % place.reps, place.s), device_id_type=MESH
        )
    pl.semaphore_wait(barrier, n - 1 + place.reps - 1)


def add_into(dst, idx, *others):
    total = dst[idx].astype(f32)
    for ref, at in others:
        total = total + ref[at].astype(f32)
    dst[idx] = total.astype(dst.dtype)


RING = 10
ZRING = 12


def halved(rows):
    return (rows // 2) // 16 * 16


class Ring:
    def __init__(self, n, rows, cols, twins=1):
        self.n, self.rows, self.cols, self.twins = n, rows, cols, twins
        self.ys = n // 4
        self.count = 0

    def scratch(self):
        k, ys, cols = RING, self.ys, self.cols
        sems = pltpu.SemaphoreType.DMA
        per = 3 + 2 * (ys - 1)
        half = self.rows - halved(self.rows)
        return [
            pltpu.VMEM((k, ys, 2, 2, self.rows, cols), bf16),
            pltpu.VMEM((k, ys, 2, self.rows, cols), bf16),
            pltpu.VMEM((k, ys, half, cols), bf16),
            pltpu.VMEM((k, ys - 1, 2, half, cols), bf16),
            pltpu.VMEM((k, ys - 1, half, cols), bf16),
            pltpu.VMEM((k, half, cols), bf16),
            pltpu.VMEM((4, ZRING, self.twins, self.rows, cols), bf16),
            sems((k, per)),
            sems((k, per)),
            sems((ZRING, 6 + self.twins)),
        ]

    def bind(self, refs):
        (self.own, self.r0, self.r1a, self.r1b, self.r2a, self.r2b, self.z, self.send, self.recv, self.zsem) = refs


class Piece:
    def __init__(self, ring, place, rows, cols, out, out_cols):
        self.ring, self.p, self.rows = ring, place, rows
        self.twin = len(out_cols) == 2
        self.side = pl.ds(0, len(out_cols))
        self.slot, self.zslot = ring.count % RING, ring.count % ZRING
        ring.count += 1
        self.w = pl.ds(0, cols)
        self.ra = halved(rows)
        self.rb = rows - self.ra
        self.all_rows = pl.ds(0, rows)
        self.outs = [out.at[:, pl.ds(at, cols)] for at in out_cols]

    def own_view(self):
        return self.ring.own.at[self.slot, :, :, :, self.all_rows, self.w]

    def store_rows(self, value):
        ring = self.ring
        shaped = value.reshape(ring.ys, 2, 2, rinself.rows, value.shape[-1])
        ring.own[self.slot, :, :, :, self.all_rows, self.w] = shaped

    def send_core(self):
        g, p, k = self.ring, self.p, self.slot
        self.c0 = remote(
            g.own.at[k, :, :, 1 - p.c, self.all_rows, self.w], g.r0.at[k, :, :, self.all_rows, self.w],
            g.send.at[k, 0], g.recv.at[k, 0], p.core_peer(),
        )
        self.c0.start()

    def after_core(self):
        g, p, k, w = self.ring, self.p, self.slot, self.w
        rows = self.all_rows
        self.c0.wait()

        def step(q, carry):
            yy, xx = q // 2, q % 2
            add_into(g.own, (k, yy, xx, p.c, rows, w), (g.r0, (k, yy, xx, rows, w)))
            return carry

        lax.fori_loop(0, g.ys * 2, step, 0)
        top, low = pl.ds(0, self.ra), pl.ds(self.ra, self.rb)
        first, second = pl.ds(0, self.ra), pl.ds(0, self.rb)
        self.c1 = [
            remote(
                g.own.at[k, :, 1 - p.x, p.c, top, w], g.r1a.at[k, :, first, w],
                g.send.at[k, 1], g.recv.at[k, 1], p.x_peer(),
            )
        ]
        for d in range(1, g.ys):
            self.c1.append(
                remote(
                    g.own.at[k, p.y_of(d), :, p.c, low, w], g.r1b.at[k, d - 1, :, second, w],
                    g.send.at[k, 1 + d], g.recv.at[k, 1 + d], p.y_peer(d),
                )
            )
        for c in self.c1:
            c.start()

    def after_first(self):
        g, p, k, w = self.ring, self.p, self.slot, self.w
        top, low = pl.ds(0, self.ra), pl.ds(self.ra, self.rb)
        first, second = pl.ds(0, self.ra), pl.ds(0, self.rb)
        for c in self.c1:
            c.wait()
        for yy in range(g.ys):
            add_into(g.own, (k, yy, p.x, p.c, top, w), (g.r1a, (k, yy, first, w)))
        for xx in range(2):
            add_into(
                g.own, (k, p.y, xx, p.c, low, w),
                *[(g.r1b, (k, d, xx, second, w)) for d in range(g.ys - 1)],
            )
        self.c2 = [
            remote(
                g.own.at[k, p.y, 1 - p.x, p.c, low, w], g.r2b.at[k, second, w],
                g.send.at[k, 1 + g.ys], g.recv.at[k, 1 + g.ys], p.x_peer(),
            )
        ]
        for d in range(1, g.ys):
            self.c2.append(
                remote(
                    g.own.at[k, p.y_of(d), p.x, p.c, top, w], g.r2a.at[k, d - 1, first, w],
                    g.send.at[k, 1 + g.ys + d], g.recv.at[k, 1 + g.ys + d], p.y_peer(d),
                )
            )
        for c in self.c2:
            c.start()

    def after_second(self):
        g, p, k, w = self.ring, self.p, self.slot, self.w
        zk = self.zslot
        for c in self.c2:
            c.wait()
        top, low = pl.ds(0, self.ra), pl.ds(self.ra, self.rb)
        total = g.own[k, p.y, p.x, p.c, top, w].astype(f32)
        for d in range(g.ys - 1):
            total = total + g.r2a[k, d, 0 : self.ra, w].astype(f32)
        side = p.half if self.twin else 0
        g.z[0, zk, side, top, w] = total.astype(bf16)
        total = g.own[k, p.y, p.x, p.c, low, w].astype(f32) + g.r2b[k, 0 : self.rb, w].astype(f32)
        g.z[0, zk, side, low, w] = total.astype(bf16)
        if self.twin:
            g.z[0, zk, 1 - side, self.all_rows, w] = jnp.zeros((self.rows, w.size), bf16)
        z = lambda i: g.z.at[i, zk, self.side, self.all_rows, w]
        target = lambda r: (r, p.s)
        sem = g.zsem
        self.up = remote(z(0), z(1), sem.at[zk, 0], sem.at[zk, 1], target(p.inner))
        self.meet = remote(z(0), z(2), sem.at[zk, 2], sem.at[zk, 3], target(p.inner))
        self.down = remote(z(3), z(2), sem.at[zk, 4], sem.at[zk, 3], target(p.outer))
        self.home = [
            pltpu.make_async_copy(g.z.at[3, zk, i, self.all_rows, w], out, sem.at[zk, 6 + i])
            for i, out in enumerate(self.outs)
        ]

        @pl.when(p.depth == 0)
        def _():
            self.send_inward()

    def send_inward(self):
        p = self.p

        @pl.when(p.middle)
        def _():
            self.meet.start()

        @pl.when(jnp.logical_not(p.middle))
        def _():
            self.up.start()

    def after_up(self):
        g, p, zk, w = self.ring, self.p, self.zslot, self.w

        @pl.when(p.deep)
        def _():
            self.up.wait_recv()
            for i in range(len(self.outs)):
                add_into(g.z, (0, zk, i, self.all_rows, w), (g.z, (1, zk, i, self.all_rows, w)))
            self.send_inward()

    def finish(self, middle):
        g, p, zk, w = self.ring, self.p, self.zslot, self.w
        rows = self.all_rows

        @pl.when(p.middle if middle else jnp.logical_not(p.middle))
        def _():
            self.meet.wait_recv()
            for i in range(len(self.outs)):
                if middle:
                    both = g.z[0, zk, i, rows, w].astype(f32) + g.z[2, zk, i, rows, w].astype(f32)
                    g.z[3, zk, i, rows, w] = both.astype(bf16)
                else:
                    g.z[3, zk, i, rows, w] = g.z[2, zk, i, rows, w]

            @pl.when(p.deep)
            def _():
                self.down.start()

            for c in self.home:
                c.start()

    def close(self):
        p = self.p

        @pl.when(p.middle)
        def _():
            self.meet.wait_send()

        @pl.when(jnp.logical_not(p.middle))
        def _():
            self.up.wait_send()

        @pl.when(p.deep)
        def _():
            self.down.wait_send()

        for c in self.home:
            c.wait()


def pump(pieces, index):
    stages = [
        (2, lambda q: q.after_core()),
        (18, lambda q: q.close()),
        (17, lambda q: q.finish(False)),
        (14, lambda q: q.finish(True)),
        (11, lambda q: q.after_up()),
        (8, lambda q: q.after_second()),
        (5, lambda q: q.after_first()),
    ]
    for lag, act in stages:
        if 0 <= index - lag < len(pieces):
            act(pieces[index - lag])


class Small:
    def __init__(self, n, reps, rows, cols):
        self.n, self.ys, self.reps = n, n // 4, reps
        self.sizes = (2, 2, self.ys, reps)
        self.rows, self.cols = rows, cols

    def scratch(self):
        total = sum(self.sizes)
        return [
            pltpu.VMEM((total, self.rows, self.cols), f32),
            pltpu.SemaphoreType.DMA((total,)),
            pltpu.SemaphoreType.DMA((total,)),
        ]

    def bind(self, refs):
        self.buf, self.send, self.recv = refs

    def begin(self, place, axis, value):
        base = sum(self.sizes[:axis])
        size = self.sizes[axis]
        p = place
        mine = (p.c, p.x, p.y, p.r)[axis]
        slot = self.buf.at[base + mine]
        slot[...] = value
        self.copies = []
        for d in range(1, size):
            at = (mine + d) % size
            device = (
                p.shard_id(p.y, p.x, at), p.shard_id(p.y, at, p.c), p.shard_id(at, p.x, p.c), (at, p.s),
            )[axis]
            self.copies.append(remote(slot, slot, self.send.at[base + d], self.recv.at[base + d], device))
        for c in self.copies:
            c.start()

    def end(self, axis):
        base = sum(self.sizes[:axis])
        for c in self.copies:
            c.wait()
        total = self.buf[base]
        for d in range(1, self.sizes[axis]):
            total = total + self.buf[base + d]
        return total


class Flow:
    @staticmethod
    def count(ys, pair):
        return 5 + 12 * (ys - 1) if pair else 3 + 6 * (ys - 1)

    def __init__(self, place, src, src_at, cols, dst, dst_at, pair, send, recv, base, mine):
        self.p, self.rows, self.pair = place, src.shape[0], pair
        self.src_ref, self.src_at, self.dst, self.dst_at, self.width = src, src_at, dst, dst_at, cols
        self.send, self.recv, self.base, self.used = send, recv, base, 0
        self.ra = halved(self.rows)
        self.part = (place.r % 2) if pair else None
        whole = self.src_ref.at[:, self.columns(src_at, None)]
        self.mine = pltpu.make_async_copy(whole, self.region(place.y, place.x, place.c), mine)
        self.whole = whole
        self.all = []

    def columns(self, at, part):
        if part is None:
            return pl.ds(at if isinstance(at, int) else pl.multiple_of(at, LANES), self.width)
        half = self.width // 2
        return pl.ds(pl.multiple_of(at + part * half, LANES), half)

    def region(self, y, x, c, half=None, part=None):
        start = ((y * 2 + x) * 2 + c) * self.rows
        size = self.rows
        if half == 0:
            size = self.ra
        elif half == 1:
            start, size = start + self.ra, self.rows - self.ra
        return self.dst.at[pl.ds(pl.multiple_of(start, 16), size), self.columns(self.dst_at, part)]

    def copy(self, dst, device, src=None):
        at = self.base + self.used
        self.used += 1
        c = remote(dst if src is None else src, dst, self.send.at[at], self.recv.at[at], device)
        c.start()
        self.all.append(c)
        return c

    def begin(self):
        p = self.p
        own = self.region(p.y, p.x, p.c, None, self.part)
        src = self.src_ref.at[:, self.columns(self.src_at, self.part)]
        self.mine.start()
        self.from_x = self.copy(own, p.x_peer(), src)
        self.from_y = [self.copy(own, p.y_peer(d), src) for d in range(1, p.ys)]
        self.from_core = [self.copy(self.region(p.y, p.x, p.c), p.core_peer(), self.whole)]
        self.from_z, self.z_regions = [], []

    def share(self, *where):
        p = self.p
        if self.pair:
            self.from_z.append(self.copy(self.region(*where, self.part), (p.r + 1 - 2 * (p.r % 2), p.s)))
            self.z_regions.append(where)
        self.from_core.append(self.copy(self.region(*where, self.part), p.core_peer()))

    def forward(self):
        p = self.p
        steps = range(1, p.ys)
        self.from_x.wait_recv()
        self.diag = [self.copy(self.region(p.y, 1 - p.x, p.c, 0, self.part), p.y_peer(d)) for d in steps]
        self.share(p.y, 1 - p.x, p.c, None)
        for d in steps:
            self.from_y[d - 1].wait_recv()
            back = p.y_of(p.ys - d)
            self.diag.append(self.copy(self.region(back, p.x, p.c, 1, self.part), p.x_peer()))
            self.share(back, p.x, p.c, None)

    def relay(self):
        p = self.p
        for i, c in enumerate(self.diag):
            c.wait_recv()
            half, d = divmod(i, p.ys - 1)
            self.share(p.y_of(p.ys - d - 1), 1 - p.x, p.c, half)

    def swap(self):
        for c, where in zip(self.from_z, self.z_regions):
            c.wait_recv()
            self.from_core.append(self.copy(self.region(*where, 1 - self.part), self.p.core_peer()))

    def done(self):
        for c in self.from_core:
            c.wait_recv()
        self.mine.wait()

    def close(self):
        for c in self.all:
            c.wait_send()


FTILE = 256
FF_TILE = 512


def cuts(total, step):
    return [(at, min(step, total - at)) for at in range(0, total, step)]


def decay_lanes(words):
    lane = lax.broadcasted_iota(jnp.int32, (1, LANES), 1)
    total = jnp.zeros((1, LANES), f32)
    for h in range(HEADS):
        total = jnp.where(lane == HEADS + h, words[h], total)
    return total


def one_hot_rows(values, count):
    return lax.broadcasted_iota(jnp.int32, (count, values.shape[1]), 0) == values


class Store:
    def __init__(self, sem):
        self.sem, self.all = sem, []

    def put(self, src, dst):
        c = pltpu.make_async_copy(src, dst, self.sem.at[len(self.all)])
        c.start()
        self.all.append(c)

    def wait(self):
        for c in self.all:
            c.wait()


FORWARD_SAVED = (
    ("xin", lambda n, d, f: ((n, d), bf16)),
    ("dy", lambda n, d, f: ((2 * n, d), bf16)),
    ("normed_t", lambda n, d, f: ((d, n), bf16)),
    ("lin", lambda n, d, f: ((n, QKV + VALS + LANES), f32)),
    ("act", lambda n, d, f: ((n, QKV), f32)),
    ("cum", lambda n, d, f: ((n, LANES), f32)),
    ("cum_t", lambda n, d, f: ((LANES, n), f32)),
    ("tinv", lambda n, d, f: ((HEADS, n, n), f32)),
    ("fresh", lambda n, d, f: ((n, VALS), f32)),
    ("heads", lambda n, d, f: ((n, VALS), f32)),
    ("mixed_t", lambda n, d, f: ((VALS, n), bf16)),
    ("middle", lambda n, d, f: ((n, d), f32)),
    ("normed_mid_t", lambda n, d, f: ((d, 2 * n), bf16)),
    ("hidden_t", lambda n, d, f: ((f // 2, 2 * n), bf16)),
    ("grads_gu", lambda n, d, f: ((2 * n, f), bf16)),
    ("pick", lambda n, d, f: ((n, n), bf16)),
    ("place", lambda n, d, f: ((n, n), bf16)),
    ("params", lambda n, d, f: ((16, d), f32)),
    ("taps", lambda n, d, f: ((4, QKV), f32)),
)


def transposed(a):
    return a.T.astype(bf16)


def forward_kernel(n_shard, reps, *refs):
    take = iter(refs)
    get = lambda k: [next(take) for _ in range(k)]
    offs, lens, rates_in, bias_in, tokens, cot, deal, small_in = get(8)
    wq, wk, wv, wt, wb, wo, wg, wu, wd = get(9)
    gp, go, gg, gu, gd = get(5)
    outs = dict(zip([name for name, _ in FORWARD_SAVED], get(len(FORWARD_SAVED))))
    kept = dict(zip([name for name, _ in FORWARD_SAVED], get(len(FORWARD_SAVED))))
    (dealt, dsend, drecv, smalls, ssend, srecv, sent, come, tsend, trecv, wbuf, wobuf, wdbuf, load_sem, fsend, frecv,
     mine_sem, out_sem, normed, mixed, normed_mid) = get(21)
    shards, shard_sem, zsend, zrecv = get(9), *get(3)
    rate, bias = get(2)
    rate[...], bias[...] = decay_lanes(rates_in), decay_lanes(bias_in)
    own_loads = []
    for k, (w, v) in enumerate(zip((wq, wk, wv, wt, wb, wo, wd, wg, wu), shards)):
        own_loads.append(pltpu.make_async_copy(w, v, shard_sem.at[k]))
        own_loads[-1].start()
    wq, wk, wv, wt, wb, wo, wd, wg, wu = shards
    rows, width = tokens.shape
    per = rows // n_shard
    place = Place(n_shard, reps)
    p = place
    greet(place, True)
    offsets = [offs[i] for i in range(offs.shape[0])]
    lengths = [lens[i] for i in range(lens.shape[0])]
    store = Store(out_sem)

    dealt[p.s] = jnp.broadcast_to(deal[...], (8, rows))
    smalls[p.s] = small_in[...]
    first = []
    for d in range(1, n_shard):
        to = (p.r, (p.s + d) % n_shard)
        first.append(remote(dealt.at[p.s], dealt.at[p.s], dsend.at[d], drecv.at[d], to))
        first[-1].start()
    for d in range(1, n_shard):
        to = (p.r, (p.s + d) % n_shard)
        first.append(remote(smalls.at[p.s], smalls.at[p.s], ssend.at[d], srecv.at[d], to))
        first[-1].start()

    made = []

    def flow(src, at, cols, dst, dst_at, pair):
        k = len(made)
        base = sum(Flow.count(p.ys, f.pair) for f in made)
        made.append(Flow(place, src, at, cols, dst, dst_at, pair, fsend, frecv, base, mine_sem.at[k]))
        return made[-1]

    ff = wg.shape[1]
    half = ff // 2
    ff_cuts = cuts(half, FF_TILE)
    stages = [
        [flow(wq, 0, KEYS, gp, 0, True), flow(wk, 0, KEYS, gp, KEYS, True), flow(wb, 0, LANES, gp, QKV + VALS, False)],
        [flow(wv, 0, VALS, gp, 2 * KEYS, True)],
        [flow(wt, 0, VALS, gp, QKV, False)],
        [flow(wo, 0, width, go, 0, True)],
        [flow(wd, 0, width // 2, gd, 0, False)],
        [flow(wd, width // 2, width // 2, gd, width // 2, False)],
    ]
    for at, cols in ff_cuts:
        stages.append([flow(wg, p.half * half + at, cols, gg, at, False), flow(wu, p.half * half + at, cols, gu, at, False)])
    last = len(stages) - 1

    events = []
    for k in range(len(stages) + 5):
        for lag, act in ((0, "begin"), (2, "forward"), (3, "relay"), (4, "swap"), (5, "done")):
            if 0 <= k - lag < len(stages):
                events.append((act, k - lag))
    owned = set()

    def poll(count=1):
        for _ in range(count):
            if events:
                act, k = events.pop(0)
                for f in stages[k]:
                    if act == "begin" and id(f.src_ref) not in owned:
                        owned.add(id(f.src_ref))
                        own_loads[[id(v) for v in shards].index(id(f.src_ref))].wait()
                    getattr(f, act)()

    def until(act, k):
        while (act, k) in events:
            poll()

    until("begin", 1)

    loads = {}

    def load(name, src, dst):
        loads[name] = pltpu.make_async_copy(src, dst, load_sem.at[len(loads)])
        loads[name].start()

    for c in first[: n_shard - 1]:
        c.wait_recv()
    i = lax.broadcasted_iota(jnp.int32, (rows, rows), 0)
    j = lax.broadcasted_iota(jnp.int32, (rows, rows), 1)
    upper = (i <= j).astype(bf16)
    everyone = dealt[:, 0, :]
    to_me = (everyone // rows) == p.s
    rank = dot(to_me.astype(f32).astype(bf16), upper).astype(jnp.int32) - 1
    rank = jnp.where(to_me, rank, -1)
    for b in range(n_shard):
        picked = one_hot_rows(rank[b : b + 1, :], per).astype(f32).astype(bf16)
        which = one_hot_rows(everyone[b : b + 1, :] % rows, rows).astype(f32).astype(bf16)
        kept["pick"][b * per : (b + 1) * per, :] = dot(picked, which, 1, 1).astype(bf16)
    pick = kept["pick"][...]
    exchange = []
    for a, src in enumerate((tokens, cot)):
        for at in range(0, width, 256):
            sent[a, :, at : at + 256] = dot(pick, src[:, at : at + 256]).astype(bf16)
        for d in range(1, n_shard):
            t = (p.s + d) % n_shard
            exchange.append(
                remote(
                    sent.at[a, pl.ds(pl.multiple_of(t * per, 16), per)],
                    come.at[a, pl.ds(pl.multiple_of(p.s * per, 16), per)],
                    tsend.at[a, d], trecv.at[a, d], (p.r, t),
                )
            )
            exchange[-1].start()
        here = pl.ds(pl.multiple_of(p.s * per, 16), per)
        come[a, here, :] = sent[a, here, :]
    mine = deal[0:1, :]
    source = mine // rows
    from_each = one_hot_rows(source, n_shard)
    cum = dot(from_each.astype(f32).astype(bf16), upper)
    slot = jnp.sum(jnp.where(from_each, cum, 0.0), axis=0, keepdims=True).astype(jnp.int32) - 1 + source * per
    kept["place"][...] = one_hot_rows(slot, rows).astype(f32).astype(bf16)
    store.put(kept["pick"], outs["pick"])
    store.put(kept["place"], outs["place"])

    for c in first[n_shard - 1 :]:
        c.wait_recv()
    total = smalls[0].astype(f32)
    for t in range(1, n_shard):
        total = total + smalls[t].astype(f32)
    kept["params"][...] = total
    for t in range(4):
        for g in range(QKV // width):
            row = t * (QKV // width) + g
            kept["taps"][t : t + 1, g * width : (g + 1) * width] = total[row : row + 1, :]
    gain1, gain2 = kept["params"].at[12:13, :], kept["params"].at[13:14, :]
    gain_o = kept["params"].at[14:15, 0:DVH]
    store.put(kept["params"], outs["params"])
    store.put(kept["taps"], outs["taps"])

    def unpack(a, name):
        for c in exchange[a * (n_shard - 1) : (a + 1) * (n_shard - 1)]:
            c.wait_recv()
        for at in range(0, width, 256):
            kept[name][0:rows, at : at + 256] = dot(kept["place"][...], come[a, :, at : at + 256], 0, 0).astype(bf16)
    unpack(0, "xin")
    store.put(kept["xin"], outs["xin"])

    def swap_rows(ref, k):
        c = remote(ref.at[pl.ds(0, rows)], ref.at[pl.ds(rows, rows)], zsend.at[k], zrecv.at[k], p.partner())
        c.start()
        return c

    x = kept["xin"][...].astype(f32)
    norm = x * lax.rsqrt(jnp.mean(x * x, axis=1, keepdims=True) + 1e-5) * gain1[...]
    normed[...] = norm.astype(bf16)
    kept["normed_t"][...] = transposed(norm)
    store.put(kept["normed_t"], outs["normed_t"])

    def project(at, cols, tile):
        def step(k, carry):
            here = pl.ds(pl.multiple_of(at + k * tile, 128), tile)
            kept["lin"][:, here] = dot(normed[...], wbuf[:, here])
            return carry

        lax.fori_loop(0, cols // tile, step, 0)

    def fetch(name, at, cols):
        here = pl.ds(at, cols)
        load(name, gp.at[:, here], wbuf.at[:, here])

    until("done", 0)
    fetch("qk", 0, 2 * KEYS)
    fetch("bd", QKV + VALS, LANES)
    until("done", 1)
    fetch("v", 2 * KEYS, VALS)
    loads["qk"].wait()
    loads["bd"].wait()
    project(0, 2 * KEYS, 256)
    project(QKV + VALS, LANES, LANES)
    poll(1)
    loads["v"].wait()
    project(2 * KEYS, VALS, 256)
    until("done", 2)
    fetch("gate", QKV, VALS)
    convolve, heads = mixer_forward(
        rows, offsets, lengths, kept["lin"], kept["taps"], rate, bias, gain_o, kept["act"], kept["cum"],
        kept["cum_t"], kept["tinv"], kept["fresh"], kept["heads"], mixed,
    )
    convolve()
    unpack(1, "dy")
    dy_swap = swap_rows(kept["dy"], 0)
    loads["gate"].wait()
    project(QKV, VALS, 256)
    store.put(kept["lin"], outs["lin"])
    for h in range(0, HEADS, 2):
        heads[h]()
        heads[h + 1]()
        poll(6)
    until("done", 3)
    load("out", go, wobuf)
    for name in ("act", "cum", "cum_t", "tinv", "fresh", "heads"):
        store.put(kept[name], outs[name])
    loads["out"].wait()

    def out_step(k, carry):
        here = pl.ds(pl.multiple_of(k * 256, 256), 256)
        kept["middle"][:, here] = kept["xin"][:, here].astype(f32) + dot(mixed[...], wobuf[:, here])
        return carry

    lax.fori_loop(0, width // 256, out_step, 0)
    store.put(kept["middle"], outs["middle"])
    m = kept["middle"][...]
    norm = m * lax.rsqrt(jnp.mean(m * m, axis=1, keepdims=True) + 1e-5) * gain2[...]
    normed_mid[0:rows, :] = norm.astype(bf16)
    mid_swap = swap_rows(normed_mid, 1)
    kept["normed_mid_t"][:, 0:rows] = transposed(norm)
    kept["mixed_t"][...] = transposed(mixed[...].astype(f32))
    store.put(kept["mixed_t"], outs["mixed_t"])
    until("done", 5)
    load("down", gd.at[pl.ds(pl.multiple_of(p.half * half, LANES), half)], wdbuf)

    def ffn(at, cols):
        def step(k, carry):
            some = pl.ds(pl.multiple_of(k * rows, rows), rows)
            here, there = slice(at, at + cols), slice(half + at, half + at + cols)
            grad = dot(kept["dy"][some, :], wdbuf[here, :], 1, 1)
            gate = dot(normed_mid[some, :], wbuf[:, here])
            up = dot(normed_mid[some, :], wbuf[:, there])
            sg = sigm(gate)
            silu = gate * sg
            hid = silu * up
            kept["hidden_t"][here, some] = transposed(hid)
            kept["grads_gu"][some, here] = (grad * up * (sg + silu * (1.0 - sg))).astype(bf16)
            kept["grads_gu"][some, there] = (grad * silu).astype(bf16)
            return carry

        lax.fori_loop(0, 2, step, 0)

    for i, (at, cols) in enumerate(ff_cuts):
        until("done", last - len(ff_cuts) + 1 + i)
        load(("g", i), gg.at[:, pl.ds(at, cols)], wbuf.at[:, pl.ds(at, cols)])
        load(("u", i), gu.at[:, pl.ds(at, cols)], wbuf.at[:, pl.ds(half + at, cols)])
        if i == 0:
            loads["down"].wait()
            dy_swap.wait()
            mid_swap.wait()
            store.put(kept["dy"], outs["dy"])
            kept["normed_mid_t"][:, rows : 2 * rows] = transposed(normed_mid[rows : 2 * rows, :].astype(f32))
            store.put(kept["normed_mid_t"], outs["normed_mid_t"])
        poll(2)
        loads[("g", i)].wait()
        loads[("u", i)].wait()
        ffn(at, cols)
    for name in ("hidden_t", "grads_gu"):
        store.put(kept[name], outs[name])
    for c in first + exchange:
        c.wait_send()
    for f in made:
        f.close()
    store.wait()


def forward_call(n_shard, reps, offs, lens, tokens, cot, deal, small_in, rate, bias, weights):
    anywhere = pl.BlockSpec(memory_space=pl.ANY)
    held = pl.BlockSpec(memory_space=pltpu.VMEM)
    words = pl.BlockSpec(memory_space=pltpu.SMEM)
    rows, width = tokens.shape
    ff = weights[6].shape[1]
    sd = jax.ShapeDtypeStruct
    wide = QKV + VALS + LANES
    vals_rows, ff_rows = weights[5].shape[0] * n_shard, weights[8].shape[0] * n_shard
    gathered = [
        sd((width, wide), bf16), sd((vals_rows, width), bf16), sd((width, ff // 2), bf16), sd((width, ff // 2), bf16),
        sd((ff_rows, width), bf16),
    ]
    shapes = [fn(rows, width, ff) for _, fn in FORWARD_SAVED]
    sems = pltpu.SemaphoreType.DMA
    flows = 8 + 2 * len(cuts(ff // 2, FF_TILE))
    count = flows * Flow.count(n_shard // 4, True)
    scratch = [pltpu.VMEM(s, d) for s, d in shapes] + [
        pltpu.VMEM((n_shard, 8, rows), jnp.int32), sems((n_shard,)), sems((n_shard,)),
        pltpu.VMEM((n_shard, 16, width), bf16), sems((n_shard,)), sems((n_shard,)),
        pltpu.VMEM((2, rows, width), bf16), pltpu.VMEM((2, rows, width), bf16), sems((2, n_shard)), sems((2, n_shard)),
        pltpu.VMEM((width, wide), bf16), pltpu.VMEM((vals_rows, width), bf16), pltpu.VMEM((ff_rows // 2, width), bf16),
        sems((16,)), sems((count,)), sems((count,)), sems((flows,)), sems((len(shapes),)),
        pltpu.VMEM((rows, width), bf16), pltpu.VMEM((rows, VALS), bf16), pltpu.VMEM((2 * rows, width), bf16),
    ]
    scratch += [pltpu.VMEM(weights[k].shape, bf16) for k in (0, 1, 2, 3, 4, 5, 8, 6, 7)] + [sems((9,)), sems((2,)), sems((2,))]
    scratch += [pltpu.VMEM((1, LANES), f32)] * 2
    res = pl.pallas_call(
        functools.partial(forward_kernel, n_shard, reps),
        in_specs=[words] * 4 + [held] * 4 + [anywhere] * 9,
        out_specs=[anywhere] * (5 + len(shapes)),
        out_shape=gathered + [sd(s, d) for s, d in shapes],
        scratch_shapes=scratch,
        compiler_params=pltpu.CompilerParams(collective_id=1, has_side_effects=True, vmem_limit_bytes=62 << 20),
    )(offs, lens, rate, bias, tokens, cot, deal, small_in, *weights)
    return res[:5], dict(zip([name for name, _ in FORWARD_SAVED], res[5:]))


WIDE = 512
PIECE = 256


class Stream:
    def __init__(self, buf, sem, parts):
        self.buf, self.sem, self.parts, self.at = buf, sem, parts, 0
        self.copies = {}

    def start(self):
        self.issue(0)

    def issue(self, k):
        if k < len(self.parts):
            pairs = self.parts[k](self.buf.at[k % 2])
            self.copies[k] = [pltpu.make_async_copy(s, d, self.sem.at[k % 2, i]) for i, (s, d) in enumerate(pairs)]
            for c in self.copies[k]:
                c.start()

    def take(self):
        k = self.at
        self.at += 1
        self.issue(k + 1)
        for c in self.copies[k]:
            c.wait()
        return k, self.buf.at[k % 2]


BACK_KEPT = tuple(name for name, _ in FORWARD_SAVED)


def backward_kernel(n_shard, reps, rings, small, *refs):
    take = iter(refs)
    get = lambda k: [next(take) for _ in range(k)]
    offs, lens, rates_in, bias_in = get(4)
    gp, go, gg, gu, gd = get(5)
    given = dict(zip(BACK_KEPT, get(len(BACK_KEPT))))
    o_rows, o_grad, o_ffn, o_down, o_out, o_proj, o_small = get(7)
    kept = dict(zip(BACK_KEPT, get(len(BACK_KEPT))))
    (ring,) = rings
    ring.bind(get(10))
    small.bind(get(3))
    (load_sem, wbuf, wsem, nbuf, nsem, acc, middle_grad, branch, mix_grad, dcols, drows, lin_grad, tap_grad, gain_grad,
     rate_grad, bias_grad, small_v, sent, come, tsend, trecv, rows_out, out_sem, swaps, zsend, zrecv, block, rate, bias) = get(29)
    rate[...], bias[...] = decay_lanes(rates_in), decay_lanes(bias_in)
    rows, width = kept["xin"].shape
    half = gg.shape[1]
    ff = 2 * half
    per = rows // n_shard
    place = Place(n_shard, reps)
    p = place
    offsets = [offs[i] for i in range(offs.shape[0])]
    lengths = [lens[i] for i in range(lens.shape[0])]
    loads = {}
    order = (
        "normed_mid_t", "grads_gu", "middle", "dy", "params", "hidden_t", "cum", "cum_t", "tinv", "fresh", "heads",
        "act", "lin", "taps", "mixed_t", "normed_t", "xin", "pick", "place",
    )
    for k, name in enumerate(order):
        loads[name] = pltpu.make_async_copy(given[name], kept[name], load_sem.at[k])
        loads[name].start()
    have = set()

    def need(*names):
        for name in names:
            if name not in have:
                have.add(name)
                loads[name].wait()

    greet(place, True)
    pieces = []

    def tick(piece=None, fill=None):
        index = tick.index
        tick.index += 1
        pump(pieces, index)
        if piece is not None:
            pieces.append(piece())
            fill(pieces[-1])
            pieces[-1].send_core()

    tick.index = 0

    size = width // n_shard

    def wide_piece(left, right, right_at, cols, out, out_at):
        def fill(piece):
            value = dot(left[...], right[:, right_at : right_at + cols]).astype(bf16)
            ring.own[piece.slot, :, :, :, :, 0:cols] = value.reshape(ring.ys, 2, 2, size, cols)

        tick(lambda: Piece(ring, place, size, cols, out, out_at), fill)

    def block_piece(left, right, at, cols, first, count, out):
        total = left.shape[0]
        long = out.shape[0]
        held = total // long
        ys = held // 4

        def fill(piece):
            if first == 0:
                block[0:total, 0:cols] = dot(left[...], right[:, at : at + cols]).astype(bf16)
            for t in range(held):
                y = t // 4 if held == n_shard else p.half * ys + t // 4
                part = block[t * long + first : t * long + first + count, 0:cols]
                ring.own[piece.slot, y, (t // 2) % 2, t % 2, 0:count, 0:cols] = part
            if held < n_shard:
                for t in range(held):
                    y = (1 - p.half) * ys + t // 4
                    ring.own[piece.slot, y, (t // 2) % 2, t % 2, 0:count, 0:cols] = jnp.zeros((count, cols), bf16)

        tick(lambda: Piece(ring, place, count, cols, out.at[pl.ds(first, count)], (at,)), fill)

    queue = []

    def run(count=1):
        for _ in range(count):
            queue.pop(0)()

    gu_cuts = [(side, at, cols) for side in (0, 1) for at, cols in cuts(half, WIDE)]

    def gu_piece(side, at, cols):
        need("normed_mid_t", "grads_gu")
        outs = (side * ff + at, side * ff + half + at)
        wide_piece(kept["normed_mid_t"], kept["grads_gu"], side * half + at, cols, o_ffn, outs)

    def down_piece(at, first, count):
        need("hidden_t", "dy")
        block_piece(kept["hidden_t"], kept["dy"], at, PIECE, first, count, o_down)

    def out_piece(at, first, count):
        need("mixed_t")
        block_piece(kept["mixed_t"], branch, at, PIECE, first, count, o_out)

    def proj_piece(at, cols):
        need("normed_t")
        wide_piece(kept["normed_t"], lin_grad, at, cols, o_proj, (at,))

    def blocks(fn, out):
        return [
            functools.partial(fn, at, first, count) for at, _ in cuts(width, PIECE) for first, count in cuts(out.shape[0], size)
        ]

    sided = [functools.partial(gu_piece, side, at, cols) for side in (0, 1) for at, cols in cuts(half, PIECE)]
    downs = blocks(down_piece, o_down)
    while sided or downs:
        queue.extend(sided[:1] + downs[:1])
        del sided[:1], downs[:1]
    queue.extend(blocks(out_piece, o_out))
    wide = cuts(QKV + VALS, PIECE)
    late = QKV // PIECE
    for at, cols in wide[late:] + wide[:late] + [(QKV + VALS, LANES)]:
        queue.append(functools.partial(proj_piece, at, cols))

    def gu_part(k):
        side, at, cols = gu_cuts[k]
        return lambda b: [((gg, gu)[side].at[:, pl.ds(at, cols)], b.at[:, pl.ds(0, cols)])]

    gu_stream = Stream(wbuf, wsem, [gu_part(k) for k in range(len(gu_cuts))])

    def gnm(count):
        need("grads_gu")
        for _ in range(count):
            k, buf = gu_stream.take()
            side, at, cols = gu_cuts[k]
            at = side * half + at
            part = dot(kept["grads_gu"][:, at : at + cols], buf[:, 0:cols], 1, 1)
            acc[...] = part if k == 0 else acc[...] + part

    def to_partner(k):
        swaps[0] = acc[rows : 2 * rows, :].astype(bf16)
        c = remote(swaps.at[0], swaps.at[1 + k], zsend.at[k], zrecv.at[k], p.partner())
        c.start()
        return c

    def norm_back(values, gain, upstream):
        n = lax.rsqrt(jnp.mean(values * values, axis=1, keepdims=True) + 1e-5)
        u = upstream * gain
        gain_part = jnp.sum(upstream * values * n, axis=0, keepdims=True)
        return n * (u - values * (n * n) * jnp.mean(u * values, axis=1, keepdims=True)), gain_part

    def norm2():
        need("middle", "dy", "params")
        mid_swap.wait()
        upstream = acc[0:rows, :] + swaps[1].astype(f32)
        back, gain_part = norm_back(kept["middle"][...], kept["params"][13:14, :], upstream)
        small_v[13:14, :] = gain_part
        total = kept["dy"][0:rows, :].astype(f32) + back
        middle_grad[...] = total
        branch[...] = total.astype(bf16)

    def row_part(src, k):
        return lambda b: [(src.at[pl.ds(k * FTILE, FTILE), :], b)]

    out_stream = Stream(nbuf, nsem, [row_part(go, k) for k in range(VALS // FTILE)])
    down_cuts = cuts(half, FTILE)

    def down_part(at, size):
        start = pl.multiple_of(p.half * half + at, LANES)
        return lambda b: [(gd.at[pl.ds(start, size), :], b.at[pl.ds(0, size)])]

    down_stream = Stream(nbuf, nsem, [down_part(at, size) for at, size in down_cuts])

    def grad_mixed(count):
        for _ in range(count):
            k, buf = out_stream.take()
            mix_grad[:, k * FTILE : (k + 1) * FTILE] = dot(branch[...], buf[...], 1, 1)

    def result(count):
        need("hidden_t", "middle")
        for _ in range(count):
            k, buf = down_stream.take()
            at, size = down_cuts[k]
            part = dot(kept["hidden_t"][at : at + size, :], buf[0:size, :], 0, 0)
            acc[...] = part if k == 0 else acc[...] + part

    exchange = {}

    def send_home(a, value):
        need("place")
        here = pl.ds(pl.multiple_of(p.s * per, 16), per)
        for at in range(0, width, 256):
            sent[a, :, at : at + 256] = dot(kept["place"][...], value[:, at : at + 256]).astype(bf16)
        exchange[a] = []
        for d in range(1, n_shard):
            t = (p.s + d) % n_shard
            exchange[a].append(
                remote(
                    sent.at[a, pl.ds(pl.multiple_of(t * per, 16), per)], come.at[a, here],
                    tsend.at[a, d], trecv.at[a, d], (p.r, t),
                )
            )
            exchange[a][-1].start()
        come[a, here, :] = sent[a, here, :]

    stores = []

    def arrive(a, out):
        need("pick")
        for c in exchange[a]:
            c.wait()
        for at in range(0, width, 256):
            rows_out[a, :, at : at + 256] = dot(kept["pick"][...], come[a, :, at : at + 256], 0, 0).astype(bf16)
        stores.append(pltpu.make_async_copy(rows_out.at[a], out, out_sem.at[a]))
        stores[-1].start()

    def wide_part(at, cols):
        return lambda b: [(gp.at[:, pl.ds(at, cols)], b.at[:, pl.ds(0, cols)])]

    proj_cuts = [(at, WIDE) for at in range(0, QKV + VALS, WIDE)] + [(QKV + VALS, LANES)]
    proj_stream = Stream(wbuf, wsem, [wide_part(at, cols) for at, cols in proj_cuts])

    def grad_normed(count):
        for _ in range(count):
            k, buf = proj_stream.take()
            at, cols = proj_cuts[k]
            part = dot(lin_grad[:, at : at + cols], buf[:, 0:cols], 1, 1)
            acc[0:rows, :] = part if k == 0 else acc[0:rows, :] + part

    def norm1():
        need("xin")
        back, gain_part = norm_back(kept["xin"][...].astype(f32), kept["params"][12:13, :], acc[0:rows, :])
        small_v[12:13, :] = gain_part
        rows_out[1] = (middle_grad[...] + back).astype(bf16)

    def pack_small():
        small_v[14:16, :] = jnp.zeros((2, width), f32)
        for t in range(4):
            for g in range(QKV // width):
                row = t * (QKV // width) + g
                small_v[row : row + 1, :] = tap_grad[t : t + 1, g * width : (g + 1) * width]
        small_v[14:15, 0:DVH] = gain_grad[...]
        small_v[14:15, DVH : DVH + LANES] = rate_grad[...]
        small_v[14:15, DVH + LANES : DVH + 2 * LANES] = bias_grad[...]

    gu_stream.start()
    out_stream.start()
    for _ in gu_cuts:
        run()
        gnm(1)
    mid_swap = to_partner(0)
    run(6)
    need("cum", "cum_t", "tinv", "fresh", "heads", "act", "lin", "taps")
    clear, heads, rates, convs = mixer_backward(
        rows, offsets, lengths, kept["lin"], kept["taps"], rate, bias, kept["params"].at[14:15, 0:DVH], kept["act"],
        kept["cum"], kept["cum_t"], kept["tinv"], kept["fresh"], kept["heads"], mix_grad,
        kept["act"], dcols, drows, lin_grad, tap_grad, gain_grad, rate_grad, bias_grad,
    )
    clear()
    norm2()
    run()
    grad_mixed(3)
    run()
    grad_mixed(3)
    down_stream.start()
    for head in heads:
        run(2)
        head()
    for step in [rates] + convs:
        run()
        step()
    while len(queue) > len(wide) + 1:
        run()
    result(3)
    run()
    result(len(down_cuts) - 3)
    result_swap = to_partner(1)
    proj_stream.start()
    run(4)
    result_swap.wait()
    rows_out[0] = (kept["middle"][...] + acc[0:rows, :] + swaps[2].astype(f32)).astype(bf16)
    send_home(0, rows_out.at[0])
    run()
    for count in (3, 3, len(proj_cuts) - 6):
        grad_normed(count)
        run()
    norm1()
    send_home(1, rows_out.at[1])
    pack_small()
    value = small_v[...]
    for k in range(4):
        small.begin(place, k, value)
        run()
        value = small.end(k)
    arrive(0, o_rows)
    run()
    arrive(1, o_grad)
    run(len(queue))
    for _ in range(18):
        tick()
    o_small[...] = value
    for c in stores:
        c.wait()


def backward_call(n_shard, reps, offs, lens, rate, bias, gathered, saved):
    anywhere = pl.BlockSpec(memory_space=pl.ANY)
    held = pl.BlockSpec(memory_space=pltpu.VMEM)
    words = pl.BlockSpec(memory_space=pltpu.SMEM)
    rows, width = saved["xin"].shape
    ff = 2 * gathered[2].shape[1]
    sd = jax.ShapeDtypeStruct
    wide = QKV + VALS + LANES
    sems = pltpu.SemaphoreType.DMA
    rings = (Ring(n_shard, width // n_shard, PIECE, 2),)
    small = Small(n_shard, reps, 16, width)
    outs = [
        sd((rows, width), bf16), sd((rows, width), bf16), sd((width // n_shard, 2 * ff), bf16),
        sd((ff // n_shard, width), bf16), sd((VALS // n_shard, width), bf16), sd((width // n_shard, wide), bf16),
        sd((16, width), f32),
    ]
    vmem = pltpu.VMEM
    scratch = [vmem(saved[name].shape, saved[name].dtype) for name in BACK_KEPT]
    scratch += rings[0].scratch() + small.scratch()
    scratch += [
        sems((len(BACK_KEPT),)), vmem((2, width, WIDE), bf16), sems((2, 2)), vmem((2, FTILE, width), bf16), sems((2, 1)),
        vmem((2 * rows, width), f32), vmem((rows, width), f32), vmem((rows, width), bf16), vmem((rows, VALS), f32),
        vmem((rows, LANES), f32), vmem((LANES, rows), f32), vmem((rows, wide), bf16), vmem((4, QKV), f32),
        vmem((1, DVH), f32), vmem((1, LANES), f32), vmem((1, LANES), f32), vmem((16, width), f32),
        vmem((2, rows, width), bf16), vmem((2, rows, width), bf16), sems((2, n_shard)), sems((2, n_shard)),
        vmem((2, rows, width), bf16), sems((2,)), vmem((3, rows, width), bf16), sems((2,)), sems((2,)),
        vmem((max(VALS, ff // 2), PIECE), bf16), vmem((1, LANES), f32), vmem((1, LANES), f32),
    ]
    return pl.pallas_call(
        functools.partial(backward_kernel, n_shard, reps, rings, small),
        in_specs=[words] * 4 + [anywhere] * (5 + len(BACK_KEPT)),
        out_specs=[anywhere] * 6 + [held],
        out_shape=outs,
        scratch_shapes=scratch,
        compiler_params=pltpu.CompilerParams(collective_id=0, has_side_effects=True, vmem_limit_bytes=63 << 20),
    )(offs, lens, rate, bias, *gathered, *[saved[name] for name in BACK_KEPT])


def local(
    reps, tokens, cotangent, deal, offsets, lengths, norm1_gain, q_weight, k_weight, v_weight, conv_weight,
    beta_weight, decay_weight, log_rate, step_bias, out_gate_weight, out_norm_gain, out_weight, norm2_gain,
    ffn_gate, ffn_up, ffn_down,
):
    rows, width = tokens.shape
    n = lax.axis_size("shard")
    s = lax.axis_index("shard")
    pad = LANES - 2 * HEADS
    bd_weight = jnp.concatenate([beta_weight, decay_weight, jnp.zeros((beta_weight.shape[0], pad), bf16)], axis=1)
    def spread(vector):
        k, size = vector.shape
        mine = jnp.arange(n)[None, :, None] == s
        return jnp.where(mine, vector[:, None, :], jnp.zeros((), bf16)).reshape(-1, min(width, n * size))

    gain = spread(out_norm_gain[None])
    small_in = jnp.concatenate(
        [
            spread(conv_weight), spread(norm1_gain[None]), spread(norm2_gain[None]),
            jnp.pad(gain, ((0, 1), (0, width - gain.shape[1]))),
        ]
    )
    weights = (q_weight, k_weight, v_weight, out_gate_weight, bd_weight, out_weight, ffn_gate, ffn_up, ffn_down)
    deals = deal[None, :]
    gathered, saved = forward_call(
        n, reps, offsets[0], lengths[0], tokens, cotangent, deals, small_in, log_rate, step_bias, weights
    )
    home_rows, home_grad, s_ffn, s_down, s_out, s_proj, small = backward_call(
        n, reps, offsets[0], lengths[0], log_rate, step_bias, gathered, saved
    )

    def part(a, dim=0):
        size = a.shape[dim] // n
        return lax.dynamic_slice_in_dim(a, s * size, size, dim)

    at = QKV + VALS
    ff = ffn_gate.shape[1]
    proj = [(0, 0, KEYS), (0, KEYS, KEYS), (0, 2 * KEYS, VALS), (0, QKV, VALS), (0, at, LANES)]
    rest = [(1, 0, ff), (1, ff, ff), (2, 0, width), (3, 0, width)]
    g_q, g_k, g_v, g_t, g_bd, g_gate, g_up, g_down, g_out = widen([s_proj, s_ffn, s_down, s_out], proj + rest)
    return (
        home_rows, home_grad, part(small[12]), g_q, g_k, g_v, part(small[:12].reshape(4, QKV), 1), g_bd[:, :HEADS],
        g_bd[:, HEADS : 2 * HEADS], small[14, DVH + HEADS : DVH + 2 * HEADS],
        small[14, DVH + LANES + HEADS : DVH + LANES + 2 * HEADS], g_t, part(small[14, :DVH]), g_out, part(small[13]),
        g_gate, g_up, g_down,
    )


def widen(sources, cut):
    k, total = len(sources), len(cut)

    def kernel(*refs):
        ins, outs = refs[:k], refs[k : k + total]
        narrow, wide = refs[k + total : 2 * k + total], refs[2 * k + total : 2 * (k + total)]
        come, go = refs[2 * (k + total) :]
        for i in range(k):
            pltpu.make_async_copy(ins[i], narrow[i], come.at[i]).start()
        ready = set()
        for j, (i, at, cols) in enumerate(cut):
            if i not in ready:
                ready.add(i)
                pltpu.make_async_copy(ins[i], narrow[i], come.at[i]).wait()
            wide[j][...] = narrow[i][:, at : at + cols].astype(f32)
            pltpu.make_async_copy(wide[j], outs[j], go.at[j]).start()
        for j in range(total):
            pltpu.make_async_copy(wide[j], outs[j], go.at[j]).wait()

    anywhere = pl.BlockSpec(memory_space=pl.ANY)
    shapes = [(sources[i].shape[0], cols) for i, _, cols in cut]
    return pl.pallas_call(
        kernel,
        in_specs=[anywhere] * k,
        out_specs=[anywhere] * total,
        out_shape=[jax.ShapeDtypeStruct(shape, f32) for shape in shapes],
        scratch_shapes=[pltpu.VMEM(a.shape, bf16) for a in sources]
        + [pltpu.VMEM(shape, f32) for shape in shapes]
        + [pltpu.SemaphoreType.DMA((k,)), pltpu.SemaphoreType.DMA((total,))],
        compiler_params=pltpu.CompilerParams(vmem_limit_bytes=62 << 20),
    )(*sources)


def solution(mesh):
    rows2, shard0 = P(("rep", "shard"), None), P("shard", None)
    vec = P("shard")
    in_specs = (
        rows2, rows2, P(("rep", "shard")), rows2, rows2, vec, shard0, shard0, shard0, P(None, "shard"),
        shard0, shard0, P(), P(), shard0, vec, shard0, vec, shard0, shard0, shard0,
    )
    out_specs = (
        rows2, rows2, vec, shard0, shard0, shard0, P(None, "shard"), shard0, shard0, P(), P(), shard0,
        vec, shard0, vec, shard0, shard0, shard0,
    )
    body = functools.partial(local, mesh.shape["rep"])
    return jax.shard_map(body, mesh=mesh, in_specs=in_specs, out_specs=out_specs, check_vma=False)
```

```python
import functools
import jax
import jax.numpy as jnp
from jax import lax
from jax.experimental import pallas as pl
from jax.experimental.pallas import tpu as pltpu
from jax.sharding import PartitionSpec as P

f32 = jnp.float32
bf16 = jnp.bfloat16
HEADS = 6
DK = 128
DVH = 256
KEYS = 768
VALS = 1536
QKV = 2 * KEYS + VALS
LANES = 128


def two_parts(a):
    hi = a.astype(bf16)
    return hi, (a - hi.astype(f32)).astype(bf16)


def dot(a, b, ca=1, cb=0):
    return lax.dot_general(a, b, (((ca,), (cb,)), ((), ())), preferred_element_type=f32)


def dot3(a, b, ca=1, cb=0):
    ah, al = a
    bh, bl = b
    return dot(ah, bh, ca, cb) + (dot(ah, bl, ca, cb) + dot(al, bh, ca, cb))


def tri_dot(tri, cols):
    hi = cols.astype(bf16)
    rest = cols - hi.astype(f32)
    mid = rest.astype(bf16)
    lo = (rest - mid.astype(f32)).astype(bf16)
    return dot(tri, hi) + (dot(tri, mid) + dot(tri, lo))


def sigm(a):
    return 1.0 / (1.0 + jnp.exp(-a))


def softplus(a):
    return jnp.maximum(a, 0.0) + jnp.log1p(jnp.exp(-jnp.abs(a)))


def layout_cols(offs, lens, n, shape, dim):
    row = lax.broadcasted_iota(jnp.int32, shape, dim)
    begin = jnp.zeros_like(row)
    extent = jnp.zeros_like(row)
    for i in range(len(offs)):
        inside = row >= offs[i]
        begin = jnp.where(inside, offs[i], begin)
        extent = jnp.where(inside, lens[i], extent)
    return begin, row - begin, (row - begin) < extent


def conv_chunk(x, taps, pos, cols):
    total = taps[0:1, cols] * x
    for t in range(1, 4):
        total = total + taps[t : t + 1, cols] * jnp.where(pos >= t, pltpu.roll(x, t, 0), 0.0)
    return total


def lane_pick(a, lane, index):
    return jnp.sum(jnp.where(lane == index, a, 0.0), axis=1, keepdims=True)


def pair_masks(n, begin_c, begin_r):
    i = lax.broadcasted_iota(jnp.int32, (n, n), 0)
    j = lax.broadcasted_iota(jnp.int32, (n, n), 1)
    same = begin_c == begin_r
    return i, j, (i >= j) & same


def mixer_forward(n, offs, lens, lin, taps, rate, bias, gain, act, cum, cum_t, tinv, fresh, heads_out, mixed):
    begin_c, pos, live = layout_cols(offs, lens, n, (n, 1), 0)
    begin_r, _, _ = layout_cols(offs, lens, n, (1, n), 1)
    live_f = live.astype(f32)
    width = 384

    def conv_step(step, carry):
        cols = pl.ds(pl.multiple_of(step * width, width), width)
        pre = conv_chunk(lin[:, cols], taps, pos, cols)
        act[:, cols] = pre * sigm(pre)
        return carry

    lane = lax.broadcasted_iota(jnp.int32, (n, LANES), 1)
    bd = lin[:, QKV + VALS : QKV + VALS + LANES]
    beta = sigm(bd) * live_f
    decay = -jnp.exp(rate[...]) * softplus(bd + bias[...]) * live_f
    i, j, low = pair_masks(n, begin_c, begin_r)
    eye = (i == j).astype(f32)

    def convolve():
        lax.fori_loop(0, QKV // width, conv_step, 0)
        total = tri_dot((i >= j).astype(bf16), decay)
        cum[...] = total
        cum_t[...] = total.T

    def one_head(h):
        kcols = pl.ds(pl.multiple_of(h * DK, DK), DK)
        ka = act[:, pl.ds(pl.multiple_of(KEYS + h * DK, DK), DK)]
        qa = act[:, kcols]
        vcols = pl.ds(pl.multiple_of(h * DVH, DVH), DVH)
        v = act[:, pl.ds(pl.multiple_of(2 * KEYS + h * DVH, DVH), DVH)]
        q = qa * (lax.rsqrt(jnp.sum(qa * qa, axis=1, keepdims=True) + 1e-6) * DK**-0.5)
        k = ka * lax.rsqrt(jnp.sum(ka * ka, axis=1, keepdims=True) + 1e-6)
        beta_c = lane_pick(beta, lane, h)
        cum_c = lane_pick(cum[...], lane, HEADS + h)
        cum_r = cum_t[pl.ds(HEADS + h, 1), :]
        kk, qq = two_parts(k), two_parts(q)
        dec = jnp.where(low, jnp.exp(jnp.where(low, cum_c - cum_r, 0.0)), 0.0)
        system = jnp.where(i > j, beta_c * dot3(kk, kk, 1, 1) * dec, 0.0)
        inv = eye - jnp.where((i // 2) == (j // 2), system, 0.0)
        size = 2
        while size < n:
            off = jnp.where(((i // (2 * size)) == (j // (2 * size))) & ((i // size) != (j // size)), system, 0.0)
            parts = two_parts(inv)
            inv = inv - dot3(two_parts(dot3(parts, two_parts(off))), parts)
            size *= 2
        tinv[h] = inv
        u = dot3(two_parts(inv), two_parts(beta_c * v))
        fresh[:, vcols] = u
        o = dot3(two_parts(dot3(qq, kk, 1, 1) * dec), two_parts(u)) * live_f
        heads_out[:, vcols] = o
        gate = lin[:, pl.ds(pl.multiple_of(QKV + h * DVH, DVH), DVH)]
        scaled = o * lax.rsqrt(jnp.mean(o * o, axis=1, keepdims=True) + 1e-5)
        mixed[:, vcols] = (scaled * gain[...] * (gate * sigm(gate))).astype(bf16)

    return convolve, [functools.partial(one_head, h) for h in range(HEADS)]


def mixer_backward(
    n, offs, lens, lin, taps, rate, bias, gain, act, cum, cum_t, tinv, fresh, heads_out, grad_mixed,
    dact, dcols, drows, lin_grad, tap_grad, gain_grad, rate_grad, bias_grad,
):
    begin_c, pos, live = layout_cols(offs, lens, n, (n, 1), 0)
    begin_r, _, _ = layout_cols(offs, lens, n, (1, n), 1)
    live_f = live.astype(f32)
    lane = lax.broadcasted_iota(jnp.int32, (n, LANES), 1)
    bd = lin[:, QKV + VALS : QKV + VALS + LANES]
    sig_b = sigm(bd)
    beta = sig_b * live_f
    i, j, low = pair_masks(n, begin_c, begin_r)
    strict = low & (i > j)

    def clear():
        gain_grad[...] = jnp.zeros_like(gain_grad)
        dcols[...] = jnp.zeros_like(dcols)
        drows[...] = jnp.zeros_like(drows)

    def one_head(h):
        kcols = pl.ds(pl.multiple_of(h * DK, DK), DK)
        kcols2 = pl.ds(pl.multiple_of(KEYS + h * DK, DK), DK)
        vcols = pl.ds(pl.multiple_of(h * DVH, DVH), DVH)
        vcols2 = pl.ds(pl.multiple_of(2 * KEYS + h * DVH, DVH), DVH)
        gcols = pl.ds(pl.multiple_of(QKV + h * DVH, DVH), DVH)
        ka = act[:, kcols2]
        qa = act[:, kcols]
        v = act[:, vcols2]
        o = heads_out[:, vcols]
        gate = lin[:, gcols]
        dm = grad_mixed[:, vcols]
        ro = lax.rsqrt(jnp.mean(o * o, axis=1, keepdims=True) + 1e-5)
        scaled = o * ro
        sg = sigm(gate)
        si = gate * sg
        gain_grad[...] += jnp.sum(dm * scaled * si, axis=0, keepdims=True)
        lin_grad[:, gcols] = (dm * scaled * gain[...] * (sg + si * (1.0 - sg))).astype(bf16)
        ds = dm * gain[...] * si
        d_o = two_parts(ro * (ds - scaled * jnp.mean(ds * scaled, axis=1, keepdims=True)) * live_f)
        rq = lax.rsqrt(jnp.sum(qa * qa, axis=1, keepdims=True) + 1e-6)
        rk = lax.rsqrt(jnp.sum(ka * ka, axis=1, keepdims=True) + 1e-6)
        qhat = qa * rq
        k = ka * rk
        kk, qq = two_parts(k), two_parts(qhat * DK**-0.5)
        beta_c = lane_pick(beta, lane, h)
        cum_c = lane_pick(cum[...], lane, HEADS + h)
        cum_r = cum_t[pl.ds(HEADS + h, 1), :]
        dec = jnp.where(low, jnp.exp(jnp.where(low, cum_c - cum_r, 0.0)), 0.0)
        gram = dot3(kk, kk, 1, 1)
        qk = dot3(qq, kk, 1, 1)
        uu = two_parts(fresh[:, vcols])
        du = dot3(two_parts(qk * dec), d_o, 0, 0)
        dp = dot3(d_o, uu, 1, 1) * dec
        db = dot3(two_parts(tinv[h]), two_parts(du), 0, 0)
        da = jnp.where(strict, -dot3(two_parts(db), uu, 1, 1), 0.0) * dec
        x = da * gram
        dbeta = jnp.sum(x, axis=1, keepdims=True) + jnp.sum(db * v, axis=1, keepdims=True)
        e = dp * qk + x * beta_c
        dcols[...] += jnp.where(lane == h, dbeta, 0.0) + jnp.where(
            lane == HEADS + h, jnp.sum(e, axis=1, keepdims=True), 0.0
        )
        drows[pl.ds(HEADS + h, 1), :] = jnp.sum(e, axis=0, keepdims=True)
        dact[:, vcols2] = beta_c * db
        dg = two_parts(da * beta_c)
        dpp = two_parts(dp)
        dq = dot3(dpp, kk)
        dk = dot3(dpp, qq, 0, 0) + dot3(dg, kk) + dot3(dg, kk, 0, 0)
        dact[:, kcols] = (rq * DK**-0.5) * (dq - qhat * jnp.sum(dq * qhat, axis=1, keepdims=True))
        dact[:, kcols2] = rk * (dk - k * jnp.sum(dk * k, axis=1, keepdims=True))

    def rates():
        dcum = jnp.where((lane >= HEADS) & (lane < 2 * HEADS), dcols[...] - drows[...].T, 0.0)
        ddecay = tri_dot((i <= j).astype(bf16), dcum)
        z = bd + bias[...]
        speed = -jnp.exp(rate[...]) * live_f
        dz = ddecay * speed * sigm(z)
        rate_grad[...] = jnp.sum(ddecay * speed * softplus(z), axis=0, keepdims=True)
        bias_grad[...] = jnp.sum(dz, axis=0, keepdims=True)
        dbeta_lin = dcols[...] * live_f * sig_b * (1.0 - sig_b)
        both = jnp.where(lane < HEADS, dbeta_lin, jnp.where(lane < 2 * HEADS, dz, 0.0))
        lin_grad[:, QKV + VALS : QKV + VALS + LANES] = both.astype(bf16)

    width = 384

    def conv_step(step, carry):
        cols = pl.ds(pl.multiple_of(step * width, width), width)
        x = lin[:, cols]
        pre = conv_chunk(x, taps, pos, cols)
        sg = sigm(pre)
        dc = dact[:, cols] * (sg + pre * sg * (1.0 - sg))
        dx = taps[0:1, cols] * dc
        tap_grad[0:1, cols] = jnp.sum(dc * x, axis=0, keepdims=True)
        for t in range(1, 4):
            masked = jnp.where(pos >= t, dc, 0.0)
            dx = dx + taps[t : t + 1, cols] * pltpu.roll(masked, n - t, 0)
            tap_grad[t : t + 1, cols] = jnp.sum(masked * pltpu.roll(x, t, 0), axis=0, keepdims=True)
        lin_grad[:, cols] = dx.astype(bf16)
        return carry

    def convolve(first, last):
        return lambda: lax.fori_loop(first, last, conv_step, 0)

    heads = [functools.partial(one_head, h) for h in range(HEADS)]
    total = QKV // width
    return clear, heads, rates, [convolve(0, total // 2), convolve(total // 2, total)]


MESH = pl.DeviceIdType.MESH


class Place:
    def __init__(self, n_shard, n_rep):
        self.n, self.reps = n_shard, n_rep
        self.ys = n_shard // 4
        self.r = lax.axis_index("rep")
        self.s = lax.axis_index("shard")
        self.c = self.s % 2
        self.x = (self.s // 2) % 2
        self.y = self.s // 4
        half = n_rep // 2
        low = self.r < half
        self.depth = jnp.where(low, self.r, n_rep - 1 - self.r)
        self.inner = jnp.where(low, self.r + 1, self.r - 1)
        self.outer = jnp.where(low, self.r - 1, self.r + 1)
        self.middle = self.depth == half - 1
        self.deep = self.depth > 0
        self.half = self.depth % 2

    def partner(self):
        return (self.r + 1 - 2 * (self.r % 2), self.s)

    def shard_id(self, y, x, c):
        return (self.r, (y * 2 + x) * 2 + c)

    def core_peer(self):
        return self.shard_id(self.y, self.x, 1 - self.c)

    def x_peer(self):
        return self.shard_id(self.y, 1 - self.x, self.c)

    def y_of(self, step):
        return (self.y + step) % self.ys

    def y_peer(self, step):
        return self.shard_id(self.y_of(step), self.x, self.c)


def remote(src, dst, send, recv, device):
    return pltpu.make_async_remote_copy(
        src_ref=src, dst_ref=dst, send_sem=send, recv_sem=recv, device_id=device, device_id_type=MESH
    )


def greet(place, with_rep):
    barrier = pltpu.get_barrier_semaphore()
    n = place.n
    for step in range(1, n):
        pl.semaphore_signal(
            barrier, inc=1, device_id=(place.r, (place.s + step) % n), device_id_type=MESH
        )
    if not with_rep:
        pl.semaphore_wait(barrier, n - 1)
        return
    for step in range(1, place.reps):
        pl.semaphore_signal(
            barrier, inc=1, device_id=((place.r + step) % place.reps, place.s), device_id_type=MESH
        )
    pl.semaphore_wait(barrier, n - 1 + place.reps - 1)


def add_into(dst, idx, *others):
    total = dst[idx].astype(f32)
    for ref, at in others:
        total = total + ref[at].astype(f32)
    dst[idx] = total.astype(dst.dtype)


RING = 10
ZRING = 12


def halved(rows):
    return (rows // 2) // 16 * 16


class Ring:
    def __init__(self, n, rows, cols, twins=1):
        self.n, self.rows, self.cols, self.twins = n, rows, cols, twins
        self.ys = n // 4
        self.count = 0

    def scratch(self):
        k, ys, cols = RING, self.ys, self.cols
        sems = pltpu.SemaphoreType.DMA
        per = 3 + 2 * (ys - 1)
        half = self.rows - halved(self.rows)
        return [
            pltpu.VMEM((k, ys, 2, 2, self.rows, cols), bf16),
            pltpu.VMEM((k, ys, 2, self.rows, cols), bf16),
            pltpu.VMEM((k, ys, half, cols), bf16),
            pltpu.VMEM((k, ys - 1, 2, half, cols), bf16),
            pltpu.VMEM((k, ys - 1, half, cols), bf16),
            pltpu.VMEM((k, half, cols), bf16),
            pltpu.VMEM((4, ZRING, self.twins, self.rows, cols), bf16),
            sems((k, per)),
            sems((k, per)),
            sems((ZRING, 6 + self.twins)),
        ]

    def bind(self, refs):
        (self.own, self.r0, self.r1a, self.r1b, self.r2a, self.r2b, self.z, self.send, self.recv, self.zsem) = refs


class Piece:
    def __init__(self, ring, place, rows, cols, out, out_cols):
        self.ring, self.p, self.rows = ring, place, rows
        self.twin = len(out_cols) == 2
        self.side = pl.ds(0, len(out_cols))
        self.slot, self.zslot = ring.count % RING, ring.count % ZRING
        ring.count += 1
        self.w = pl.ds(0, cols)
        self.ra = halved(rows)
        self.rb = rows - self.ra
        self.all_rows = pl.ds(0, rows)
        self.outs = [out.at[:, pl.ds(at, cols)] for at in out_cols]

    def own_view(self):
        return self.ring.own.at[self.slot, :, :, :, self.all_rows, self.w]

    def store_rows(self, value):
        ring = self.ring
        shaped = value.reshape(ring.ys, 2, 2, rinself.rows, value.shape[-1])
        ring.own[self.slot, :, :, :, self.all_rows, self.w] = shaped

    def send_core(self):
        g, p, k = self.ring, self.p, self.slot
        self.c0 = remote(
            g.own.at[k, :, :, 1 - p.c, self.all_rows, self.w], g.r0.at[k, :, :, self.all_rows, self.w],
            g.send.at[k, 0], g.recv.at[k, 0], p.core_peer(),
        )
        self.c0.start()

    def after_core(self):
        g, p, k, w = self.ring, self.p, self.slot, self.w
        rows = self.all_rows
        self.c0.wait()

        def step(q, carry):
            yy, xx = q // 2, q % 2
            add_into(g.own, (k, yy, xx, p.c, rows, w), (g.r0, (k, yy, xx, rows, w)))
            return carry

        lax.fori_loop(0, g.ys * 2, step, 0)
        top, low = pl.ds(0, self.ra), pl.ds(self.ra, self.rb)
        first, second = pl.ds(0, self.ra), pl.ds(0, self.rb)
        self.c1 = [
            remote(
                g.own.at[k, :, 1 - p.x, p.c, top, w], g.r1a.at[k, :, first, w],
                g.send.at[k, 1], g.recv.at[k, 1], p.x_peer(),
            )
        ]
        for d in range(1, g.ys):
            self.c1.append(
                remote(
                    g.own.at[k, p.y_of(d), :, p.c, low, w], g.r1b.at[k, d - 1, :, second, w],
                    g.send.at[k, 1 + d], g.recv.at[k, 1 + d], p.y_peer(d),
                )
            )
        for c in self.c1:
            c.start()

    def after_first(self):
        g, p, k, w = self.ring, self.p, self.slot, self.w
        top, low = pl.ds(0, self.ra), pl.ds(self.ra, self.rb)
        first, second = pl.ds(0, self.ra), pl.ds(0, self.rb)
        for c in self.c1:
            c.wait()
        for yy in range(g.ys):
            add_into(g.own, (k, yy, p.x, p.c, top, w), (g.r1a, (k, yy, first, w)))
        for xx in range(2):
            add_into(
                g.own, (k, p.y, xx, p.c, low, w),
                *[(g.r1b, (k, d, xx, second, w)) for d in range(g.ys - 1)],
            )
        self.c2 = [
            remote(
                g.own.at[k, p.y, 1 - p.x, p.c, low, w], g.r2b.at[k, second, w],
                g.send.at[k, 1 + g.ys], g.recv.at[k, 1 + g.ys], p.x_peer(),
            )
        ]
        for d in range(1, g.ys):
            self.c2.append(
                remote(
                    g.own.at[k, p.y_of(d), p.x, p.c, top, w], g.r2a.at[k, d - 1, first, w],
                    g.send.at[k, 1 + g.ys + d], g.recv.at[k, 1 + g.ys + d], p.y_peer(d),
                )
            )
        for c in self.c2:
            c.start()

    def after_second(self):
        g, p, k, w = self.ring, self.p, self.slot, self.w
        zk = self.zslot
        for c in self.c2:
            c.wait()
        top, low = pl.ds(0, self.ra), pl.ds(self.ra, self.rb)
        total = g.own[k, p.y, p.x, p.c, top, w].astype(f32)
        for d in range(g.ys - 1):
            total = total + g.r2a[k, d, 0 : self.ra, w].astype(f32)
        side = p.half if self.twin else 0
        g.z[0, zk, side, top, w] = total.astype(bf16)
        total = g.own[k, p.y, p.x, p.c, low, w].astype(f32) + g.r2b[k, 0 : self.rb, w].astype(f32)
        g.z[0, zk, side, low, w] = total.astype(bf16)
        if self.twin:
            g.z[0, zk, 1 - side, self.all_rows, w] = jnp.zeros((self.rows, w.size), bf16)
        z = lambda i: g.z.at[i, zk, self.side, self.all_rows, w]
        target = lambda r: (r, p.s)
        sem = g.zsem
        self.up = remote(z(0), z(1), sem.at[zk, 0], sem.at[zk, 1], target(p.inner))
        self.meet = remote(z(0), z(2), sem.at[zk, 2], sem.at[zk, 3], target(p.inner))
        self.down = remote(z(3), z(2), sem.at[zk, 4], sem.at[zk, 3], target(p.outer))
        self.home = [
            pltpu.make_async_copy(g.z.at[3, zk, i, self.all_rows, w], out, sem.at[zk, 6 + i])
            for i, out in enumerate(self.outs)
        ]

        @pl.when(p.depth == 0)
        def _():
            self.send_inward()

    def send_inward(self):
        p = self.p

        @pl.when(p.middle)
        def _():
            self.meet.start()

        @pl.when(jnp.logical_not(p.middle))
        def _():
            self.up.start()

    def after_up(self):
        g, p, zk, w = self.ring, self.p, self.zslot, self.w

        @pl.when(p.deep)
        def _():
            self.up.wait_recv()
            for i in range(len(self.outs)):
                add_into(g.z, (0, zk, i, self.all_rows, w), (g.z, (1, zk, i, self.all_rows, w)))
            self.send_inward()

    def finish(self, middle):
        g, p, zk, w = self.ring, self.p, self.zslot, self.w
        rows = self.all_rows

        @pl.when(p.middle if middle else jnp.logical_not(p.middle))
        def _():
            self.meet.wait_recv()
            for i in range(len(self.outs)):
                if middle:
                    both = g.z[0, zk, i, rows, w].astype(f32) + g.z[2, zk, i, rows, w].astype(f32)
                    g.z[3, zk, i, rows, w] = both.astype(bf16)
                else:
                    g.z[3, zk, i, rows, w] = g.z[2, zk, i, rows, w]

            @pl.when(p.deep)
            def _():
                self.down.start()

            for c in self.home:
                c.start()

    def close(self):
        p = self.p

        @pl.when(p.middle)
        def _():
            self.meet.wait_send()

        @pl.when(jnp.logical_not(p.middle))
        def _():
            self.up.wait_send()

        @pl.when(p.deep)
        def _():
            self.down.wait_send()

        for c in self.home:
            c.wait()


def pump(pieces, index):
    stages = [
        (2, lambda q: q.after_core()),
        (18, lambda q: q.close()),
        (17, lambda q: q.finish(False)),
        (14, lambda q: q.finish(True)),
        (11, lambda q: q.after_up()),
        (8, lambda q: q.after_second()),
        (5, lambda q: q.after_first()),
    ]
    for lag, act in stages:
        if 0 <= index - lag < len(pieces):
            act(pieces[index - lag])


class Small:
    def __init__(self, n, reps, rows, cols):
        self.n, self.ys, self.reps = n, n // 4, reps
        self.sizes = (2, 2, self.ys, reps)
        self.rows, self.cols = rows, cols

    def scratch(self):
        total = sum(self.sizes)
        return [
            pltpu.VMEM((total, self.rows, self.cols), f32),
            pltpu.SemaphoreType.DMA((total,)),
            pltpu.SemaphoreType.DMA((total,)),
        ]

    def bind(self, refs):
        self.buf, self.send, self.recv = refs

    def begin(self, place, axis, value):
        base = sum(self.sizes[:axis])
        size = self.sizes[axis]
        p = place
        mine = (p.c, p.x, p.y, p.r)[axis]
        slot = self.buf.at[base + mine]
        slot[...] = value
        self.copies = []
        for d in range(1, size):
            at = (mine + d) % size
            device = (
                p.shard_id(p.y, p.x, at), p.shard_id(p.y, at, p.c), p.shard_id(at, p.x, p.c), (at, p.s),
            )[axis]
            self.copies.append(remote(slot, slot, self.send.at[base + d], self.recv.at[base + d], device))
        for c in self.copies:
            c.start()

    def end(self, axis):
        base = sum(self.sizes[:axis])
        for c in self.copies:
            c.wait()
        total = self.buf[base]
        for d in range(1, self.sizes[axis]):
            total = total + self.buf[base + d]
        return total


class Flow:
    @staticmethod
    def count(ys, pair):
        return 5 + 12 * (ys - 1) if pair else 3 + 6 * (ys - 1)

    def __init__(self, place, src, src_at, cols, dst, dst_at, pair, send, recv, base, mine):
        self.p, self.rows, self.pair = place, src.shape[0], pair
        self.src_ref, self.src_at, self.dst, self.dst_at, self.width = src, src_at, dst, dst_at, cols
        self.send, self.recv, self.base, self.used = send, recv, base, 0
        self.ra = halved(self.rows)
        self.part = (place.r % 2) if pair else None
        whole = self.src_ref.at[:, self.columns(src_at, None)]
        self.mine = pltpu.make_async_copy(whole, self.region(place.y, place.x, place.c), mine)
        self.whole = whole
        self.all = []

    def columns(self, at, part):
        if part is None:
            return pl.ds(at if isinstance(at, int) else pl.multiple_of(at, LANES), self.width)
        half = self.width // 2
        return pl.ds(pl.multiple_of(at + part * half, LANES), half)

    def region(self, y, x, c, half=None, part=None):
        start = ((y * 2 + x) * 2 + c) * self.rows
        size = self.rows
        if half == 0:
            size = self.ra
        elif half == 1:
            start, size = start + self.ra, self.rows - self.ra
        return self.dst.at[pl.ds(pl.multiple_of(start, 16), size), self.columns(self.dst_at, part)]

    def copy(self, dst, device, src=None):
        at = self.base + self.used
        self.used += 1
        c = remote(dst if src is None else src, dst, self.send.at[at], self.recv.at[at], device)
        c.start()
        self.all.append(c)
        return c

    def begin(self):
        p = self.p
        own = self.region(p.y, p.x, p.c, None, self.part)
        src = self.src_ref.at[:, self.columns(self.src_at, self.part)]
        self.mine.start()
        self.from_x = self.copy(own, p.x_peer(), src)
        self.from_y = [self.copy(own, p.y_peer(d), src) for d in range(1, p.ys)]
        self.from_core = [self.copy(self.region(p.y, p.x, p.c), p.core_peer(), self.whole)]
        self.from_z, self.z_regions = [], []

    def share(self, *where):
        p = self.p
        if self.pair:
            self.from_z.append(self.copy(self.region(*where, self.part), (p.r + 1 - 2 * (p.r % 2), p.s)))
            self.z_regions.append(where)
        self.from_core.append(self.copy(self.region(*where, self.part), p.core_peer()))

    def forward(self):
        p = self.p
        steps = range(1, p.ys)
        self.from_x.wait_recv()
        self.diag = [self.copy(self.region(p.y, 1 - p.x, p.c, 0, self.part), p.y_peer(d)) for d in steps]
        self.share(p.y, 1 - p.x, p.c, None)
        for d in steps:
            self.from_y[d - 1].wait_recv()
            back = p.y_of(p.ys - d)
            self.diag.append(self.copy(self.region(back, p.x, p.c, 1, self.part), p.x_peer()))
            self.share(back, p.x, p.c, None)

    def relay(self):
        p = self.p
        for i, c in enumerate(self.diag):
            c.wait_recv()
            half, d = divmod(i, p.ys - 1)
            self.share(p.y_of(p.ys - d - 1), 1 - p.x, p.c, half)

    def swap(self):
        for c, where in zip(self.from_z, self.z_regions):
            c.wait_recv()
            self.from_core.append(self.copy(self.region(*where, 1 - self.part), self.p.core_peer()))

    def done(self):
        for c in self.from_core:
            c.wait_recv()
        self.mine.wait()

    def close(self):
        for c in self.all:
            c.wait_send()


FTILE = 256
FF_TILE = 512


def cuts(total, step):
    return [(at, min(step, total - at)) for at in range(0, total, step)]


def decay_lanes(words):
    lane = lax.broadcasted_iota(jnp.int32, (1, LANES), 1)
    total = jnp.zeros((1, LANES), f32)
    for h in range(HEADS):
        total = jnp.where(lane == HEADS + h, words[h], total)
    return total


def one_hot_rows(values, count):
    return lax.broadcasted_iota(jnp.int32, (count, values.shape[1]), 0) == values


class Store:
    def __init__(self, sem):
        self.sem, self.all = sem, []

    def put(self, src, dst):
        c = pltpu.make_async_copy(src, dst, self.sem.at[len(self.all)])
        c.start()
        self.all.append(c)

    def wait(self):
        for c in self.all:
            c.wait()


FORWARD_SAVED = (
    ("xin", lambda n, d, f: ((n, d), bf16)),
    ("dy", lambda n, d, f: ((2 * n, d), bf16)),
    ("normed_t", lambda n, d, f: ((d, n), bf16)),
    ("lin", lambda n, d, f: ((n, QKV + VALS + LANES), f32)),
    ("act", lambda n, d, f: ((n, QKV), f32)),
    ("cum", lambda n, d, f: ((n, LANES), f32)),
    ("cum_t", lambda n, d, f: ((LANES, n), f32)),
    ("tinv", lambda n, d, f: ((HEADS, n, n), f32)),
    ("fresh", lambda n, d, f: ((n, VALS), f32)),
    ("heads", lambda n, d, f: ((n, VALS), f32)),
    ("mixed_t", lambda n, d, f: ((VALS, n), bf16)),
    ("middle", lambda n, d, f: ((n, d), f32)),
    ("normed_mid_t", lambda n, d, f: ((d, 2 * n), bf16)),
    ("hidden_t", lambda n, d, f: ((f // 2, 2 * n), bf16)),
    ("grads_gu", lambda n, d, f: ((2 * n, f), bf16)),
    ("pick", lambda n, d, f: ((n, n), bf16)),
    ("place", lambda n, d, f: ((n, n), bf16)),
    ("params", lambda n, d, f: ((16, d), f32)),
    ("taps", lambda n, d, f: ((4, QKV), f32)),
)


def transposed(a):
    return a.T.astype(bf16)


def forward_kernel(n_shard, reps, *refs):
    take = iter(refs)
    get = lambda k: [next(take) for _ in range(k)]
    offs, lens, rates_in, bias_in, tokens, cot, deal, small_in = get(8)
    wq, wk, wv, wt, wb, wo, wg, wu, wd = get(9)
    gp, go, gg, gu, gd = get(5)
    outs = dict(zip([name for name, _ in FORWARD_SAVED], get(len(FORWARD_SAVED))))
    kept = dict(zip([name for name, _ in FORWARD_SAVED], get(len(FORWARD_SAVED))))
    (dealt, dsend, drecv, smalls, ssend, srecv, sent, come, tsend, trecv, wbuf, wobuf, wdbuf, load_sem, fsend, frecv,
     mine_sem, out_sem, normed, mixed, normed_mid) = get(21)
    shards, shard_sem, zsend, zrecv = get(9), *get(3)
    rate, bias = get(2)
    rate[...], bias[...] = decay_lanes(rates_in), decay_lanes(bias_in)
    own_loads = []
    for k, (w, v) in enumerate(zip((wq, wk, wv, wt, wb, wo, wd, wg, wu), shards)):
        own_loads.append(pltpu.make_async_copy(w, v, shard_sem.at[k]))
        own_loads[-1].start()
    wq, wk, wv, wt, wb, wo, wd, wg, wu = shards
    rows, width = tokens.shape
    per = rows // n_shard
    place = Place(n_shard, reps)
    p = place
    greet(place, True)
    offsets = [offs[i] for i in range(offs.shape[0])]
    lengths = [lens[i] for i in range(lens.shape[0])]
    store = Store(out_sem)

    dealt[p.s] = jnp.broadcast_to(deal[...], (8, rows))
    smalls[p.s] = small_in[...]
    first = []
    for d in range(1, n_shard):
        to = (p.r, (p.s + d) % n_shard)
        first.append(remote(dealt.at[p.s], dealt.at[p.s], dsend.at[d], drecv.at[d], to))
        first[-1].start()
    for d in range(1, n_shard):
        to = (p.r, (p.s + d) % n_shard)
        first.append(remote(smalls.at[p.s], smalls.at[p.s], ssend.at[d], srecv.at[d], to))
        first[-1].start()

    made = []

    def flow(src, at, cols, dst, dst_at, pair):
        k = len(made)
        base = sum(Flow.count(p.ys, f.pair) for f in made)
        made.append(Flow(place, src, at, cols, dst, dst_at, pair, fsend, frecv, base, mine_sem.at[k]))
        return made[-1]

    ff = wg.shape[1]
    half = ff // 2
    ff_cuts = cuts(half, FF_TILE)
    stages = [
        [flow(wq, 0, KEYS, gp, 0, True), flow(wk, 0, KEYS, gp, KEYS, True), flow(wb, 0, LANES, gp, QKV + VALS, False)],
        [flow(wv, 0, VALS, gp, 2 * KEYS, True)],
        [flow(wt, 0, VALS, gp, QKV, False)],
        [flow(wo, 0, width, go, 0, True)],
        [flow(wd, 0, width // 2, gd, 0, False)],
        [flow(wd, width // 2, width // 2, gd, width // 2, False)],
    ]
    for at, cols in ff_cuts:
        stages.append([flow(wg, p.half * half + at, cols, gg, at, False), flow(wu, p.half * half + at, cols, gu, at, False)])
    last = len(stages) - 1

    events = []
    for k in range(len(stages) + 5):
        for lag, act in ((0, "begin"), (2, "forward"), (3, "relay"), (4, "swap"), (5, "done")):
            if 0 <= k - lag < len(stages):
                events.append((act, k - lag))
    owned = set()

    def poll(count=1):
        for _ in range(count):
            if events:
                act, k = events.pop(0)
                for f in stages[k]:
                    if act == "begin" and id(f.src_ref) not in owned:
                        owned.add(id(f.src_ref))
                        own_loads[[id(v) for v in shards].index(id(f.src_ref))].wait()
                    getattr(f, act)()

    def until(act, k):
        while (act, k) in events:
            poll()

    until("begin", 1)

    loads = {}

    def load(name, src, dst):
        loads[name] = pltpu.make_async_copy(src, dst, load_sem.at[len(loads)])
        loads[name].start()

    for c in first[: n_shard - 1]:
        c.wait_recv()
    i = lax.broadcasted_iota(jnp.int32, (rows, rows), 0)
    j = lax.broadcasted_iota(jnp.int32, (rows, rows), 1)
    upper = (i <= j).astype(bf16)
    everyone = dealt[:, 0, :]
    to_me = (everyone // rows) == p.s
    rank = dot(to_me.astype(f32).astype(bf16), upper).astype(jnp.int32) - 1
    rank = jnp.where(to_me, rank, -1)
    for b in range(n_shard):
        picked = one_hot_rows(rank[b : b + 1, :], per).astype(f32).astype(bf16)
        which = one_hot_rows(everyone[b : b + 1, :] % rows, rows).astype(f32).astype(bf16)
        kept["pick"][b * per : (b + 1) * per, :] = dot(picked, which, 1, 1).astype(bf16)
    pick = kept["pick"][...]
    exchange = []
    for a, src in enumerate((tokens, cot)):
        for at in range(0, width, 256):
            sent[a, :, at : at + 256] = dot(pick, src[:, at : at + 256]).astype(bf16)
        for d in range(1, n_shard):
            t = (p.s + d) % n_shard
            exchange.append(
                remote(
                    sent.at[a, pl.ds(pl.multiple_of(t * per, 16), per)],
                    come.at[a, pl.ds(pl.multiple_of(p.s * per, 16), per)],
                    tsend.at[a, d], trecv.at[a, d], (p.r, t),
                )
            )
            exchange[-1].start()
        here = pl.ds(pl.multiple_of(p.s * per, 16), per)
        come[a, here, :] = sent[a, here, :]
    mine = deal[0:1, :]
    source = mine // rows
    from_each = one_hot_rows(source, n_shard)
    cum = dot(from_each.astype(f32).astype(bf16), upper)
    slot = jnp.sum(jnp.where(from_each, cum, 0.0), axis=0, keepdims=True).astype(jnp.int32) - 1 + source * per
    kept["place"][...] = one_hot_rows(slot, rows).astype(f32).astype(bf16)
    store.put(kept["pick"], outs["pick"])
    store.put(kept["place"], outs["place"])

    for c in first[n_shard - 1 :]:
        c.wait_recv()
    total = smalls[0].astype(f32)
    for t in range(1, n_shard):
        total = total + smalls[t].astype(f32)
    kept["params"][...] = total
    for t in range(4):
        for g in range(QKV // width):
            row = t * (QKV // width) + g
            kept["taps"][t : t + 1, g * width : (g + 1) * width] = total[row : row + 1, :]
    gain1, gain2 = kept["params"].at[12:13, :], kept["params"].at[13:14, :]
    gain_o = kept["params"].at[14:15, 0:DVH]
    store.put(kept["params"], outs["params"])
    store.put(kept["taps"], outs["taps"])

    def unpack(a, name):
        for c in exchange[a * (n_shard - 1) : (a + 1) * (n_shard - 1)]:
            c.wait_recv()
        for at in range(0, width, 256):
            kept[name][0:rows, at : at + 256] = dot(kept["place"][...], come[a, :, at : at + 256], 0, 0).astype(bf16)
    unpack(0, "xin")
    store.put(kept["xin"], outs["xin"])

    def swap_rows(ref, k):
        c = remote(ref.at[pl.ds(0, rows)], ref.at[pl.ds(rows, rows)], zsend.at[k], zrecv.at[k], p.partner())
        c.start()
        return c

    x = kept["xin"][...].astype(f32)
    norm = x * lax.rsqrt(jnp.mean(x * x, axis=1, keepdims=True) + 1e-5) * gain1[...]
    normed[...] = norm.astype(bf16)

    def project(at, cols, tile):
        def step(k, carry):
            here = pl.ds(pl.multiple_of(at + k * tile, 128), tile)
            kept["lin"][:, here] = dot(normed[...], wbuf[:, here])
            return carry

        lax.fori_loop(0, cols // tile, step, 0)

    def fetch(name, at, cols):
        here = pl.ds(at, cols)
        load(name, gp.at[:, here], wbuf.at[:, here])

    until("done", 0)
    fetch("qk", 0, 2 * KEYS)
    fetch("bd", QKV + VALS, LANES)
    until("done", 1)
    fetch("v", 2 * KEYS, VALS)
    loads["qk"].wait()
    loads["bd"].wait()
    project(0, 2 * KEYS, 256)
    project(QKV + VALS, LANES, LANES)
    poll(1)
    loads["v"].wait()
    project(2 * KEYS, VALS, 256)
    until("done", 2)
    fetch("gate", QKV, VALS)
    convolve, heads = mixer_forward(
        rows, offsets, lengths, kept["lin"], kept["taps"], rate, bias, gain_o, kept["act"], kept["cum"],
        kept["cum_t"], kept["tinv"], kept["fresh"], kept["heads"], mixed,
    )
    convolve()
    unpack(1, "dy")
    dy_swap = swap_rows(kept["dy"], 0)
    loads["gate"].wait()
    project(QKV, VALS, 256)
    store.put(kept["lin"], outs["lin"])
    for h in range(0, HEADS, 2):
        heads[h]()
        heads[h + 1]()
        poll(6)
    until("done", 3)
    load("out", go, wobuf)
    for name in ("act", "cum", "cum_t", "tinv", "fresh", "heads"):
        store.put(kept[name], outs[name])
    loads["out"].wait()

    def out_step(k, carry):
        here = pl.ds(pl.multiple_of(k * 256, 256), 256)
        kept["middle"][:, here] = kept["xin"][:, here].astype(f32) + dot(mixed[...], wobuf[:, here])
        return carry

    lax.fori_loop(0, width // 256, out_step, 0)
    store.put(kept["middle"], outs["middle"])
    m = kept["middle"][...]
    norm = m * lax.rsqrt(jnp.mean(m * m, axis=1, keepdims=True) + 1e-5) * gain2[...]
    normed_mid[0:rows, :] = norm.astype(bf16)
    mid_swap = swap_rows(normed_mid, 1)
    kept["normed_mid_t"][:, 0:rows] = transposed(norm)
    kept["mixed_t"][...] = transposed(mixed[...].astype(f32))
    store.put(kept["mixed_t"], outs["mixed_t"])
    until("done", 5)
    load("down", gd.at[pl.ds(pl.multiple_of(p.half * half, LANES), half)], wdbuf)

    def ffn(k, at, cols):
        some = slice(k * rows, (k + 1) * rows)
        here, there = slice(at, at + cols), slice(half + at, half + at + cols)
        grad = dot(kept["dy"][some, :], wdbuf[here, :], 1, 1)
        gate = dot(normed_mid[some, :], wbuf[:, here])
        up = dot(normed_mid[some, :], wbuf[:, there])
        sg = sigm(gate)
        silu = gate * sg
        hid = silu * up
        kept["hidden_t"][here, some] = transposed(hid)
        kept["grads_gu"][some, here] = (grad * up * (sg + silu * (1.0 - sg))).astype(bf16)
        kept["grads_gu"][some, there] = (grad * silu).astype(bf16)

    loads["down"].wait()
    for i, (at, cols) in enumerate(ff_cuts):
        until("done", last - len(ff_cuts) + 1 + i)
        load(("g", i), gg.at[:, pl.ds(at, cols)], wbuf.at[:, pl.ds(at, cols)])
        load(("u", i), gu.at[:, pl.ds(at, cols)], wbuf.at[:, pl.ds(half + at, cols)])
        poll(2)
        loads[("g", i)].wait()
        loads[("u", i)].wait()
        ffn(0, at, cols)
    kept["normed_t"][...] = transposed(normed[...].astype(f32))
    store.put(kept["normed_t"], outs["normed_t"])
    dy_swap.wait()
    mid_swap.wait()
    store.put(kept["dy"], outs["dy"])
    for at, cols in ff_cuts:
        ffn(1, at, cols)
    kept["normed_mid_t"][:, rows : 2 * rows] = transposed(normed_mid[rows : 2 * rows, :].astype(f32))
    store.put(kept["normed_mid_t"], outs["normed_mid_t"])
    for name in ("hidden_t", "grads_gu"):
        store.put(kept[name], outs[name])
    for c in first + exchange:
        c.wait_send()
    for f in made:
        f.close()
    store.wait()


def forward_call(n_shard, reps, offs, lens, tokens, cot, deal, small_in, rate, bias, weights):
    anywhere = pl.BlockSpec(memory_space=pl.ANY)
    held = pl.BlockSpec(memory_space=pltpu.VMEM)
    words = pl.BlockSpec(memory_space=pltpu.SMEM)
    rows, width = tokens.shape
    ff = weights[6].shape[1]
    sd = jax.ShapeDtypeStruct
    wide = QKV + VALS + LANES
    vals_rows, ff_rows = weights[5].shape[0] * n_shard, weights[8].shape[0] * n_shard
    gathered = [
        sd((width, wide), bf16), sd((vals_rows, width), bf16), sd((width, ff // 2), bf16), sd((width, ff // 2), bf16),
        sd((ff_rows, width), bf16),
    ]
    shapes = [fn(rows, width, ff) for _, fn in FORWARD_SAVED]
    sems = pltpu.SemaphoreType.DMA
    flows = 8 + 2 * len(cuts(ff // 2, FF_TILE))
    count = flows * Flow.count(n_shard // 4, True)
    scratch = [pltpu.VMEM(s, d) for s, d in shapes] + [
        pltpu.VMEM((n_shard, 8, rows), jnp.int32), sems((n_shard,)), sems((n_shard,)),
        pltpu.VMEM((n_shard, 16, width), bf16), sems((n_shard,)), sems((n_shard,)),
        pltpu.VMEM((2, rows, width), bf16), pltpu.VMEM((2, rows, width), bf16), sems((2, n_shard)), sems((2, n_shard)),
        pltpu.VMEM((width, wide), bf16), pltpu.VMEM((vals_rows, width), bf16), pltpu.VMEM((ff_rows // 2, width), bf16),
        sems((16,)), sems((count,)), sems((count,)), sems((flows,)), sems((len(shapes),)),
        pltpu.VMEM((rows, width), bf16), pltpu.VMEM((rows, VALS), bf16), pltpu.VMEM((2 * rows, width), bf16),
    ]
    scratch += [pltpu.VMEM(weights[k].shape, bf16) for k in (0, 1, 2, 3, 4, 5, 8, 6, 7)] + [sems((9,)), sems((2,)), sems((2,))]
    scratch += [pltpu.VMEM((1, LANES), f32)] * 2
    res = pl.pallas_call(
        functools.partial(forward_kernel, n_shard, reps),
        in_specs=[words] * 4 + [held] * 4 + [anywhere] * 9,
        out_specs=[anywhere] * (5 + len(shapes)),
        out_shape=gathered + [sd(s, d) for s, d in shapes],
        scratch_shapes=scratch,
        compiler_params=pltpu.CompilerParams(collective_id=1, has_side_effects=True, vmem_limit_bytes=62 << 20),
    )(offs, lens, rate, bias, tokens, cot, deal, small_in, *weights)
    return res[:5], dict(zip([name for name, _ in FORWARD_SAVED], res[5:]))


WIDE = 512
PIECE = 256


class Stream:
    def __init__(self, buf, sem, parts):
        self.buf, self.sem, self.parts, self.at = buf, sem, parts, 0
        self.copies = {}

    def start(self):
        self.issue(0)

    def issue(self, k):
        if k < len(self.parts):
            pairs = self.parts[k](self.buf.at[k % 2])
            self.copies[k] = [pltpu.make_async_copy(s, d, self.sem.at[k % 2, i]) for i, (s, d) in enumerate(pairs)]
            for c in self.copies[k]:
                c.start()

    def take(self):
        k = self.at
        self.at += 1
        self.issue(k + 1)
        for c in self.copies[k]:
            c.wait()
        return k, self.buf.at[k % 2]


BACK_KEPT = tuple(name for name, _ in FORWARD_SAVED)


def backward_kernel(n_shard, reps, rings, small, *refs):
    take = iter(refs)
    get = lambda k: [next(take) for _ in range(k)]
    offs, lens, rates_in, bias_in = get(4)
    gp, go, gg, gu, gd = get(5)
    given = dict(zip(BACK_KEPT, get(len(BACK_KEPT))))
    o_rows, o_grad, o_ffn, o_down, o_out, o_proj, o_small = get(7)
    kept = dict(zip(BACK_KEPT, get(len(BACK_KEPT))))
    (ring,) = rings
    ring.bind(get(10))
    small.bind(get(3))
    (load_sem, wbuf, wsem, nbuf, nsem, acc, middle_grad, branch, mix_grad, dcols, drows, lin_grad, tap_grad, gain_grad,
     rate_grad, bias_grad, small_v, sent, come, tsend, trecv, rows_out, out_sem, swaps, zsend, zrecv, block, rate, bias) = get(29)
    rate[...], bias[...] = decay_lanes(rates_in), decay_lanes(bias_in)
    rows, width = kept["xin"].shape
    half = gg.shape[1]
    ff = 2 * half
    per = rows // n_shard
    place = Place(n_shard, reps)
    p = place
    offsets = [offs[i] for i in range(offs.shape[0])]
    lengths = [lens[i] for i in range(lens.shape[0])]
    loads = {}
    order = (
        "normed_mid_t", "grads_gu", "middle", "dy", "params", "hidden_t", "cum", "cum_t", "tinv", "fresh", "heads",
        "act", "lin", "taps", "mixed_t", "normed_t", "xin", "pick", "place",
    )
    for k, name in enumerate(order):
        loads[name] = pltpu.make_async_copy(given[name], kept[name], load_sem.at[k])
        loads[name].start()
    have = set()

    def need(*names):
        for name in names:
            if name not in have:
                have.add(name)
                loads[name].wait()

    greet(place, True)
    pieces = []

    def tick(piece=None, fill=None):
        index = tick.index
        tick.index += 1
        pump(pieces, index)
        if piece is not None:
            pieces.append(piece())
            fill(pieces[-1])
            pieces[-1].send_core()

    tick.index = 0

    size = width // n_shard

    def wide_piece(left, right, right_at, cols, out, out_at):
        def fill(piece):
            value = dot(left[...], right[:, right_at : right_at + cols]).astype(bf16)
            ring.own[piece.slot, :, :, :, :, 0:cols] = value.reshape(ring.ys, 2, 2, size, cols)

        tick(lambda: Piece(ring, place, size, cols, out, out_at), fill)

    def block_piece(left, right, at, cols, first, count, out):
        total = left.shape[0]
        long = out.shape[0]
        held = total // long
        ys = held // 4

        def fill(piece):
            if first == 0:
                block[0:total, 0:cols] = dot(left[...], right[:, at : at + cols]).astype(bf16)
            for t in range(held):
                y = t // 4 if held == n_shard else p.half * ys + t // 4
                part = block[t * long + first : t * long + first + count, 0:cols]
                ring.own[piece.slot, y, (t // 2) % 2, t % 2, 0:count, 0:cols] = part
            if held < n_shard:
                for t in range(held):
                    y = (1 - p.half) * ys + t // 4
                    ring.own[piece.slot, y, (t // 2) % 2, t % 2, 0:count, 0:cols] = jnp.zeros((count, cols), bf16)

        tick(lambda: Piece(ring, place, count, cols, out.at[pl.ds(first, count)], (at,)), fill)

    queue = []

    def run(count=1):
        for _ in range(count):
            queue.pop(0)()

    gu_cuts = [(side, at, cols) for side in (0, 1) for at, cols in cuts(half, WIDE)]

    def gu_piece(side, at, cols):
        need("normed_mid_t", "grads_gu")
        outs = (side * ff + at, side * ff + half + at)
        wide_piece(kept["normed_mid_t"], kept["grads_gu"], side * half + at, cols, o_ffn, outs)

    def down_piece(at, first, count):
        need("hidden_t", "dy")
        block_piece(kept["hidden_t"], kept["dy"], at, PIECE, first, count, o_down)

    def out_piece(at, first, count):
        need("mixed_t")
        block_piece(kept["mixed_t"], branch, at, PIECE, first, count, o_out)

    def proj_piece(at, cols):
        need("normed_t")
        wide_piece(kept["normed_t"], lin_grad, at, cols, o_proj, (at,))

    def blocks(fn, out):
        return [
            functools.partial(fn, at, first, count) for at, _ in cuts(width, PIECE) for first, count in cuts(out.shape[0], size)
        ]

    sided = [functools.partial(gu_piece, side, at, cols) for side in (0, 1) for at, cols in cuts(half, PIECE)]
    downs = blocks(down_piece, o_down)
    while sided or downs:
        queue.extend(sided[:1] + downs[:1])
        del sided[:1], downs[:1]
    queue.extend(blocks(out_piece, o_out))
    wide = cuts(QKV + VALS, PIECE)
    late = QKV // PIECE
    for at, cols in wide[late:] + wide[:late] + [(QKV + VALS, LANES)]:
        queue.append(functools.partial(proj_piece, at, cols))

    def gu_part(k):
        side, at, cols = gu_cuts[k]
        return lambda b: [((gg, gu)[side].at[:, pl.ds(at, cols)], b.at[:, pl.ds(0, cols)])]

    gu_stream = Stream(wbuf, wsem, [gu_part(k) for k in range(len(gu_cuts))])

    def gnm(count):
        need("grads_gu")
        for _ in range(count):
            k, buf = gu_stream.take()
            side, at, cols = gu_cuts[k]
            at = side * half + at
            part = dot(kept["grads_gu"][:, at : at + cols], buf[:, 0:cols], 1, 1)
            acc[...] = part if k == 0 else acc[...] + part

    def to_partner(k):
        swaps[0] = acc[rows : 2 * rows, :].astype(bf16)
        c = remote(swaps.at[0], swaps.at[1 + k], zsend.at[k], zrecv.at[k], p.partner())
        c.start()
        return c

    def norm_back(values, gain, upstream):
        n = lax.rsqrt(jnp.mean(values * values, axis=1, keepdims=True) + 1e-5)
        u = upstream * gain
        gain_part = jnp.sum(upstream * values * n, axis=0, keepdims=True)
        return n * (u - values * (n * n) * jnp.mean(u * values, axis=1, keepdims=True)), gain_part

    def norm2():
        need("middle", "dy", "params")
        mid_swap.wait()
        upstream = acc[0:rows, :] + swaps[1].astype(f32)
        back, gain_part = norm_back(kept["middle"][...], kept["params"][13:14, :], upstream)
        small_v[13:14, :] = gain_part
        total = kept["dy"][0:rows, :].astype(f32) + back
        middle_grad[...] = total
        branch[...] = total.astype(bf16)

    def row_part(src, k):
        return lambda b: [(src.at[pl.ds(k * FTILE, FTILE), :], b)]

    out_stream = Stream(nbuf, nsem, [row_part(go, k) for k in range(VALS // FTILE)])
    down_cuts = cuts(half, FTILE)

    def down_part(at, size):
        start = pl.multiple_of(p.half * half + at, LANES)
        return lambda b: [(gd.at[pl.ds(start, size), :], b.at[pl.ds(0, size)])]

    down_stream = Stream(nbuf, nsem, [down_part(at, size) for at, size in down_cuts])

    def grad_mixed(count):
        for _ in range(count):
            k, buf = out_stream.take()
            mix_grad[:, k * FTILE : (k + 1) * FTILE] = dot(branch[...], buf[...], 1, 1)

    def result(count):
        need("hidden_t", "middle")
        for _ in range(count):
            k, buf = down_stream.take()
            at, size = down_cuts[k]
            part = dot(kept["hidden_t"][at : at + size, :], buf[0:size, :], 0, 0)
            acc[...] = part if k == 0 else acc[...] + part

    exchange = {}

    def send_home(a, value):
        need("place")
        here = pl.ds(pl.multiple_of(p.s * per, 16), per)
        for at in range(0, width, 256):
            sent[a, :, at : at + 256] = dot(kept["place"][...], value[:, at : at + 256]).astype(bf16)
        exchange[a] = []
        for d in range(1, n_shard):
            t = (p.s + d) % n_shard
            exchange[a].append(
                remote(
                    sent.at[a, pl.ds(pl.multiple_of(t * per, 16), per)], come.at[a, here],
                    tsend.at[a, d], trecv.at[a, d], (p.r, t),
                )
            )
            exchange[a][-1].start()
        come[a, here, :] = sent[a, here, :]

    stores = []

    def arrive(a, out):
        need("pick")
        for c in exchange[a]:
            c.wait()
        for at in range(0, width, 256):
            rows_out[a, :, at : at + 256] = dot(kept["pick"][...], come[a, :, at : at + 256], 0, 0).astype(bf16)
        stores.append(pltpu.make_async_copy(rows_out.at[a], out, out_sem.at[a]))
        stores[-1].start()

    def wide_part(at, cols):
        return lambda b: [(gp.at[:, pl.ds(at, cols)], b.at[:, pl.ds(0, cols)])]

    proj_cuts = [(at, WIDE) for at in range(0, QKV + VALS, WIDE)] + [(QKV + VALS, LANES)]
    proj_stream = Stream(wbuf, wsem, [wide_part(at, cols) for at, cols in proj_cuts])

    def grad_normed(count):
        for _ in range(count):
            k, buf = proj_stream.take()
            at, cols = proj_cuts[k]
            part = dot(lin_grad[:, at : at + cols], buf[:, 0:cols], 1, 1)
            acc[0:rows, :] = part if k == 0 else acc[0:rows, :] + part

    def norm1():
        need("xin")
        back, gain_part = norm_back(kept["xin"][...].astype(f32), kept["params"][12:13, :], acc[0:rows, :])
        small_v[12:13, :] = gain_part
        rows_out[1] = (middle_grad[...] + back).astype(bf16)

    def pack_small():
        small_v[14:16, :] = jnp.zeros((2, width), f32)
        for t in range(4):
            for g in range(QKV // width):
                row = t * (QKV // width) + g
                small_v[row : row + 1, :] = tap_grad[t : t + 1, g * width : (g + 1) * width]
        small_v[14:15, 0:DVH] = gain_grad[...]
        small_v[14:15, DVH : DVH + LANES] = rate_grad[...]
        small_v[14:15, DVH + LANES : DVH + 2 * LANES] = bias_grad[...]

    gu_stream.start()
    out_stream.start()
    for _ in gu_cuts:
        run()
        gnm(1)
    mid_swap = to_partner(0)
    run(6)
    need("cum", "cum_t", "tinv", "fresh", "heads", "act", "lin", "taps")
    clear, heads, rates, convs = mixer_backward(
        rows, offsets, lengths, kept["lin"], kept["taps"], rate, bias, kept["params"].at[14:15, 0:DVH], kept["act"],
        kept["cum"], kept["cum_t"], kept["tinv"], kept["fresh"], kept["heads"], mix_grad,
        kept["act"], dcols, drows, lin_grad, tap_grad, gain_grad, rate_grad, bias_grad,
    )
    clear()
    norm2()
    run()
    grad_mixed(3)
    run()
    grad_mixed(3)
    down_stream.start()
    for head in heads:
        run(2)
        head()
    for step in [rates] + convs:
        run()
        step()
    while len(queue) > len(wide) + 1:
        run()
    result(3)
    run()
    result(len(down_cuts) - 3)
    result_swap = to_partner(1)
    proj_stream.start()
    run(4)
    result_swap.wait()
    rows_out[0] = (kept["middle"][...] + acc[0:rows, :] + swaps[2].astype(f32)).astype(bf16)
    send_home(0, rows_out.at[0])
    run()
    for count in (3, 3, len(proj_cuts) - 6):
        grad_normed(count)
        run()
    norm1()
    send_home(1, rows_out.at[1])
    pack_small()
    value = small_v[...]
    for k in range(4):
        small.begin(place, k, value)
        run()
        value = small.end(k)
    arrive(0, o_rows)
    run()
    arrive(1, o_grad)
    run(len(queue))
    for _ in range(18):
        tick()
    o_small[...] = value
    for c in stores:
        c.wait()


def backward_call(n_shard, reps, offs, lens, rate, bias, gathered, saved):
    anywhere = pl.BlockSpec(memory_space=pl.ANY)
    held = pl.BlockSpec(memory_space=pltpu.VMEM)
    words = pl.BlockSpec(memory_space=pltpu.SMEM)
    rows, width = saved["xin"].shape
    ff = 2 * gathered[2].shape[1]
    sd = jax.ShapeDtypeStruct
    wide = QKV + VALS + LANES
    sems = pltpu.SemaphoreType.DMA
    rings = (Ring(n_shard, width // n_shard, PIECE, 2),)
    small = Small(n_shard, reps, 16, width)
    outs = [
        sd((rows, width), bf16), sd((rows, width), bf16), sd((width // n_shard, 2 * ff), bf16),
        sd((ff // n_shard, width), bf16), sd((VALS // n_shard, width), bf16), sd((width // n_shard, wide), bf16),
        sd((16, width), f32),
    ]
    vmem = pltpu.VMEM
    scratch = [vmem(saved[name].shape, saved[name].dtype) for name in BACK_KEPT]
    scratch += rings[0].scratch() + small.scratch()
    scratch += [
        sems((len(BACK_KEPT),)), vmem((2, width, WIDE), bf16), sems((2, 2)), vmem((2, FTILE, width), bf16), sems((2, 1)),
        vmem((2 * rows, width), f32), vmem((rows, width), f32), vmem((rows, width), bf16), vmem((rows, VALS), f32),
        vmem((rows, LANES), f32), vmem((LANES, rows), f32), vmem((rows, wide), bf16), vmem((4, QKV), f32),
        vmem((1, DVH), f32), vmem((1, LANES), f32), vmem((1, LANES), f32), vmem((16, width), f32),
        vmem((2, rows, width), bf16), vmem((2, rows, width), bf16), sems((2, n_shard)), sems((2, n_shard)),
        vmem((2, rows, width), bf16), sems((2,)), vmem((3, rows, width), bf16), sems((2,)), sems((2,)),
        vmem((max(VALS, ff // 2), PIECE), bf16), vmem((1, LANES), f32), vmem((1, LANES), f32),
    ]
    return pl.pallas_call(
        functools.partial(backward_kernel, n_shard, reps, rings, small),
        in_specs=[words] * 4 + [anywhere] * (5 + len(BACK_KEPT)),
        out_specs=[anywhere] * 6 + [held],
        out_shape=outs,
        scratch_shapes=scratch,
        compiler_params=pltpu.CompilerParams(collective_id=0, has_side_effects=True, vmem_limit_bytes=63 << 20),
    )(offs, lens, rate, bias, *gathered, *[saved[name] for name in BACK_KEPT])


def local(
    reps, tokens, cotangent, deal, offsets, lengths, norm1_gain, q_weight, k_weight, v_weight, conv_weight,
    beta_weight, decay_weight, log_rate, step_bias, out_gate_weight, out_norm_gain, out_weight, norm2_gain,
    ffn_gate, ffn_up, ffn_down,
):
    rows, width = tokens.shape
    n = lax.axis_size("shard")
    s = lax.axis_index("shard")
    pad = LANES - 2 * HEADS
    bd_weight = jnp.concatenate([beta_weight, decay_weight, jnp.zeros((beta_weight.shape[0], pad), bf16)], axis=1)
    def spread(vector):
        k, size = vector.shape
        mine = jnp.arange(n)[None, :, None] == s
        return jnp.where(mine, vector[:, None, :], jnp.zeros((), bf16)).reshape(-1, min(width, n * size))

    gain = spread(out_norm_gain[None])
    small_in = jnp.concatenate(
        [
            spread(conv_weight), spread(norm1_gain[None]), spread(norm2_gain[None]),
            jnp.pad(gain, ((0, 1), (0, width - gain.shape[1]))),
        ]
    )
    weights = (q_weight, k_weight, v_weight, out_gate_weight, bd_weight, out_weight, ffn_gate, ffn_up, ffn_down)
    deals = deal[None, :]
    gathered, saved = forward_call(
        n, reps, offsets[0], lengths[0], tokens, cotangent, deals, small_in, log_rate, step_bias, weights
    )
    home_rows, home_grad, s_ffn, s_down, s_out, s_proj, small = backward_call(
        n, reps, offsets[0], lengths[0], log_rate, step_bias, gathered, saved
    )

    def part(a, dim=0):
        size = a.shape[dim] // n
        return lax.dynamic_slice_in_dim(a, s * size, size, dim)

    at = QKV + VALS
    ff = ffn_gate.shape[1]
    proj = [(0, 0, KEYS), (0, KEYS, KEYS), (0, 2 * KEYS, VALS), (0, QKV, VALS), (0, at, LANES)]
    rest = [(1, 0, ff), (1, ff, ff), (2, 0, width), (3, 0, width)]
    g_q, g_k, g_v, g_t, g_bd, g_gate, g_up, g_down, g_out = widen([s_proj, s_ffn, s_down, s_out], proj + rest)
    return (
        home_rows, home_grad, part(small[12]), g_q, g_k, g_v, part(small[:12].reshape(4, QKV), 1), g_bd[:, :HEADS],
        g_bd[:, HEADS : 2 * HEADS], small[14, DVH + HEADS : DVH + 2 * HEADS],
        small[14, DVH + LANES + HEADS : DVH + LANES + 2 * HEADS], g_t, part(small[14, :DVH]), g_out, part(small[13]),
        g_gate, g_up, g_down,
    )


def widen(sources, cut):
    k, total = len(sources), len(cut)

    def kernel(*refs):
        ins, outs = refs[:k], refs[k : k + total]
        narrow, wide = refs[k + total : 2 * k + total], refs[2 * k + total : 2 * (k + total)]
        come, go = refs[2 * (k + total) :]
        for i in range(k):
            pltpu.make_async_copy(ins[i], narrow[i], come.at[i]).start()
        ready = set()
        for j, (i, at, cols) in enumerate(cut):
            if i not in ready:
                ready.add(i)
                pltpu.make_async_copy(ins[i], narrow[i], come.at[i]).wait()
            wide[j][...] = narrow[i][:, at : at + cols].astype(f32)
            pltpu.make_async_copy(wide[j], outs[j], go.at[j]).start()
        for j in range(total):
            pltpu.make_async_copy(wide[j], outs[j], go.at[j]).wait()

    anywhere = pl.BlockSpec(memory_space=pl.ANY)
    shapes = [(sources[i].shape[0], cols) for i, _, cols in cut]
    return pl.pallas_call(
        kernel,
        in_specs=[anywhere] * k,
        out_specs=[anywhere] * total,
        out_shape=[jax.ShapeDtypeStruct(shape, f32) for shape in shapes],
        scratch_shapes=[pltpu.VMEM(a.shape, bf16) for a in sources]
        + [pltpu.VMEM(shape, f32) for shape in shapes]
        + [pltpu.SemaphoreType.DMA((k,)), pltpu.SemaphoreType.DMA((total,))],
        compiler_params=pltpu.CompilerParams(vmem_limit_bytes=62 << 20),
    )(*sources)


def solution(mesh):
    rows2, shard0 = P(("rep", "shard"), None), P("shard", None)
    vec = P("shard")
    in_specs = (
        rows2, rows2, P(("rep", "shard")), rows2, rows2, vec, shard0, shard0, shard0, P(None, "shard"),
        shard0, shard0, P(), P(), shard0, vec, shard0, vec, shard0, shard0, shard0,
    )
    out_specs = (
        rows2, rows2, vec, shard0, shard0, shard0, P(None, "shard"), shard0, shard0, P(), P(), shard0,
        vec, shard0, vec, shard0, shard0, shard0,
    )
    body = functools.partial(local, mesh.shape["rep"])
    return jax.shard_map(body, mesh=mesh, in_specs=in_specs, out_specs=out_specs, check_vma=False)
```
